32 devices in a mesh: brick: 8 (over y, x, core), kvec: 4 (over z).
Axes of the slice: x: 2, y: 2, z: 4, core: 2. Of those that a mesh axis runs over, the one named last changes fastest.
Arguments:
- features: bfloat16 [8192, 256], P(('brick', 'kvec')), may hold values from -6 to 6
- positions: float32 [3, 8192], P(None, ('brick', 'kvec')), may hold values from 0 to 128, as said below
- neighbours: int32 [8192, 64], P(('brick', 'kvec')), may hold values from 0 to 383, as said below
- counts: int32 [8192], P(('brick', 'kvec')), may hold values from 32 to 64
- w_in: bfloat16 [2, 256, 256], replicated, may hold values from -0.375 to 0.375
- w_out: bfloat16 [2, 256, 256], replicated, may hold values from -0.375 to 0.375
- w_charge: float32 [256], replicated, may hold values from -0.375 to 0.375
- wave: float32 [3, 16384], replicated, may hold values from -3 to 3, as said below
Outputs:
- hidden_state: bfloat16 [8192, 256], P(('brick', 'kvec'))
- potential: float32 [8192], P(('brick', 'kvec'))
- field: float32 [3, 8192], P(None, ('brick', 'kvec'))
The draws below stay inside these ranges and needn't reach their ends.
Inputs may be any that keep to these rules, and one draw needn't show every extreme that they name: `neighbours`: index e in row i names atom (i // 256) * 256 - 64 + e, which always exists and is never atom i itself; it lies within 64 rows of i. `positions`: atom i has first coordinate in [4 (i // 256), 4 (i // 256) + 4), growing with i; the other two lie in [0, 6]. `wave`: each component's magnitude lies in [0.3, 3].
All inputs are finite; a program needn't handle non-finite values.
Results may differ from the reference program's by a relative error of at most 0.0056.
Values may be sent and summed in bfloat16 or wider, within the bound.
No kernel may reach another device: no remote copies, remote signals or barrier semaphores. Data moves between devices by JAX's collectives and lax.ppermute only.
A program may use at most 192 MiB of HBM per device.

```python
import math
import jax
import jax.numpy as jnp
from jax import lax

D = 256
LAYERS = 2
NEIGH = 64
HALO = 64
ATOM_DEV = 256
ATOMS = 8192
KVECS = 16384


def draw_positions(key, part):
    key = jax.random.fold_in(key, 11)
    side = 4.0
    noise = jax.random.uniform(key, (3, ATOMS), jnp.float32)
    along = (jnp.arange(ATOMS, dtype=jnp.float32) + noise[0]) * (4.0 / ATOM_DEV)
    return jnp.stack([along, noise[1] * side, noise[2] * side])


def draw_neighbours(key, part):
    key = jax.random.fold_in(key, 12)
    key_off, key_sign = jax.random.split(key)
    rows = jnp.arange(ATOMS, dtype=jnp.int32)
    device = rows // ATOM_DEV
    local = rows % ATOM_DEV
    offset = jax.random.randint(key_off, (ATOMS, NEIGH), 1, HALO + 1, dtype=jnp.int32)
    signs = jax.random.randint(key_sign, (ATOMS, NEIGH), 0, 2, dtype=jnp.int32) * 2 - 1
    last_device = ATOMS // ATOM_DEV - 1
    signs = signs.at[ATOM_DEV - 1, 0].set(1)
    offset = offset.at[ATOM_DEV - 1, 0].set(HALO)
    signs = signs.at[last_device * ATOM_DEV, 0].set(-1)
    offset = offset.at[last_device * ATOM_DEV, 0].set(HALO)
    target = local[:, None] + signs * offset
    flip_low = (device[:, None] == 0) & (target < 0)
    flip_high = (device[:, None] == last_device) & (target >= ATOM_DEV)
    target = jnp.where(flip_low | flip_high, local[:, None] - signs * offset, target)
    return (target + HALO).astype(jnp.int32)


def draw_counts(key, part):
    key = jax.random.fold_in(key, 13)
    values = jax.random.randint(key, (ATOMS,), NEIGH // 2, NEIGH + 1, dtype=jnp.int32)
    values = values.at[0].set(NEIGH)
    return values.at[1].set(NEIGH // 2)


def draw_wave(key, part):
    key = jax.random.fold_in(key, 14)
    key_mag, key_sign = jax.random.split(key)
    noise = jax.random.uniform(key_mag, (3, KVECS), jnp.float32)
    magnitude = 0.3 + 2.7 * noise
    signs = jax.random.randint(key_sign, (3, KVECS), 0, 2, dtype=jnp.int32) * 2 - 1
    return magnitude * signs.astype(jnp.float32)


def block_scale(own_key, dims, cuts, low, largest):
    level, own = 1.0, jax.random.fold_in(own_key, 6)
    for position, blocks in cuts:
        draws = jnp.exp(jax.random.uniform(jax.random.fold_in(own, position), (blocks,), jnp.float32, low / len(cuts), largest / len(cuts)))
        level = level * jnp.repeat(draws, dims[position] // blocks).reshape([-1 if axis == position else 1 for axis in range(len(dims))])
    return level


def gaussian(key, dims, spread, bound, cuts=(), kind=jnp.bfloat16):
    loudness = block_scale(key, dims, cuts, -0.22, 0.18) if cuts else 1.0
    values = jax.random.normal(key, dims, jnp.float32) * spread * loudness
    return jnp.minimum(jnp.maximum(values, -bound), bound).astype(kind)


def setup_inputs(seed: int = 0) -> dict:
    streams_of = jax.random.split(jax.random.key(seed), 9)
    features = gaussian(streams_of[0], (ATOMS, D), 1.0, 6.0, ((0, 32),))
    positions = draw_positions(jax.random.fold_in(streams_of[8], 71), 0)
    neighbours = draw_neighbours(jax.random.fold_in(streams_of[8], 71), 0)
    counts = draw_counts(jax.random.fold_in(streams_of[8], 71), 0)
    w_in = gaussian(streams_of[4], (LAYERS, D, D), D ** -0.5, 0.375)
    w_out = gaussian(streams_of[5], (LAYERS, D, D), D ** -0.5, 0.375)
    w_charge = gaussian(streams_of[6], (D,), D ** -0.5, 0.375, (), jnp.float32)
    wave = draw_wave(jax.random.fold_in(streams_of[8], 71), 0)
    return {"features": features, "positions": positions, "neighbours": neighbours, "counts": counts, "w_in": w_in, "w_out": w_out, "w_charge": w_charge, "wave": wave}


def advance(hidden_block, near_rows, weights, w_first, w_second):
    message = lax.optimization_barrier(jnp.sum(weights[:, :, None] * near_rows.astype(jnp.float32), axis=1))
    normed = (message * lax.rsqrt(lax.optimization_barrier(jnp.mean(message * message, axis=-1, keepdims=True)) + 1e-05)).astype(jnp.bfloat16)
    inner = jax.nn.silu(jnp.dot(normed, w_first, preferred_element_type=jnp.float32)).astype(jnp.bfloat16)
    update = jnp.dot(inner, w_second, preferred_element_type=jnp.float32)
    return (hidden_block.astype(jnp.float32) + update).astype(jnp.bfloat16)

def pair_weights(coords, near, counts):
    diff = near - coords[:, :, None]
    dist = lax.optimization_barrier(jnp.sum(diff * diff, axis=0))
    slots = jnp.arange(near.shape[2], dtype=jnp.int32)
    live = slots[None, :] < counts[:, None]
    return jnp.where(live, 1.0 / (1.0 + dist), jnp.zeros_like(dist))

def phases(coords, tile):
    return coords[0][:, None] * tile[0][None, :] + coords[1][:, None] * tile[1][None, :] + coords[2][:, None] * tile[2][None, :]

def structure(coords, charge, wave, width):
    total = wave.shape[1]
    tiles = wave.reshape(3, total // width, width).transpose(1, 0, 2)

    def single(tile):
        angle = phases(coords, tile)
        return (lax.optimization_barrier(jnp.sum(charge[:, None] * jnp.cos(angle), axis=0)), lax.optimization_barrier(jnp.sum(charge[:, None] * jnp.sin(angle), axis=0)))
    cosine, sine = lax.map(single, tiles)
    return (cosine.reshape(total), sine.reshape(total))

def response(coords, wave, cos_sum, sin_sum, factor, width):
    total = wave.shape[1]
    ksq = lax.optimization_barrier(jnp.sum(wave * wave, axis=0))
    coef = factor * jnp.exp(-0.1 * ksq) / ksq
    stacked = jnp.concatenate([wave, (coef * cos_sum)[None, :], (coef * sin_sum)[None, :]], axis=0)
    tiles = stacked.reshape(5, total // width, width).transpose(1, 0, 2)

    def step(carry, tile):
        potential, field = carry
        angle = phases(coords, tile)
        cosine = jnp.cos(angle)
        sine = jnp.sin(angle)
        potential = potential + lax.optimization_barrier(jnp.sum(cosine * tile[3][None, :] + sine * tile[4][None, :], axis=1))
        mixed = sine * tile[3][None, :] - cosine * tile[4][None, :]
        parts = jnp.stack([lax.optimization_barrier(jnp.sum(mixed * tile[c][None, :], axis=1)) for c in range(3)])
        return ((potential, field + parts), None)
    count = coords.shape[1]
    start = (jnp.zeros((count,), jnp.float32), jnp.zeros((3, count), jnp.float32))
    (potential, field), unused = lax.scan(step, start, tiles)
    return (potential, field)

def reference(features, positions, neighbours, counts, w_in, w_out, w_charge, wave):
    atoms = features.shape[0]
    rows = jnp.arange(atoms, dtype=jnp.int32)
    glob = (rows // ATOM_DEV * ATOM_DEV - HALO)[:, None] + neighbours
    near = positions[:, glob]
    weights = pair_weights(positions, near, counts)
    blocks = atoms // ATOM_DEV
    hidden = features
    for layer_index in range(LAYERS):
        current = hidden
        w_first = w_in[layer_index]
        w_second = w_out[layer_index]

        def single(pieces):
            index_block, weight_block, hidden_block = pieces
            return advance(hidden_block, current[index_block], weight_block, w_first, w_second)
        hidden = lax.map(single, (glob.reshape(blocks, ATOM_DEV, NEIGH), weights.reshape(blocks, ATOM_DEV, NEIGH), current.reshape(blocks, ATOM_DEV, D))).reshape(atoms, D)
    charge = jnp.dot(hidden.astype(jnp.float32), w_charge, precision=lax.Precision.HIGHEST)
    total = wave.shape[1]
    factor = 4.0 / math.sqrt(atoms * total)
    width = math.gcd(512, total)
    cos_sum, sin_sum = structure(positions, charge, wave, width)
    potential, field = response(positions, wave, cos_sum, sin_sum, factor, width)
    return (hidden, potential, field)
```

```python
import functools
import math

import jax
import jax.numpy as jnp
import numpy as np
from jax import lax
from jax.experimental import pallas as pl
from jax.experimental.pallas import tpu as pltpu
from jax.sharding import PartitionSpec as P

LAYERS = 2
HALO = 64
AXES = ("brick", "kvec")
LANES = 128
F32 = jnp.float32
BF16 = jnp.bfloat16

VMEM = pl.BlockSpec(memory_space=pltpu.VMEM)


def pieces(x):
    first = x.astype(BF16).astype(F32)
    rest = x - first
    second = rest.astype(BF16).astype(F32)
    return first, second, rest - second


def pack_kernel(feat_ref, pos_ref, neigh_ref, counts_ref, first_ref, last_ref):
    own, slots = neigh_ref.shape
    channels = feat_ref.shape[1]
    pos = pos_ref[...]
    count_row = counts_ref[...].astype(F32)
    hi, mid, lo = pieces(pos)
    zero5 = jnp.zeros((5, own), F32)
    stack = jnp.concatenate(
        [jnp.zeros((64, own), F32), hi, count_row, zero5[:4], mid, zero5, lo, zero5]
        + [jnp.zeros((40, own), F32)],
        axis=0,
    )
    columns = stack.T
    rows = lax.broadcasted_iota(jnp.int32, (own, slots), 0)
    slot = lax.broadcasted_iota(jnp.int32, (own, slots), 1).astype(F32)
    delta = (neigh_ref[...] - HALO - rows).astype(F32)
    delta = jnp.where(slot < columns[:, 67:68], delta, jnp.zeros_like(delta))
    wide = jnp.concatenate([delta, jnp.zeros((own, LANES - slots), F32)], axis=1)
    lane = lax.broadcasted_iota(jnp.int32, (own, LANES), 1)
    side = jnp.where(lane < slots, wide, columns).astype(BF16)
    half = own // 2
    for ref, start in ((first_ref, 0), (last_ref, half)):
        ref[:, :channels] = feat_ref[start : start + half, :]
        ref[:, channels:] = side[start : start + half, :]


def make_series():
    nodes = 400
    x = np.cos((np.arange(nodes) + 0.5) * np.pi / nodes)
    s = 0.125 * (x + 1.0)
    r = np.sqrt(s)

    def fitted(values, degree):
        cheb = np.polynomial.chebyshev.Chebyshev.fit(s, values, degree, domain=[0.0, 0.25])
        return [float(v) for v in cheb.convert(kind=np.polynomial.Polynomial).coef]

    root = math.sqrt(2.0)
    half_sine = fitted(root * np.sin(np.pi * r) / r, 3)
    half_cosine = fitted(root * np.cos(np.pi * r), 3)
    return half_sine, half_cosine


HALF_SINE, HALF_COSINE = make_series()


def horner(s, coefs):
    value = coefs[-1] * s + coefs[-2]
    for c in coefs[-3::-1]:
        value = value * s + c
    return value


def trig_kernel(pos_ref, wave_ref, cos_ref, sin_ref, left_ref, *, tile, chunk):
    own = pos_ref.shape[1]
    total = wave_ref.shape[1]
    zero5 = jnp.zeros((5, own), F32)
    a, b, c = (jnp.concatenate([p, zero5], axis=0) for p in pieces(pos_ref[...]))
    left = jnp.concatenate([a, a, b, b, a, c] + [jnp.zeros((80, own), F32)], axis=0)
    left_ref[...] = left.T.astype(BF16)
    tail5 = jnp.zeros((5, tile), F32)
    magic = 12582912.0

    @pl.loop(0, total // tile)
    def _(step):
        span = pl.ds(pl.multiple_of(step * tile, tile), tile)
        turns = wave_ref[:, span] * (0.5 / math.pi)
        u, v, w = (jnp.concatenate([p, tail5], axis=0) for p in pieces(turns))
        right = jnp.concatenate([u, v, u, v, w, u] + [jnp.zeros((80, tile), F32)], axis=0)
        right = right.astype(BF16)
        for start in range(0, own, chunk):
            t = jnp.dot(left_ref[start : start + chunk, :], right, preferred_element_type=F32)
            r = t - ((t + magic) - magic)
            s = r * r
            x = r * horner(s, HALF_SINE)
            y = horner(s, HALF_COSINE)
            cos_ref[start : start + chunk, span] = (1.0 - x * x).astype(BF16)
            sin_ref[start : start + chunk, span] = (x * y).astype(BF16)


def silu(x):
    return x / (1.0 + jnp.exp(-x))


def layer_kernel(
    before_ref, first_ref, last_ref, after_ref, w_in_ref, w_out_ref, w_charge_ref, cos_ref,
    sin_ref, hidden_ref, sums_ref, feat_ref, mid_ref, matrix_ref, *, tile,
):
    parts = (before_ref, first_ref, last_ref, after_ref)
    half, width = before_ref.shape
    channels = w_in_ref.shape[1]
    own = 2 * half
    pad = HALO
    for n, ref in enumerate(parts):
        feat_ref[n * half : (n + 1) * half, :] = ref[:, :channels]
    feat_ref[4 * half :, :] = jnp.zeros((pad, channels), BF16)
    sides = [ref[:, channels:].astype(F32) for ref in parts]
    flipped = [side.T for side in sides]
    rows = [f[64:72] + f[72:80] + f[80:88] for f in flipped]
    ext_rows = jnp.concatenate(rows + [jnp.zeros((8, LANES), F32)], axis=1)
    side_all = jnp.concatenate(sides, axis=0)
    lane = lax.broadcasted_iota(jnp.int32, (HALO, LANES), 1)
    lane_f = lane.astype(F32)
    blocks = (own + 2 * HALO) // HALO
    zeros = jnp.zeros((HALO, LANES), F32)
    for block in range(blocks):
        base = HALO * (block + 1)
        side = side_all[base : base + HALO, :]
        delta = side[:, :64]
        place = jnp.where(delta > 0, delta + 63.0, delta + 64.0)
        place = jnp.where(delta == 0, -1.0, place)
        hist = zeros
        for slot in range(64):
            hist = hist + jnp.where(lane_f == place[:, slot : slot + 1], 1.0, 0.0)
        low = jnp.concatenate([jnp.where(lane < 64, hist, 0.0), zeros], axis=1)
        high = jnp.concatenate([jnp.where(lane < 64, 0.0, hist), zeros], axis=1)
        counted = pltpu.roll(low, 0, 1, stride=1, stride_axis=0) + pltpu.roll(
            high, 1, 1, stride=1, stride_axis=0
        )
        dist = jnp.zeros((HALO, 2 * LANES), F32)
        for c in range(3):
            here = side[:, 64 + c : 65 + c] + side[:, 72 + c : 73 + c] + side[:, 80 + c : 81 + c]
            there = ext_rows[c : c + 1, HALO * block : HALO * block + 2 * LANES]
            diff = there - here
            dist = dist + diff * diff
        weight = counted / (1.0 + dist)
        upper = weight.astype(BF16)
        lower = (weight - upper.astype(F32)).astype(BF16)
        matrix_ref[block, :HALO, :] = upper
        matrix_ref[block, HALO:, :] = lower

    def advance(source_ref, layer, block_ids, row0, residual):
        messages = []
        for block in block_ids:
            start = HALO * (block - row0)
            out = jnp.dot(
                matrix_ref[block],
                source_ref[start : start + 2 * LANES, :],
                preferred_element_type=F32,
            )
            messages.append(out[:HALO] + out[HALO:])
        message = jnp.concatenate(messages, axis=0)
        scale = lax.rsqrt(jnp.mean(message * message, axis=-1, keepdims=True) + 1e-05)
        normed = (message * scale).astype(BF16)
        inner = silu(jnp.dot(normed, w_in_ref[layer], preferred_element_type=F32)).astype(BF16)
        update = jnp.dot(inner, w_out_ref[layer], preferred_element_type=F32)
        return (residual.astype(F32) + update).astype(BF16)

    grown = own + 2 * HALO
    mid_ref[:grown, :] = advance(
        feat_ref, 0, range(blocks), 0, feat_ref[HALO : HALO + grown, :]
    )
    mid_ref[grown:, :] = jnp.zeros((pad, channels), BF16)
    final = advance(mid_ref, 1, range(1, blocks - 1), 1, mid_ref[HALO : HALO + own, :])
    hidden_ref[...] = final
    reader = jnp.concatenate(
        list(pieces(w_charge_ref[...])) + [jnp.zeros((5, channels), F32)], axis=0
    ).astype(BF16)
    read = lax.dot_general(
        reader, final, (((1,), (1,)), ((), ())), preferred_element_type=F32
    )
    charge = read[0:1] + read[1:2] + read[2:3]
    hi, mid, lo = pieces(charge)
    charges = jnp.concatenate([hi, mid, lo, jnp.zeros((5, own), F32)], axis=0).astype(BF16)

    @pl.loop(0, sums_ref.shape[0])
    def _(step):
        span = pl.ds(pl.multiple_of(step * tile, tile), tile)
        for n, ref in enumerate((cos_ref, sin_ref)):
            part = jnp.dot(charges, ref[:, span], preferred_element_type=F32)
            sums_ref[step, n : n + 1, :] = part[0:1] + part[1:2] + part[2:3]


def response_kernel(sums_ref, wave_ref, cos_ref, sin_ref, pot_ref, field_ref, acc_ref, *, tile, factor):
    acc_ref[...] = jnp.zeros_like(acc_ref)
    lead = lax.broadcasted_iota(jnp.int32, (4, tile), 0) == 0
    dims = (((1,), (1,)), ((), ()))

    @pl.loop(0, sums_ref.shape[0])
    def _(step):
        span = pl.ds(pl.multiple_of(step * tile, tile), tile)
        wave = wave_ref[:, span]
        ksq = jnp.sum(wave * wave, axis=0, keepdims=True)
        coef = factor * jnp.exp(-0.1 * ksq) / ksq
        scaled = coef * jnp.concatenate([jnp.ones((1, tile), F32), wave], axis=0)
        sums = sums_ref[step]
        cosine = sums[0:1]
        sine = sums[1:2]
        for ref, top, other in ((cos_ref, cosine, -sine), (sin_ref, sine, cosine)):
            full = scaled * jnp.where(lead, top, other)
            hi = full.astype(BF16).astype(F32)
            both = jnp.concatenate([hi, full - hi], axis=0).astype(BF16)
            acc_ref[...] += lax.dot_general(
                both, ref[:, span], dims, preferred_element_type=F32
            )

    result = acc_ref[:4] + acc_ref[4:]
    pot_ref[...] = result[0:1]
    field_ref[...] = result[1:4]


def shifted(x, step):
    devices = lax.axis_size(AXES)
    pairs = [(i, i + step) for i in range(devices) if 0 <= i + step < devices]
    return lax.ppermute(x, AXES, pairs)


def per_device(features, positions, neighbours, counts, w_in, w_out, w_charge, wave):
    own, channels = features.shape
    total = wave.shape[1]
    devices = lax.axis_size(AXES)
    half = own // 2
    width = channels + LANES
    share = total // devices

    edge = jax.ShapeDtypeStruct((half, width), BF16)
    first, last = pl.pallas_call(
        pack_kernel,
        out_shape=(edge, edge),
        in_specs=[VMEM] * 4,
        out_specs=(VMEM, VMEM),
    )(features, positions, neighbours, counts.reshape(1, own))
    before = shifted(last, 1)
    after = shifted(first, -1)

    table = pltpu.VMEM((own, total), BF16)
    cosine, sine = pl.pallas_call(
        functools.partial(trig_kernel, tile=256, chunk=32),
        out_shape=(table, table),
        in_specs=[VMEM] * 2,
        out_specs=(VMEM, VMEM),
        scratch_shapes=[pltpu.VMEM((own, LANES), BF16)],
        compiler_params=pltpu.CompilerParams(vmem_limit_bytes=16 << 20),
        cost_estimate=pl.CostEstimate(
            flops=own * total * 40, bytes_accessed=4 * own * total, transcendentals=0
        ),
    )(positions, wave)

    hidden, partial = pl.pallas_call(
        functools.partial(layer_kernel, tile=share),
        out_shape=(
            jax.ShapeDtypeStruct((own, channels), BF16),
            jax.ShapeDtypeStruct((devices, 2, share), F32),
        ),
        in_specs=[VMEM] * 9,
        out_specs=(VMEM, VMEM),
        scratch_shapes=[
            pltpu.VMEM((4 * half + HALO, channels), BF16),
            pltpu.VMEM((own + 3 * HALO, channels), BF16),
            pltpu.VMEM((own // HALO + 2, 2 * HALO, 2 * LANES), BF16),
        ],
        compiler_params=pltpu.CompilerParams(vmem_limit_bytes=16 << 20),
    )(before, first, last, after, w_in, w_out, w_charge.reshape(1, channels), cosine, sine)

    swapped = lax.all_to_all(partial, AXES, 0, 0, tiled=True)
    mine = jnp.sum(swapped, axis=0)
    sums = lax.all_gather(mine, AXES)

    factor = 4.0 / math.sqrt(own * devices * total)
    potential, field = pl.pallas_call(
        functools.partial(response_kernel, tile=share, factor=factor),
        out_shape=(
            jax.ShapeDtypeStruct((1, own), F32),
            jax.ShapeDtypeStruct((3, own), F32),
        ),
        in_specs=[VMEM] * 4,
        out_specs=(VMEM, VMEM),
        scratch_shapes=[pltpu.VMEM((8, own), F32)],
        compiler_params=pltpu.CompilerParams(vmem_limit_bytes=16 << 20),
    )(sums, wave, cosine, sine)
    return (hidden, potential.reshape(own), field)


def solution(mesh):
    placed = (
        P(AXES, None),
        P(None, AXES),
        P(AXES, None),
        P(AXES),
        P(),
        P(),
        P(),
        P(),
    )
    return jax.shard_map(
        per_device,
        mesh=mesh,
        in_specs=placed,
        out_specs=(P(AXES, None), P(AXES), P(None, AXES)),
        check_vma=False,
    )
```

```python
import functools
import math

import jax
import jax.numpy as jnp
import numpy as np
from jax import lax
from jax.experimental import pallas as pl
from jax.experimental.pallas import tpu as pltpu
from jax.sharding import PartitionSpec as P

LAYERS = 2
HALO = 64
AXES = ("brick", "kvec")
LANES = 128
F32 = jnp.float32
BF16 = jnp.bfloat16

VMEM = pl.BlockSpec(memory_space=pltpu.VMEM)
HBM = pl.BlockSpec(memory_space=pltpu.HBM)


def pieces(x):
    first = x.astype(BF16).astype(F32)
    rest = x - first
    second = rest.astype(BF16).astype(F32)
    return first, second, rest - second


def pack_kernel(
    feat_ref, pos_ref, neigh_ref, counts_ref, wave_ref, first_ref, last_ref, waves_ref, sem
):
    slots, own = neigh_ref.shape
    channels = feat_ref.shape[1]
    copy = pltpu.make_async_copy(wave_ref, waves_ref, sem)
    copy.start()
    rows = lax.broadcasted_iota(jnp.int32, (slots, own), 1)
    slot = lax.broadcasted_iota(jnp.int32, (slots, own), 0)
    delta = (neigh_ref[...] - HALO - rows).astype(F32)
    delta = jnp.where(slot < counts_ref[...], delta, 0.0)
    zero5 = jnp.zeros((5, own), F32)
    coords = [jnp.concatenate([p, zero5], axis=0) for p in pieces(pos_ref[...])]
    rest = jnp.zeros((LANES - slots - 24, own), F32)
    extra = jnp.concatenate([delta] + coords + [rest], axis=0).astype(BF16)
    half = own // 2
    for ref, start in ((first_ref, 0), (last_ref, half)):
        ref[:, :channels] = feat_ref[start : start + half, :]
        ref[:, channels:] = extra[:, start : start + half]
    copy.wait()


def make_series():
    nodes = 400
    x = np.cos((np.arange(nodes) + 0.5) * np.pi / nodes)
    s = 0.125 * (x + 1.0)
    r = np.sqrt(s)

    def fitted(values, degree):
        cheb = np.polynomial.chebyshev.Chebyshev.fit(s, values, degree, domain=[0.0, 0.25])
        return [float(v) for v in cheb.convert(kind=np.polynomial.Polynomial).coef]

    root = math.sqrt(2.0)
    half_sine = fitted(root * np.sin(np.pi * r) / r, 3)
    half_cosine = fitted(root * np.cos(np.pi * r), 3)
    return half_sine, half_cosine


HALF_SINE, HALF_COSINE = make_series()


def horner(s, coefs):
    value = coefs[-1] * s + coefs[-2]
    for c in coefs[-3::-1]:
        value = value * s + c
    return value


def trig_kernel(
    pos_ref, wave_ref, w_in_ref, w_out_ref, w_charge_ref, cos_ref, sin_ref, coef_ref, w_in_out,
    w_out_out, w_charge_out, left_ref, even_ref, odd_ref, sems, *, tile, chunk, factor,
):
    own = pos_ref.shape[1]
    total = wave_ref.shape[1]
    copies = [
        pltpu.make_async_copy(source, target, sems.at[n])
        for n, (source, target) in enumerate(
            ((w_in_ref, w_in_out), (w_out_ref, w_out_out), (w_charge_ref, w_charge_out))
        )
    ]
    for copy in copies:
        copy.start()
    zero5 = jnp.zeros((5, own), F32)
    a, b, c = (jnp.concatenate([p, zero5], axis=0) for p in pieces(pos_ref[...]))
    left = jnp.concatenate([a, a, b, b, a, c] + [jnp.zeros((80, own), F32)], axis=0)
    left_ref[...] = left.T.astype(BF16)
    tail5 = jnp.zeros((5, tile), F32)
    magic = 12582912.0
    count = total // tile

    def place(step):
        return pl.ds(pl.multiple_of(step * tile, tile), tile)

    def phase(step, out_ref):
        turns = wave_ref[:, place(step)] * (0.5 / math.pi)
        u, v, w = (jnp.concatenate([p, tail5], axis=0) for p in pieces(turns))
        right = jnp.concatenate([u, v, u, v, w, u] + [jnp.zeros((80, tile), F32)], axis=0)
        out_ref[...] = jnp.dot(left_ref[...], right.astype(BF16), preferred_element_type=F32)

    def evaluate(step, in_ref):
        span = place(step)
        for start in range(0, own, chunk):
            t = in_ref[start : start + chunk, :]
            r = t - ((t + magic) - magic)
            s = r * r
            x = r * horner(s, HALF_SINE)
            y = horner(s, HALF_COSINE)
            cos_ref[start : start + chunk, span] = (1.0 - x * x).astype(BF16)
            sin_ref[start : start + chunk, span] = (x * y).astype(BF16)
        wave = wave_ref[:, span]
        ksq = jnp.sum(wave * wave, axis=0, keepdims=True)
        coef = factor * jnp.exp(-0.1 * ksq) / ksq
        scaled = coef * jnp.concatenate([jnp.ones((1, tile), F32), wave], axis=0)
        coef_ref[:, span] = jnp.concatenate([scaled, scaled], axis=0)

    phase(0, even_ref)

    @pl.loop(0, count // 2)
    def _(pair):
        step = 2 * pair
        phase(step + 1, odd_ref)
        evaluate(step, even_ref)
        phase(jnp.minimum(step + 2, count - 1), even_ref)
        evaluate(step + 1, odd_ref)

    for copy in copies:
        copy.wait()


def silu(x):
    return x / (1.0 + jnp.exp(-x))


def layer_kernel(
    before_ref, first_ref, last_ref, after_ref, w_in_ref, w_out_ref, w_charge_ref, cos_ref,
    sin_ref, hidden_ref, sums_ref, feat_ref, mid_ref, matrix_ref, *, tile,
):
    parts = (before_ref, first_ref, last_ref, after_ref)
    half = before_ref.shape[0]
    channels = w_in_ref.shape[1]
    own = 2 * half
    for n, ref in enumerate(parts):
        feat_ref[n * half : (n + 1) * half, :] = ref[:, :channels]
    feat_ref[4 * half :, :] = jnp.zeros((HALO, channels), BF16)
    extras = [ref[:, channels:].astype(F32) for ref in parts]
    rows = [e[64:72] + e[72:80] + e[80:88] for e in extras]
    ext_rows = jnp.concatenate(rows + [jnp.zeros((8, LANES), F32)], axis=1)
    ext_cols = jnp.concatenate([r.T for r in rows], axis=0)
    lane = lax.broadcasted_iota(jnp.int32, (HALO, LANES), 1)
    deep = lax.broadcasted_iota(jnp.int32, (LANES, LANES), 0).astype(F32)
    deltas = [e[:64] for e in extras]
    ends = jnp.where(lane < HALO, deltas[3], deltas[0])
    hists = []
    for delta in (ends, deltas[1], deltas[2]):
        place = jnp.where(delta > 0, delta + 63.0, delta + 64.0)
        place = jnp.where(delta == 0, -1.0, place)
        hist = jnp.zeros((LANES, LANES), F32)
        for slot in range(64):
            hist = hist + jnp.where(deep == place[slot : slot + 1, :], 1.0, 0.0)
        hists.append(hist.T)
    hist_all = (hists[0][HALO:], hists[1][:HALO], hists[1][HALO:], hists[2][:HALO])
    hist_all = hist_all + (hists[2][HALO:], hists[0][:HALO])
    blocks = (own + 2 * HALO) // HALO
    zeros = jnp.zeros((HALO, LANES), F32)
    for block in range(blocks):
        base = HALO * (block + 1)
        hist = hist_all[block]
        low = jnp.concatenate([jnp.where(lane < 64, hist, 0.0), zeros], axis=1)
        high = jnp.concatenate([jnp.where(lane < 64, 0.0, hist), zeros], axis=1)
        counted = pltpu.roll(low, 0, 1, stride=1, stride_axis=0) + pltpu.roll(
            high, 1, 1, stride=1, stride_axis=0
        )
        dist = jnp.zeros((HALO, 2 * LANES), F32)
        for c in range(3):
            there = ext_rows[c : c + 1, HALO * block : HALO * block + 2 * LANES]
            diff = there - ext_cols[base : base + HALO, c : c + 1]
            dist = dist + diff * diff
        weight = counted / (1.0 + dist)
        upper = weight.astype(BF16)
        lower = (weight - upper.astype(F32)).astype(BF16)
        matrix_ref[block, :HALO, :] = upper
        matrix_ref[block, HALO:, :] = lower

    def advance(source_ref, layer, block_ids, row0, residual):
        messages = []
        for block in block_ids:
            start = HALO * (block - row0)
            out = jnp.dot(
                matrix_ref[block],
                source_ref[start : start + 2 * LANES, :],
                preferred_element_type=F32,
            )
            messages.append(out[:HALO] + out[HALO:])
        message = jnp.concatenate(messages, axis=0)
        scale = lax.rsqrt(jnp.mean(message * message, axis=-1, keepdims=True) + 1e-05)
        normed = (message * scale).astype(BF16)
        inner = silu(jnp.dot(normed, w_in_ref[layer], preferred_element_type=F32)).astype(BF16)
        update = jnp.dot(inner, w_out_ref[layer], preferred_element_type=F32)
        return (residual.astype(F32) + update).astype(BF16)

    grown = own + 2 * HALO
    mid_ref[:grown, :] = advance(
        feat_ref, 0, range(blocks), 0, feat_ref[HALO : HALO + grown, :]
    )
    mid_ref[grown:, :] = jnp.zeros((HALO, channels), BF16)
    final = advance(mid_ref, 1, range(1, blocks - 1), 1, mid_ref[HALO : HALO + own, :])
    hidden_ref[...] = final
    reader = jnp.concatenate(
        list(pieces(w_charge_ref[...])) + [jnp.zeros((5, channels), F32)], axis=0
    ).astype(BF16)
    read = lax.dot_general(
        reader, final, (((1,), (1,)), ((), ())), preferred_element_type=F32
    )
    charge = read[0:1] + read[1:2] + read[2:3]
    hi, mid, lo = pieces(charge)
    charges = jnp.concatenate([hi, mid, lo, jnp.zeros((5, own), F32)], axis=0).astype(BF16)

    share = sums_ref.shape[2]
    per = tile // share

    @pl.loop(0, sums_ref.shape[0] // per)
    def _(step):
        span = pl.ds(pl.multiple_of(step * tile, tile), tile)
        for n, ref in enumerate((cos_ref, sin_ref)):
            part = jnp.dot(charges, ref[:, span], preferred_element_type=F32)
            part = part[0:1] + part[1:2] + part[2:3]
            for q in range(per):
                sums_ref[step * per + q, n : n + 1, :] = part[:, q * share : (q + 1) * share]


def response_kernel(sums_ref, coef_ref, cos_ref, sin_ref, pot_ref, field_ref, acc_ref):
    step = pl.program_id(0)
    per, _, share = sums_ref.shape
    row = lax.broadcasted_iota(jnp.int32, (8, share), 0)
    lead = row % 4 == 0
    upper = row < 4
    dims = (((1,), (1,)), ((), ()))

    @pl.when(step == 0)
    def _():
        acc_ref[...] = jnp.zeros_like(acc_ref)

    factors = ([], [])
    for q in range(per):
        scaled = coef_ref[:, q * share : (q + 1) * share]
        cosine = sums_ref[q, 0:1, :]
        sine = sums_ref[q, 1:2, :]
        for n, (top, other) in enumerate(((cosine, -sine), (sine, cosine))):
            full = scaled * jnp.where(lead, top, other)
            hi = full.astype(BF16).astype(F32)
            factors[n].append(jnp.where(upper, hi, full - hi))
    total = acc_ref[...]
    for n, ref in enumerate((cos_ref, sin_ref)):
        wide = jnp.concatenate(factors[n], axis=1).astype(BF16)
        total = total + lax.dot_general(wide, ref[...], dims, preferred_element_type=F32)
    acc_ref[...] = total

    @pl.when(step == pl.num_programs(0) - 1)
    def _():
        result = acc_ref[:4] + acc_ref[4:]
        pot_ref[...] = result[0:1]
        field_ref[...] = result[1:4]


def shifted(x, step):
    devices = lax.axis_size(AXES)
    pairs = [(i, i + step) for i in range(devices) if 0 <= i + step < devices]
    return lax.ppermute(x, AXES, pairs)


def per_device(features, positions, neighbours, counts, w_in, w_out, w_charge, wave):
    own, channels = features.shape
    total = wave.shape[1]
    devices = lax.axis_size(AXES)
    half = own // 2
    width = channels + LANES
    share = total // devices
    factor = 4.0 / math.sqrt(own * devices * total)
    wide = 2048
    dma = pltpu.SemaphoreType.DMA
    w_charge = w_charge.reshape(1, channels)
    wave, w_in, w_out, w_charge = (
        pltpu.with_memory_space_constraint(x, pltpu.HBM) for x in (wave, w_in, w_out, w_charge)
    )

    edge = pltpu.VMEM((half, width), BF16)
    first, last, waves = pl.pallas_call(
        pack_kernel,
        out_shape=(edge, edge, pltpu.VMEM(wave.shape, F32)),
        in_specs=[VMEM] * 4 + [HBM],
        out_specs=(VMEM,) * 3,
        scratch_shapes=[dma],
    )(features, positions, neighbours.T, counts.reshape(1, own), wave)
    before = shifted(last, 1)
    after = shifted(first, -1)

    table = pltpu.VMEM((own, total), BF16)
    kept = pltpu.VMEM(w_in.shape, BF16)
    cosine, sine, coef, w_first, w_second, w_read = pl.pallas_call(
        functools.partial(trig_kernel, tile=256, chunk=32, factor=factor),
        out_shape=(table, table, pltpu.VMEM((8, total), F32), kept, kept)
        + (pltpu.VMEM((1, channels), F32),),
        in_specs=[VMEM] * 2 + [HBM] * 3,
        out_specs=(VMEM,) * 6,
        scratch_shapes=[pltpu.VMEM((own, LANES), BF16)]
        + [pltpu.VMEM((own, 256), F32)] * 2
        + [dma((3,))],
        compiler_params=pltpu.CompilerParams(vmem_limit_bytes=16 << 20),
        cost_estimate=pl.CostEstimate(
            flops=own * total * 40, bytes_accessed=4 * own * total, transcendentals=0
        ),
    )(positions, waves, w_in, w_out, w_charge)

    hidden, partial = pl.pallas_call(
        functools.partial(layer_kernel, tile=wide),
        out_shape=(
            jax.ShapeDtypeStruct((own, channels), BF16),
            jax.ShapeDtypeStruct((devices, 2, share), F32),
        ),
        in_specs=[VMEM] * 9,
        out_specs=(VMEM, VMEM),
        scratch_shapes=[
            pltpu.VMEM((4 * half + HALO, channels), BF16),
            pltpu.VMEM((own + 3 * HALO, channels), BF16),
            pltpu.VMEM((own // HALO + 2, 2 * HALO, 2 * LANES), BF16),
        ],
        compiler_params=pltpu.CompilerParams(vmem_limit_bytes=16 << 20),
    )(before, first, last, after, w_first, w_second, w_read, cosine, sine)

    swapped = lax.all_to_all(partial, AXES, 0, 0, tiled=True)
    mine = jnp.sum(swapped, axis=0)
    spread = jnp.broadcast_to(mine[None], (devices, 2, share))
    sums = lax.all_to_all(spread, AXES, 0, 0, tiled=True)

    per = wide // share
    fixed = lambda step: (0, 0)
    across = lambda step: (0, step)
    potential, field = pl.pallas_call(
        response_kernel,
        grid=(total // wide,),
        out_shape=(
            jax.ShapeDtypeStruct((1, own), F32),
            jax.ShapeDtypeStruct((3, own), F32),
        ),
        in_specs=[
            pl.BlockSpec((per, 2, share), lambda step: (step, 0, 0)),
            pl.BlockSpec((8, wide), across),
            pl.BlockSpec((own, wide), across),
            pl.BlockSpec((own, wide), across),
        ],
        out_specs=(pl.BlockSpec((1, own), fixed), pl.BlockSpec((3, own), fixed)),
        scratch_shapes=[pltpu.VMEM((8, own), F32)],
        compiler_params=pltpu.CompilerParams(vmem_limit_bytes=56 << 20),
    )(sums, coef, cosine, sine)
    return (hidden, potential.reshape(own), field)


def solution(mesh):
    placed = (
        P(AXES, None),
        P(None, AXES),
        P(AXES, None),
        P(AXES),
        P(),
        P(),
        P(),
        P(),
    )
    return jax.shard_map(
        per_device,
        mesh=mesh,
        in_specs=placed,
        out_specs=(P(AXES, None), P(AXES), P(None, AXES)),
        check_vma=False,
    )
```

```python
import functools
import math

import jax
import jax.numpy as jnp
import numpy as np
from jax import lax
from jax.experimental import pallas as pl
from jax.experimental.pallas import tpu as pltpu
from jax.sharding import PartitionSpec as P

LAYERS = 2
HALO = 64
AXES = ("brick", "kvec")
LANES = 128
F32 = jnp.float32
BF16 = jnp.bfloat16

VMEM = pl.BlockSpec(memory_space=pltpu.VMEM)
HBM = pl.BlockSpec(memory_space=pltpu.HBM)


def pieces(x):
    first = x.astype(BF16).astype(F32)
    rest = x - first
    second = rest.astype(BF16).astype(F32)
    return first, second, rest - second


def pack_kernel(
    feat_ref, pos_ref, neigh_ref, counts_ref, wave_ref, first_ref, last_ref, waves_ref,
    held_ref, sem,
):
    slots, own = neigh_ref.shape
    channels = feat_ref.shape[1]
    copy = pltpu.make_async_copy(wave_ref, waves_ref, sem)
    copy.start()
    held_ref[...] = pos_ref[...]
    rows = lax.broadcasted_iota(jnp.int32, (slots, own), 1)
    slot = lax.broadcasted_iota(jnp.int32, (slots, own), 0)
    delta = (neigh_ref[...] - HALO - rows).astype(F32)
    delta = jnp.where(slot < counts_ref[...], delta, 0.0)
    zero5 = jnp.zeros((5, own), F32)
    coords = [jnp.concatenate([p, zero5], axis=0) for p in pieces(pos_ref[...])]
    rest = jnp.zeros((LANES - slots - 24, own), F32)
    extra = jnp.concatenate([delta] + coords + [rest], axis=0).astype(BF16)
    half = own // 2
    for ref, start in ((first_ref, 0), (last_ref, half)):
        ref[:, :channels] = feat_ref[start : start + half, :]
        ref[:, channels:] = extra[:, start : start + half]
    copy.wait()


def make_series():
    nodes = 400
    x = np.cos((np.arange(nodes) + 0.5) * np.pi / nodes)
    s = 0.125 * (x + 1.0)
    r = np.sqrt(s)

    def fitted(values, degree):
        cheb = np.polynomial.chebyshev.Chebyshev.fit(s, values, degree, domain=[0.0, 0.25])
        return [float(v) for v in cheb.convert(kind=np.polynomial.Polynomial).coef]

    root = math.sqrt(2.0)
    return fitted(root * np.sin(np.pi * r) / r, 3)


HALF_SINE = make_series()


def horner(s, coefs):
    value = coefs[-1] * s + coefs[-2]
    for c in coefs[-3::-1]:
        value = value * s + c
    return value


def trig_kernel(
    pos_ref, wave_ref, w_in_ref, w_out_ref, w_charge_ref, cos_ref, sin_ref, cos_t_ref, sin_t_ref,
    coef_ref, w_in_out, w_out_out, w_charge_out, left_ref, even_ref, odd_ref, turned_ref, sems,
    turned_sems, *, tile, chunk, factor,
):
    own = pos_ref.shape[1]
    total = wave_ref.shape[1]
    copies = [
        pltpu.make_async_copy(source, target, sems.at[n])
        for n, (source, target) in enumerate(
            ((w_in_ref, w_in_out), (w_out_ref, w_out_out), (w_charge_ref, w_charge_out))
        )
    ]
    for copy in copies:
        copy.start()
    zero5 = jnp.zeros((5, own), F32)
    a, b, c = (jnp.concatenate([p, zero5], axis=0) for p in pieces(pos_ref[...]))
    left = jnp.concatenate([a, a, b, b, a, c] + [jnp.zeros((80, own), F32)], axis=0)
    left_ref[...] = left.T.astype(BF16)
    tail5 = jnp.zeros((5, tile), F32)
    magic = 12582912.0
    count = total // tile

    def place(step):
        return pl.ds(pl.multiple_of(step * tile, tile), tile)

    def phase(step, out_ref):
        turns = wave_ref[:, place(step)] * (0.5 / math.pi)
        u, v, w = (jnp.concatenate([p, tail5], axis=0) for p in pieces(turns))
        right = jnp.concatenate([u, v, u, v, w, u] + [jnp.zeros((80, tile), F32)], axis=0)
        out_ref[...] = jnp.dot(left_ref[...], right.astype(BF16), preferred_element_type=F32)

    def evaluate(step, in_ref):
        span = place(step)
        for start in range(0, own, chunk):
            t = in_ref[start : start + chunk, :]
            r = t - ((t + magic) - magic)
            s = r * r
            x = r * horner(s, HALF_SINE)
            square = x * x
            rest = jnp.maximum(2.0 - square, 1e-20)
            cos_ref[start : start + chunk, span] = (1.0 - square).astype(BF16)
            sin_ref[start : start + chunk, span] = (x * rest * lax.rsqrt(rest)).astype(BF16)
        wave = wave_ref[:, span]
        ksq = jnp.sum(wave * wave, axis=0, keepdims=True)
        coef = factor * jnp.exp(-0.1 * ksq) / ksq
        scaled = coef * jnp.concatenate([jnp.ones((1, tile), F32), wave], axis=0)
        coef_ref[:, span] = jnp.concatenate([scaled, scaled], axis=0)

    def moves(slot, target):
        rows = place(target)
        return [
            pltpu.make_async_copy(
                turned_ref.at[slot, n], out_ref.at[rows, :], turned_sems.at[slot, n]
            )
            for n, out_ref in enumerate((cos_t_ref, sin_t_ref))
        ]

    def flip(slot, step, target):
        for n, ref in enumerate((cos_ref, sin_ref)):
            turned_ref[slot, n] = ref[:, place(step)].T
        for move in moves(slot, target):
            move.start()

    def drain():
        for slot in range(2):
            for move in moves(slot, count):
                move.wait()

    phase(0, even_ref)

    @pl.loop(0, count // 2)
    def _(pair):
        step = 2 * pair

        @pl.when(pair > 0)
        def _():
            drain()

        flip(0, jnp.maximum(step - 1, 0), jnp.where(pair == 0, count, step - 1))
        phase(step + 1, odd_ref)
        evaluate(step, even_ref)
        flip(1, step, step)
        phase(jnp.minimum(step + 2, count - 1), even_ref)
        evaluate(step + 1, odd_ref)

    drain()
    flip(0, count - 1, count - 1)
    for move in moves(0, count):
        move.wait()
    for copy in copies:
        copy.wait()


def silu(x):
    return x / (1.0 + jnp.exp(-x))


def layer_kernel(
    before_ref, first_ref, last_ref, after_ref, w_in_ref, w_out_ref, w_charge_ref, cos_ref,
    sin_ref, hidden_ref, sums_ref, feat_ref, mid_ref, matrix_ref, *, tile,
):
    parts = (before_ref, first_ref, last_ref, after_ref)
    half = before_ref.shape[0]
    channels = w_in_ref.shape[1]
    own = 2 * half
    for n, ref in enumerate(parts):
        feat_ref[n * half : (n + 1) * half, :] = ref[:, :channels]
    feat_ref[4 * half :, :] = jnp.zeros((HALO, channels), BF16)
    extras = [ref[:, channels:].astype(F32) for ref in parts]
    rows = [e[64:72] + e[72:80] + e[80:88] for e in extras]
    ext_rows = jnp.concatenate(rows + [jnp.zeros((8, LANES), F32)], axis=1)
    ext_cols = jnp.concatenate([r.T for r in rows], axis=0)
    lane = lax.broadcasted_iota(jnp.int32, (HALO, LANES), 1)
    deep = lax.broadcasted_iota(jnp.int32, (LANES, LANES), 0).astype(F32)
    deltas = [e[:64] for e in extras]
    ends = jnp.where(lane < HALO, deltas[3], deltas[0])
    hists = []
    for delta in (ends, deltas[1], deltas[2]):
        place = jnp.where(delta > 0, delta + 63.0, delta + 64.0)
        place = jnp.where(delta == 0, -1.0, place)
        hist = jnp.zeros((LANES, LANES), F32)
        for slot in range(64):
            hist = hist + jnp.where(deep == place[slot : slot + 1, :], 1.0, 0.0)
        hists.append(hist.T)
    hist_all = (hists[0][HALO:], hists[1][:HALO], hists[1][HALO:], hists[2][:HALO])
    hist_all = hist_all + (hists[2][HALO:], hists[0][:HALO])
    blocks = (own + 2 * HALO) // HALO
    zeros = jnp.zeros((HALO, LANES), F32)
    for block in range(blocks):
        base = HALO * (block + 1)
        hist = hist_all[block]
        low = jnp.concatenate([jnp.where(lane < 64, hist, 0.0), zeros], axis=1)
        high = jnp.concatenate([jnp.where(lane < 64, 0.0, hist), zeros], axis=1)
        counted = pltpu.roll(low, 0, 1, stride=1, stride_axis=0) + pltpu.roll(
            high, 1, 1, stride=1, stride_axis=0
        )
        dist = jnp.zeros((HALO, 2 * LANES), F32)
        for c in range(3):
            there = ext_rows[c : c + 1, HALO * block : HALO * block + 2 * LANES]
            diff = there - ext_cols[base : base + HALO, c : c + 1]
            dist = dist + diff * diff
        weight = counted / (1.0 + dist)
        upper = weight.astype(BF16)
        lower = (weight - upper.astype(F32)).astype(BF16)
        matrix_ref[block, :HALO, :] = upper
        matrix_ref[block, HALO:, :] = lower

    def advance(source_ref, layer, block_ids, row0, residual):
        messages = []
        for block in block_ids:
            start = HALO * (block - row0)
            out = jnp.dot(
                matrix_ref[block],
                source_ref[start : start + 2 * LANES, :],
                preferred_element_type=F32,
            )
            messages.append(out[:HALO] + out[HALO:])
        message = jnp.concatenate(messages, axis=0)
        scale = lax.rsqrt(jnp.mean(message * message, axis=-1, keepdims=True) + 1e-05)
        normed = (message * scale).astype(BF16)
        inner = silu(jnp.dot(normed, w_in_ref[layer], preferred_element_type=F32)).astype(BF16)
        update = jnp.dot(inner, w_out_ref[layer], preferred_element_type=F32)
        return (residual.astype(F32) + update).astype(BF16)

    grown = own + 2 * HALO
    mid_ref[:grown, :] = advance(
        feat_ref, 0, range(blocks), 0, feat_ref[HALO : HALO + grown, :]
    )
    mid_ref[grown:, :] = jnp.zeros((HALO, channels), BF16)
    final = advance(mid_ref, 1, range(1, blocks - 1), 1, mid_ref[HALO : HALO + own, :])
    hidden_ref[...] = final
    reader = jnp.concatenate(
        list(pieces(w_charge_ref[...])) + [jnp.zeros((5, channels), F32)], axis=0
    ).astype(BF16)
    read = lax.dot_general(
        reader, final, (((1,), (1,)), ((), ())), preferred_element_type=F32
    )
    charge = read[0:1] + read[1:2] + read[2:3]
    hi, mid, lo = pieces(charge)
    charges = jnp.concatenate([hi, mid, lo, jnp.zeros((5, own), F32)], axis=0).astype(BF16)

    share = sums_ref.shape[2]
    per = tile // share

    @pl.loop(0, sums_ref.shape[0] // per)
    def _(step):
        span = pl.ds(pl.multiple_of(step * tile, tile), tile)
        for n, ref in enumerate((cos_ref, sin_ref)):
            part = jnp.dot(charges, ref[:, span], preferred_element_type=F32)
            part = part[0:1] + part[1:2] + part[2:3]
            for q in range(per):
                sums_ref[step * per + q, n : n + 1, :] = part[:, q * share : (q + 1) * share]


def response_kernel(sums_ref, coef_ref, cos_ref, sin_ref, pot_ref, field_ref, acc_ref):
    step = pl.program_id(0)
    per, _, share = sums_ref.shape
    row = lax.broadcasted_iota(jnp.int32, (8, share), 0)
    lead = row % 4 == 0
    upper = row < 4

    @pl.when(step == 0)
    def _():
        acc_ref[...] = jnp.zeros_like(acc_ref)

    factors = ([], [])
    for q in range(per):
        scaled = coef_ref[:, q * share : (q + 1) * share]
        cosine = sums_ref[q, 0:1, :]
        sine = sums_ref[q, 1:2, :]
        for n, (top, other) in enumerate(((cosine, -sine), (sine, cosine))):
            full = scaled * jnp.where(lead, top, other)
            hi = full.astype(BF16).astype(F32)
            factors[n].append(jnp.where(upper, hi, full - hi))
    total = acc_ref[...]
    for n, ref in enumerate((cos_ref, sin_ref)):
        wide = jnp.concatenate(factors[n], axis=1).astype(BF16)
        total = total + jnp.dot(wide, ref[...], preferred_element_type=F32)
    acc_ref[...] = total

    @pl.when(step == pl.num_programs(0) - 1)
    def _():
        result = acc_ref[:4] + acc_ref[4:]
        pot_ref[...] = result[0:1]
        field_ref[...] = result[1:4]


def shifted(x, step):
    devices = lax.axis_size(AXES)
    pairs = [(i, i + step) for i in range(devices) if 0 <= i + step < devices]
    return lax.ppermute(x, AXES, pairs)


def per_device(features, positions, neighbours, counts, w_in, w_out, w_charge, wave):
    own, channels = features.shape
    total = wave.shape[1]
    devices = lax.axis_size(AXES)
    half = own // 2
    width = channels + LANES
    share = total // devices
    factor = 4.0 / math.sqrt(own * devices * total)
    wide = 2048
    dma = pltpu.SemaphoreType.DMA
    w_charge = w_charge.reshape(1, channels)
    wave, w_in, w_out, w_charge = (
        pltpu.with_memory_space_constraint(x, pltpu.HBM) for x in (wave, w_in, w_out, w_charge)
    )

    edge = pltpu.VMEM((half, width), BF16)
    first, last, waves, held = pl.pallas_call(
        pack_kernel,
        out_shape=(edge, edge, pltpu.VMEM(wave.shape, F32), pltpu.VMEM(positions.shape, F32)),
        in_specs=[VMEM] * 4 + [HBM],
        out_specs=(VMEM,) * 4,
        scratch_shapes=[dma],
    )(features, positions, neighbours.T, counts.reshape(1, own), wave)
    before = shifted(last, 1)
    after = shifted(first, -1)

    table = pltpu.VMEM((own, total), BF16)
    table_t = pltpu.HBM((total + 256, own), BF16)
    kept = pltpu.VMEM(w_in.shape, BF16)
    cosine, sine, cosine_t, sine_t, coef, w_first, w_second, w_read = pl.pallas_call(
        functools.partial(trig_kernel, tile=256, chunk=32, factor=factor),
        out_shape=(table, table, table_t, table_t, pltpu.VMEM((8, total), F32), kept, kept)
        + (pltpu.VMEM((1, channels), F32),),
        in_specs=[VMEM] * 2 + [HBM] * 3,
        out_specs=(VMEM,) * 2 + (HBM,) * 2 + (VMEM,) * 4,
        scratch_shapes=[pltpu.VMEM((own, LANES), BF16)]
        + [pltpu.VMEM((own, 256), F32)] * 2
        + [pltpu.VMEM((2, 2, 256, own), BF16), dma((3,)), dma((2, 2))],
        compiler_params=pltpu.CompilerParams(vmem_limit_bytes=16 << 20),
        cost_estimate=pl.CostEstimate(
            flops=own * total * 40, bytes_accessed=4 * own * total, transcendentals=0
        ),
    )(held, waves, w_in, w_out, w_charge)

    hidden, partial = pl.pallas_call(
        functools.partial(layer_kernel, tile=wide),
        out_shape=(
            jax.ShapeDtypeStruct((own, channels), BF16),
            jax.ShapeDtypeStruct((devices, 2, share), F32),
        ),
        in_specs=[VMEM] * 9,
        out_specs=(VMEM, VMEM),
        scratch_shapes=[
            pltpu.VMEM((4 * half + HALO, channels), BF16),
            pltpu.VMEM((own + 3 * HALO, channels), BF16),
            pltpu.VMEM((own // HALO + 2, 2 * HALO, 2 * LANES), BF16),
        ],
        compiler_params=pltpu.CompilerParams(vmem_limit_bytes=16 << 20),
    )(before, first, last, after, w_first, w_second, w_read, cosine, sine)

    swapped = lax.all_to_all(partial.astype(BF16), AXES, 0, 0, tiled=True)
    mine = jnp.sum(swapped.astype(F32), axis=0).astype(BF16)
    spread = jnp.broadcast_to(mine[None], (devices, 2, share))
    sums = lax.all_to_all(spread, AXES, 0, 0, tiled=True).astype(F32)

    per = wide // share
    fixed = lambda step: (0, 0)
    across = lambda step: (0, step)
    potential, field = pl.pallas_call(
        response_kernel,
        grid=(total // wide,),
        out_shape=(
            jax.ShapeDtypeStruct((1, own), F32),
            jax.ShapeDtypeStruct((3, own), F32),
        ),
        in_specs=[
            pl.BlockSpec((per, 2, share), lambda step: (step, 0, 0)),
            pl.BlockSpec((8, wide), across),
            pl.BlockSpec((wide, own), lambda step: (step, 0)),
            pl.BlockSpec((wide, own), lambda step: (step, 0)),
        ],
        out_specs=(pl.BlockSpec((1, own), fixed), pl.BlockSpec((3, own), fixed)),
        scratch_shapes=[pltpu.VMEM((8, own), F32)],
        compiler_params=pltpu.CompilerParams(vmem_limit_bytes=56 << 20),
    )(sums, coef, cosine_t, sine_t)
    return (hidden, potential.reshape(own), field)


def solution(mesh):
    placed = (
        P(AXES, None),
        P(None, AXES),
        P(AXES, None),
        P(AXES),
        P(),
        P(),
        P(),
        P(),
    )
    return jax.shard_map(
        per_device,
        mesh=mesh,
        in_specs=placed,
        out_specs=(P(AXES, None), P(AXES), P(None, AXES)),
        check_vma=False,
    )
```

```python
import functools
import math

import jax
import jax.numpy as jnp
import numpy as np
from jax import lax
from jax.experimental import pallas as pl
from jax.experimental.pallas import tpu as pltpu
from jax.sharding import PartitionSpec as P

LAYERS = 2
HALO = 64
AXES = ("brick", "kvec")
LANES = 128
F32 = jnp.float32
BF16 = jnp.bfloat16

VMEM = pl.BlockSpec(memory_space=pltpu.VMEM)
HBM = pl.BlockSpec(memory_space=pltpu.HBM)


def pieces(x):
    first = x.astype(BF16).astype(F32)
    rest = x - first
    second = rest.astype(BF16).astype(F32)
    return first, second, rest - second


def pack_kernel(
    feat_ref, pos_ref, neigh_ref, counts_ref, wave_ref, first_ref, last_ref, waves_ref,
    held_ref, sem,
):
    slots, own = neigh_ref.shape
    channels = feat_ref.shape[1]
    copy = pltpu.make_async_copy(wave_ref, waves_ref, sem)
    copy.start()
    held_ref[...] = pos_ref[...]
    rows = lax.broadcasted_iota(jnp.int32, (slots, own), 1)
    slot = lax.broadcasted_iota(jnp.int32, (slots, own), 0)
    delta = (neigh_ref[...] - HALO - rows).astype(F32)
    delta = jnp.where(slot < counts_ref[...], delta, 0.0)
    zero5 = jnp.zeros((5, own), F32)
    coords = [jnp.concatenate([p, zero5], axis=0) for p in pieces(pos_ref[...])]
    rest = jnp.zeros((LANES - slots - 24, own), F32)
    extra = jnp.concatenate([delta] + coords + [rest], axis=0).astype(BF16)
    half = own // 2
    for ref, start in ((first_ref, 0), (last_ref, half)):
        ref[:, :channels] = feat_ref[start : start + half, :]
        ref[:, channels:] = extra[:, start : start + half]
    copy.wait()


def make_series():
    nodes = 400
    x = np.cos((np.arange(nodes) + 0.5) * np.pi / nodes)
    s = 0.125 * (x + 1.0)
    r = np.sqrt(s)

    def fitted(values, degree):
        cheb = np.polynomial.chebyshev.Chebyshev.fit(s, values, degree, domain=[0.0, 0.25])
        return [float(v) for v in cheb.convert(kind=np.polynomial.Polynomial).coef]

    root = math.sqrt(2.0)
    return fitted(root * np.sin(np.pi * r) / r, 3)


HALF_SINE = make_series()


def horner(s, coefs):
    value = coefs[-1] * s + coefs[-2]
    for c in coefs[-3::-1]:
        value = value * s + c
    return value


def trig_kernel(
    pos_ref, wave_ref, w_in_ref, w_out_ref, w_charge_ref, cos_ref, sin_ref, coef_ref, w_in_out,
    w_out_out, w_charge_out, left_ref, even_ref, odd_ref, sems, *, tile, chunk, factor,
):
    own = pos_ref.shape[1]
    total = wave_ref.shape[1]
    copies = [
        pltpu.make_async_copy(source, target, sems.at[n])
        for n, (source, target) in enumerate(
            ((w_in_ref, w_in_out), (w_out_ref, w_out_out), (w_charge_ref, w_charge_out))
        )
    ]
    for copy in copies:
        copy.start()
    zero5 = jnp.zeros((5, own), F32)
    a, b, c = (jnp.concatenate([p, zero5], axis=0) for p in pieces(pos_ref[...]))
    left = jnp.concatenate([a, a, b, b, a, c] + [jnp.zeros((80, own), F32)], axis=0)
    left_ref[...] = left.T.astype(BF16)
    tail5 = jnp.zeros((5, tile), F32)
    magic = 12582912.0
    count = total // tile

    def place(step):
        return pl.ds(pl.multiple_of(step * tile, tile), tile)

    def phase(step, out_ref):
        turns = wave_ref[:, place(step)] * (0.5 / math.pi)
        u, v, w = (jnp.concatenate([p, tail5], axis=0) for p in pieces(turns))
        right = jnp.concatenate([u, v, u, v, w, u] + [jnp.zeros((80, tile), F32)], axis=0)
        out_ref[...] = jnp.dot(left_ref[...], right.astype(BF16), preferred_element_type=F32)

    def evaluate(step, in_ref):
        span = place(step)
        for start in range(0, own, chunk):
            t = in_ref[start : start + chunk, :]
            r = t - ((t + magic) - magic)
            s = r * r
            x = r * horner(s, HALF_SINE)
            square = x * x
            rest = jnp.maximum(2.0 - square, 1e-20)
            cos_ref[start : start + chunk, span] = (1.0 - square).astype(BF16)
            sin_ref[start : start + chunk, span] = (x * rest * lax.rsqrt(rest)).astype(BF16)
        wave = wave_ref[:, span]
        ksq = jnp.sum(wave * wave, axis=0, keepdims=True)
        coef = factor * jnp.exp(-0.1 * ksq) / ksq
        scaled = coef * jnp.concatenate([jnp.ones((1, tile), F32), wave], axis=0)
        coef_ref[:, span] = jnp.concatenate([scaled, scaled], axis=0)

    phase(0, even_ref)

    @pl.loop(0, count // 2)
    def _(pair):
        step = 2 * pair
        phase(step + 1, odd_ref)
        evaluate(step, even_ref)
        phase(jnp.minimum(step + 2, count - 1), even_ref)
        evaluate(step + 1, odd_ref)

    for copy in copies:
        copy.wait()


def silu(x):
    return x / (1.0 + jnp.exp(-x))


def layer_kernel(
    before_ref, first_ref, last_ref, after_ref, w_in_ref, w_out_ref, w_charge_ref, cos_ref,
    sin_ref, hidden_ref, sums_ref, feat_ref, mid_ref, matrix_ref, *, tile,
):
    parts = (before_ref, first_ref, last_ref, after_ref)
    half = before_ref.shape[0]
    channels = w_in_ref.shape[1]
    own = 2 * half
    for n, ref in enumerate(parts):
        feat_ref[n * half : (n + 1) * half, :] = ref[:, :channels]
    feat_ref[4 * half :, :] = jnp.zeros((HALO, channels), BF16)
    extras = [ref[:, channels:].astype(F32) for ref in parts]
    rows = [e[64:72] + e[72:80] + e[80:88] for e in extras]
    ext_rows = jnp.concatenate(rows + [jnp.zeros((8, LANES), F32)], axis=1)
    ext_cols = jnp.concatenate([r.T for r in rows], axis=0)
    lane = lax.broadcasted_iota(jnp.int32, (HALO, LANES), 1)
    deep = lax.broadcasted_iota(jnp.int32, (LANES, LANES), 0).astype(F32)
    deltas = [e[:64] for e in extras]
    ends = jnp.where(lane < HALO, deltas[3], deltas[0])
    hists = []
    for delta in (ends, deltas[1], deltas[2]):
        place = jnp.where(delta > 0, delta + 63.0, delta + 64.0)
        place = jnp.where(delta == 0, -1.0, place)
        hist = jnp.zeros((LANES, LANES), F32)
        for slot in range(64):
            hist = hist + jnp.where(deep == place[slot : slot + 1, :], 1.0, 0.0)
        hists.append(hist.T)
    hist_all = (hists[0][HALO:], hists[1][:HALO], hists[1][HALO:], hists[2][:HALO])
    hist_all = hist_all + (hists[2][HALO:], hists[0][:HALO])
    blocks = (own + 2 * HALO) // HALO
    zeros = jnp.zeros((HALO, LANES), F32)
    for block in range(blocks):
        base = HALO * (block + 1)
        hist = hist_all[block]
        low = jnp.concatenate([jnp.where(lane < 64, hist, 0.0), zeros], axis=1)
        high = jnp.concatenate([jnp.where(lane < 64, 0.0, hist), zeros], axis=1)
        counted = pltpu.roll(low, 0, 1, stride=1, stride_axis=0) + pltpu.roll(
            high, 1, 1, stride=1, stride_axis=0
        )
        dist = jnp.zeros((HALO, 2 * LANES), F32)
        for c in range(3):
            there = ext_rows[c : c + 1, HALO * block : HALO * block + 2 * LANES]
            diff = there - ext_cols[base : base + HALO, c : c + 1]
            dist = dist + diff * diff
        weight = counted / (1.0 + dist)
        upper = weight.astype(BF16)
        lower = (weight - upper.astype(F32)).astype(BF16)
        matrix_ref[block, :HALO, :] = upper
        matrix_ref[block, HALO:, :] = lower

    def advance(source_ref, layer, block_ids, row0, residual):
        messages = []
        for block in block_ids:
            start = HALO * (block - row0)
            out = jnp.dot(
                matrix_ref[block],
                source_ref[start : start + 2 * LANES, :],
                preferred_element_type=F32,
            )
            messages.append(out[:HALO] + out[HALO:])
        message = jnp.concatenate(messages, axis=0)
        scale = lax.rsqrt(jnp.mean(message * message, axis=-1, keepdims=True) + 1e-05)
        normed = (message * scale).astype(BF16)
        inner = silu(jnp.dot(normed, w_in_ref[layer], preferred_element_type=F32)).astype(BF16)
        update = jnp.dot(inner, w_out_ref[layer], preferred_element_type=F32)
        return (residual.astype(F32) + update).astype(BF16)

    grown = own + 2 * HALO
    mid_ref[:grown, :] = advance(
        feat_ref, 0, range(blocks), 0, feat_ref[HALO : HALO + grown, :]
    )
    mid_ref[grown:, :] = jnp.zeros((HALO, channels), BF16)
    final = advance(mid_ref, 1, range(1, blocks - 1), 1, mid_ref[HALO : HALO + own, :])
    hidden_ref[...] = final
    reader = jnp.concatenate(
        list(pieces(w_charge_ref[...])) + [jnp.zeros((5, channels), F32)], axis=0
    ).astype(BF16)
    read = lax.dot_general(
        reader, final, (((1,), (1,)), ((), ())), preferred_element_type=F32
    )
    charge = read[0:1] + read[1:2] + read[2:3]
    hi, mid, lo = pieces(charge)
    charges = jnp.concatenate([hi, mid, lo, jnp.zeros((5, own), F32)], axis=0).astype(BF16)

    share = sums_ref.shape[2]
    per = tile // share

    @pl.loop(0, sums_ref.shape[0] // per)
    def _(step):
        span = pl.ds(pl.multiple_of(step * tile, tile), tile)
        for n, ref in enumerate((cos_ref, sin_ref)):
            part = jnp.dot(charges, ref[:, span], preferred_element_type=F32)
            part = part[0:1] + part[1:2] + part[2:3]
            for q in range(per):
                sums_ref[step * per + q, n : n + 1, :] = part[:, q * share : (q + 1) * share]


def response_kernel(sums_ref, coef_ref, cos_ref, sin_ref, pot_ref, field_ref, acc_ref, *, tile):
    groups, _, share = sums_ref.shape
    per = tile // share
    row = lax.broadcasted_iota(jnp.int32, (8, share), 0)
    lead = row % 4 == 0
    upper = row < 4
    dims = (((1,), (1,)), ((), ()))
    acc_ref[...] = jnp.zeros_like(acc_ref)

    @pl.loop(0, groups // per)
    def _(step):
        span = pl.ds(pl.multiple_of(step * tile, tile), tile)
        coef = coef_ref[:, span]
        factors = ([], [])
        for q in range(per):
            scaled = coef[:, q * share : (q + 1) * share]
            sums = sums_ref[step * per + q].astype(F32)
            cosine = sums[0:1]
            sine = sums[1:2]
            for n, (top, other) in enumerate(((cosine, -sine), (sine, cosine))):
                full = scaled * jnp.where(lead, top, other)
                hi = full.astype(BF16).astype(F32)
                factors[n].append(jnp.where(upper, hi, full - hi))
        total = acc_ref[...]
        for n, ref in enumerate((cos_ref, sin_ref)):
            wide = jnp.concatenate(factors[n], axis=1).astype(BF16)
            total = total + lax.dot_general(
                wide, ref[:, span], dims, preferred_element_type=F32
            )
        acc_ref[...] = total

    result = acc_ref[:4] + acc_ref[4:]
    pot_ref[...] = result[0:1]
    field_ref[...] = result[1:4]


def shifted(x, step):
    devices = lax.axis_size(AXES)
    pairs = [(i, i + step) for i in range(devices) if 0 <= i + step < devices]
    return lax.ppermute(x, AXES, pairs)


def per_device(features, positions, neighbours, counts, w_in, w_out, w_charge, wave):
    own, channels = features.shape
    total = wave.shape[1]
    devices = lax.axis_size(AXES)
    half = own // 2
    width = channels + LANES
    share = total // devices
    factor = 4.0 / math.sqrt(own * devices * total)
    wide = 2048
    dma = pltpu.SemaphoreType.DMA
    w_charge = w_charge.reshape(1, channels)
    wave, w_in, w_out, w_charge = (
        pltpu.with_memory_space_constraint(x, pltpu.HBM) for x in (wave, w_in, w_out, w_charge)
    )

    edge = pltpu.VMEM((half, width), BF16)
    first, last, waves, held = pl.pallas_call(
        pack_kernel,
        out_shape=(edge, edge, pltpu.VMEM(wave.shape, F32), pltpu.VMEM(positions.shape, F32)),
        in_specs=[VMEM] * 4 + [HBM],
        out_specs=(VMEM,) * 4,
        scratch_shapes=[dma],
    )(features, positions, neighbours.T, counts.reshape(1, own), wave)
    before = shifted(last, 1)
    after = shifted(first, -1)

    table = pltpu.VMEM((own, total), BF16)
    kept = pltpu.VMEM(w_in.shape, BF16)
    cosine, sine, coef, w_first, w_second, w_read = pl.pallas_call(
        functools.partial(trig_kernel, tile=256, chunk=32, factor=factor),
        out_shape=(table, table, pltpu.VMEM((8, total), F32), kept, kept)
        + (pltpu.VMEM((1, channels), F32),),
        in_specs=[VMEM] * 2 + [HBM] * 3,
        out_specs=(VMEM,) * 6,
        scratch_shapes=[pltpu.VMEM((own, LANES), BF16)]
        + [pltpu.VMEM((own, 256), F32)] * 2
        + [dma((3,))],
        compiler_params=pltpu.CompilerParams(vmem_limit_bytes=16 << 20),
        cost_estimate=pl.CostEstimate(
            flops=own * total * 40, bytes_accessed=4 * own * total, transcendentals=0
        ),
    )(held, waves, w_in, w_out, w_charge)

    hidden, partial = pl.pallas_call(
        functools.partial(layer_kernel, tile=wide),
        out_shape=(
            jax.ShapeDtypeStruct((own, channels), BF16),
            jax.ShapeDtypeStruct((devices, 2, share), F32),
        ),
        in_specs=[VMEM] * 9,
        out_specs=(VMEM, VMEM),
        scratch_shapes=[
            pltpu.VMEM((4 * half + HALO, channels), BF16),
            pltpu.VMEM((own + 3 * HALO, channels), BF16),
            pltpu.VMEM((own // HALO + 2, 2 * HALO, 2 * LANES), BF16),
        ],
        compiler_params=pltpu.CompilerParams(vmem_limit_bytes=16 << 20),
    )(before, first, last, after, w_first, w_second, w_read, cosine, sine)

    swapped = lax.all_to_all(partial.astype(BF16), AXES, 0, 0, tiled=True)
    mine = jnp.sum(swapped.astype(F32), axis=0).astype(BF16)
    spread = jnp.broadcast_to(mine[None], (devices, 2, share))
    sums = lax.all_to_all(spread, AXES, 0, 0, tiled=True)

    cosine, sine = (pltpu.with_memory_space_constraint(x, pltpu.VMEM) for x in (cosine, sine))
    potential, field = pl.pallas_call(
        functools.partial(response_kernel, tile=wide),
        out_shape=(
            jax.ShapeDtypeStruct((1, own), F32),
            jax.ShapeDtypeStruct((3, own), F32),
        ),
        in_specs=[VMEM] * 4,
        out_specs=(VMEM, VMEM),
        scratch_shapes=[pltpu.VMEM((8, own), F32)],
        compiler_params=pltpu.CompilerParams(vmem_limit_bytes=4 << 20),
    )(sums, coef, cosine, sine)
    return (hidden, potential.reshape(own), field)


def solution(mesh):
    placed = (
        P(AXES, None),
        P(None, AXES),
        P(AXES, None),
        P(AXES),
        P(),
        P(),
        P(),
        P(),
    )
    return jax.shard_map(
        per_device,
        mesh=mesh,
        in_specs=placed,
        out_specs=(P(AXES, None), P(AXES), P(None, AXES)),
        check_vma=False,
    )
```

```python
import functools
import math

import jax
import jax.numpy as jnp
from jax import lax
from jax.experimental import pallas as pl
from jax.experimental.pallas import tpu as pltpu
from jax.sharding import PartitionSpec as P

LAYERS = 2
HALO = 64
AXES = ("brick", "kvec")
LANES = 128
F32 = jnp.float32
BF16 = jnp.bfloat16

VMEM = pl.BlockSpec(memory_space=pltpu.VMEM)
HBM = pl.BlockSpec(memory_space=pltpu.HBM)


def pieces(x):
    first = x.astype(BF16).astype(F32)
    rest = x - first
    second = rest.astype(BF16).astype(F32)
    return first, second, rest - second


def pack_kernel(
    feat_ref, pos_ref, neigh_ref, counts_ref, wave_ref, first_ref, last_ref, waves_ref,
    held_ref, sem,
):
    slots, own = neigh_ref.shape
    channels = feat_ref.shape[1]
    copy = pltpu.make_async_copy(wave_ref, waves_ref, sem)
    copy.start()
    held_ref[...] = pos_ref[...]
    rows = lax.broadcasted_iota(jnp.int32, (slots, own), 1)
    slot = lax.broadcasted_iota(jnp.int32, (slots, own), 0)
    delta = (neigh_ref[...] - HALO - rows).astype(F32)
    delta = jnp.where(slot < counts_ref[...], delta, 0.0)
    zero5 = jnp.zeros((5, own), F32)
    coords = [jnp.concatenate([p, zero5], axis=0) for p in pieces(pos_ref[...])]
    rest = jnp.zeros((LANES - slots - 24, own), F32)
    extra = jnp.concatenate([delta] + coords + [rest], axis=0).astype(BF16)
    half = own // 2
    for ref, start in ((first_ref, 0), (last_ref, half)):
        ref[:, :channels] = feat_ref[start : start + half, :]
        ref[:, channels:] = extra[:, start : start + half]
    copy.wait()


HALF_SINE = (4.438831262995637, -7.228964613368321, 3.149392241482131)


def horner(s, coefs):
    value = coefs[-1] * s + coefs[-2]
    for c in coefs[-3::-1]:
        value = value * s + c
    return value


def trig_kernel(
    pos_ref, wave_ref, w_in_ref, w_out_ref, w_charge_ref, cos_ref, sin_ref, coef_ref, w_in_out,
    w_out_out, w_charge_out, left_ref, even_ref, odd_ref, sems, *, tile, chunk, factor,
):
    own = pos_ref.shape[1]
    total = wave_ref.shape[1]
    copies = [
        pltpu.make_async_copy(source, target, sems.at[n])
        for n, (source, target) in enumerate(
            ((w_in_ref, w_in_out), (w_out_ref, w_out_out), (w_charge_ref, w_charge_out))
        )
    ]
    for copy in copies:
        copy.start()
    zero5 = jnp.zeros((5, own), F32)
    a, b, c = (jnp.concatenate([p, zero5], axis=0) for p in pieces(pos_ref[...]))
    left = jnp.concatenate([a, a, b, b, a, c] + [jnp.zeros((80, own), F32)], axis=0)
    left_ref[...] = left.T.astype(BF16)
    tail5 = jnp.zeros((5, tile), F32)
    count = total // tile
    group = 8

    def place(step):
        return pl.ds(pl.multiple_of(step * tile, tile), tile)

    def phase(step, out_ref):
        turns = wave_ref[:, place(step)] * (0.5 / math.pi)
        u, v, w = (jnp.concatenate([p, tail5], axis=0) for p in pieces(turns))
        right = jnp.concatenate([u, v, u, v, w, u] + [jnp.zeros((80, tile), F32)], axis=0)
        out_ref[...] = jnp.dot(left_ref[...], right.astype(BF16), preferred_element_type=F32)

    def evaluate(step, in_ref):
        span = place(step)
        for start in range(0, own, chunk):
            t = in_ref[start : start + chunk, :]
            r = t - jnp.round(t)
            x = r * horner(r * r, HALF_SINE)
            square = x * x
            rest = 2.000002 - square
            cos_ref[start : start + chunk, span] = (1.0 - square).astype(BF16)
            sin_ref[start : start + chunk, span] = (x * rest * lax.rsqrt(rest)).astype(BF16)

    def scale(step):
        waves = [wave_ref[:, place(step + n)] for n in range(group)]
        ksq = jnp.zeros((group, tile), F32)
        for c in range(3):
            part = jnp.concatenate([w[c : c + 1] for w in waves], axis=0)
            ksq = ksq + part * part
        coef = factor * jnp.exp(-0.1 * ksq) / ksq
        one = jnp.ones((1, tile), F32)
        for n, w in enumerate(waves):
            coef_ref[:, place(step + n)] = coef[n : n + 1] * jnp.concatenate(
                [one, w, one, w], axis=0
            )

    phase(0, even_ref)

    @pl.loop(0, count // group)
    def _(block):
        base = group * block
        scale(base)
        for step in range(0, group, 2):
            phase(base + step + 1, odd_ref)
            evaluate(base + step, even_ref)
            phase(jnp.minimum(base + step + 2, count - 1), even_ref)
            evaluate(base + step + 1, odd_ref)

    for copy in copies:
        copy.wait()


def silu(x):
    return x / (1.0 + jnp.exp(-x))


def layer_kernel(
    before_ref, first_ref, last_ref, after_ref, w_in_ref, w_out_ref, w_charge_ref, cos_ref,
    sin_ref, hidden_ref, sums_ref, feat_ref, mid_ref, matrix_ref, *, tile,
):
    parts = (before_ref, first_ref, last_ref, after_ref)
    half = before_ref.shape[0]
    channels = w_in_ref.shape[1]
    own = 2 * half
    for n, ref in enumerate(parts):
        feat_ref[n * half : (n + 1) * half, :] = ref[:, :channels]
    feat_ref[4 * half :, :] = jnp.zeros((HALO, channels), BF16)
    extras = [ref[:, channels:].astype(F32) for ref in parts]
    rows = [e[64:72] + e[72:80] + e[80:88] for e in extras]
    ext_rows = jnp.concatenate(rows + [jnp.zeros((8, LANES), F32)], axis=1)
    ext_cols = jnp.concatenate([r.T for r in rows], axis=0)
    lane = lax.broadcasted_iota(jnp.int32, (HALO, LANES), 1)
    deep = lax.broadcasted_iota(jnp.int32, (LANES, LANES), 0).astype(F32)
    deltas = [e[:64] for e in extras]
    ends = jnp.where(lane < HALO, deltas[3], deltas[0])
    hists = []
    for delta in (ends, deltas[1], deltas[2]):
        place = jnp.where(delta > 0, delta + 63.0, delta + 64.0)
        place = jnp.where(delta == 0, -1.0, place)
        hist = jnp.zeros((LANES, LANES), F32)
        for slot in range(64):
            hist = hist + jnp.where(deep == place[slot : slot + 1, :], 1.0, 0.0)
        hists.append(hist.T)
    hist_all = (hists[0][HALO:], hists[1][:HALO], hists[1][HALO:], hists[2][:HALO])
    hist_all = hist_all + (hists[2][HALO:], hists[0][:HALO])
    blocks = (own + 2 * HALO) // HALO
    zeros = jnp.zeros((HALO, LANES), F32)
    for block in range(blocks):
        base = HALO * (block + 1)
        hist = hist_all[block]
        low = jnp.concatenate([jnp.where(lane < 64, hist, 0.0), zeros], axis=1)
        high = jnp.concatenate([jnp.where(lane < 64, 0.0, hist), zeros], axis=1)
        counted = pltpu.roll(low, 0, 1, stride=1, stride_axis=0) + pltpu.roll(
            high, 1, 1, stride=1, stride_axis=0
        )
        dist = jnp.zeros((HALO, 2 * LANES), F32)
        for c in range(3):
            there = ext_rows[c : c + 1, HALO * block : HALO * block + 2 * LANES]
            diff = there - ext_cols[base : base + HALO, c : c + 1]
            dist = dist + diff * diff
        weight = counted / (1.0 + dist)
        upper = weight.astype(BF16)
        lower = (weight - upper.astype(F32)).astype(BF16)
        matrix_ref[block, :HALO, :] = upper
        matrix_ref[block, HALO:, :] = lower

    def advance(source_ref, layer, block_ids, row0, residual):
        messages = []
        for block in block_ids:
            start = HALO * (block - row0)
            out = jnp.dot(
                matrix_ref[block],
                source_ref[start : start + 2 * LANES, :],
                preferred_element_type=F32,
            )
            messages.append(out[:HALO] + out[HALO:])
        message = jnp.concatenate(messages, axis=0)
        scale = lax.rsqrt(jnp.mean(message * message, axis=-1, keepdims=True) + 1e-05)
        normed = (message * scale).astype(BF16)
        inner = silu(jnp.dot(normed, w_in_ref[layer], preferred_element_type=F32)).astype(BF16)
        update = jnp.dot(inner, w_out_ref[layer], preferred_element_type=F32)
        return (residual.astype(F32) + update).astype(BF16)

    grown = own + 2 * HALO
    mid_ref[:grown, :] = advance(
        feat_ref, 0, range(blocks), 0, feat_ref[HALO : HALO + grown, :]
    )
    mid_ref[grown:, :] = jnp.zeros((HALO, channels), BF16)
    final = advance(mid_ref, 1, range(1, blocks - 1), 1, mid_ref[HALO : HALO + own, :])
    hidden_ref[...] = final
    reader = jnp.concatenate(
        list(pieces(w_charge_ref[...])) + [jnp.zeros((5, channels), F32)], axis=0
    ).astype(BF16)
    read = lax.dot_general(
        reader, final, (((1,), (1,)), ((), ())), preferred_element_type=F32
    )
    charge = read[0:1] + read[1:2] + read[2:3]
    hi, mid, lo = pieces(charge)
    charges = jnp.concatenate([hi, mid, lo, jnp.zeros((5, own), F32)], axis=0).astype(BF16)

    share = sums_ref.shape[2]
    per = tile // share

    @pl.loop(0, sums_ref.shape[0] // per)
    def _(step):
        span = pl.ds(pl.multiple_of(step * tile, tile), tile)
        both = []
        for ref in (cos_ref, sin_ref):
            part = jnp.dot(charges, ref[:, span], preferred_element_type=F32)
            both.append(part[0:1] + part[1:2] + part[2:3])
        both = jnp.concatenate(both, axis=0).astype(BF16)
        for q in range(per):
            sums_ref[step * per + q] = both[:, q * share : (q + 1) * share]


def sum_kernel(parts_ref, out_ref):
    total = jnp.sum(parts_ref[...].astype(F32), axis=0, keepdims=True)
    out_ref[...] = jnp.broadcast_to(total, parts_ref.shape).astype(BF16)


def response_kernel(sums_ref, coef_ref, cos_ref, sin_ref, pot_ref, field_ref, acc_ref, *, tile):
    groups, _, share = sums_ref.shape
    per = tile // share
    row = lax.broadcasted_iota(jnp.int32, (8, share), 0)
    lead = row % 4 == 0
    upper = row < 4
    dims = (((1,), (1,)), ((), ()))
    acc_ref[...] = jnp.zeros_like(acc_ref)

    @pl.loop(0, groups // per)
    def _(step):
        span = pl.ds(pl.multiple_of(step * tile, tile), tile)
        coef = coef_ref[:, span]
        factors = ([], [])
        for q in range(per):
            scaled = coef[:, q * share : (q + 1) * share]
            sums = sums_ref[step * per + q].astype(F32)
            cosine = sums[0:1]
            sine = sums[1:2]
            for n, (top, other) in enumerate(((cosine, -sine), (sine, cosine))):
                full = scaled * jnp.where(lead, top, other)
                hi = full.astype(BF16).astype(F32)
                factors[n].append(jnp.where(upper, hi, full - hi))
        total = acc_ref[...]
        for n, ref in enumerate((cos_ref, sin_ref)):
            wide = jnp.concatenate(factors[n], axis=1).astype(BF16)
            total = total + lax.dot_general(
                wide, ref[:, span], dims, preferred_element_type=F32
            )
        acc_ref[...] = total

    result = acc_ref[:4] + acc_ref[4:]
    pot_ref[...] = result[0:1]
    field_ref[...] = result[1:4]


def shifted(x, step):
    devices = lax.axis_size(AXES)
    pairs = [(i, i + step) for i in range(devices) if 0 <= i + step < devices]
    return lax.ppermute(x, AXES, pairs)


def per_device(features, positions, neighbours, counts, w_in, w_out, w_charge, wave):
    own, channels = features.shape
    total = wave.shape[1]
    devices = lax.axis_size(AXES)
    half = own // 2
    width = channels + LANES
    share = total // devices
    factor = 4.0 / math.sqrt(own * devices * total)
    wide = 4096
    dma = pltpu.SemaphoreType.DMA
    w_charge = w_charge.reshape(1, channels)
    wave, w_in, w_out, w_charge = (
        pltpu.with_memory_space_constraint(x, pltpu.HBM) for x in (wave, w_in, w_out, w_charge)
    )

    edge = pltpu.VMEM((half, width), BF16)
    first, last, waves, held = pl.pallas_call(
        pack_kernel,
        out_shape=(edge, edge, pltpu.VMEM(wave.shape, F32), pltpu.VMEM(positions.shape, F32)),
        in_specs=[VMEM] * 4 + [HBM],
        out_specs=(VMEM,) * 4,
        scratch_shapes=[dma],
    )(features, positions, neighbours.T, counts.reshape(1, own), wave)
    before = shifted(last, 1)
    after = shifted(first, -1)

    table = pltpu.VMEM((own, total), BF16)
    kept = pltpu.VMEM(w_in.shape, BF16)
    cosine, sine, coef, w_first, w_second, w_read = pl.pallas_call(
        functools.partial(trig_kernel, tile=256, chunk=32, factor=factor),
        out_shape=(table, table, pltpu.VMEM((8, total), F32), kept, kept)
        + (pltpu.VMEM((1, channels), F32),),
        in_specs=[VMEM] * 2 + [HBM] * 3,
        out_specs=(VMEM,) * 6,
        scratch_shapes=[pltpu.VMEM((own, LANES), BF16)]
        + [pltpu.VMEM((own, 256), F32)] * 2
        + [dma((3,))],
        compiler_params=pltpu.CompilerParams(vmem_limit_bytes=16 << 20),
        cost_estimate=pl.CostEstimate(
            flops=own * total * 40, bytes_accessed=4 * own * total, transcendentals=0
        ),
    )(held, waves, w_in, w_out, w_charge)

    hidden, partial = pl.pallas_call(
        functools.partial(layer_kernel, tile=wide),
        out_shape=(
            jax.ShapeDtypeStruct((own, channels), BF16),
            jax.ShapeDtypeStruct((devices, 2, share), BF16),
        ),
        in_specs=[VMEM] * 9,
        out_specs=(VMEM, VMEM),
        scratch_shapes=[
            pltpu.VMEM((4 * half + HALO, channels), BF16),
            pltpu.VMEM((own + 3 * HALO, channels), BF16),
            pltpu.VMEM((own // HALO + 2, 2 * HALO, 2 * LANES), BF16),
        ],
        compiler_params=pltpu.CompilerParams(vmem_limit_bytes=16 << 20),
    )(before, first, last, after, w_first, w_second, w_read, cosine, sine)

    swapped = lax.all_to_all(partial, AXES, 0, 0, tiled=True)
    spread = pl.pallas_call(
        sum_kernel,
        out_shape=jax.ShapeDtypeStruct((devices, 2, share), BF16),
        in_specs=[VMEM],
        out_specs=VMEM,
        compiler_params=pltpu.CompilerParams(vmem_limit_bytes=4 << 20),
    )(swapped)
    sums = lax.all_to_all(spread, AXES, 0, 0, tiled=True)

    cosine, sine = (pltpu.with_memory_space_constraint(x, pltpu.VMEM) for x in (cosine, sine))
    potential, field = pl.pallas_call(
        functools.partial(response_kernel, tile=wide),
        out_shape=(
            jax.ShapeDtypeStruct((1, own), F32),
            jax.ShapeDtypeStruct((3, own), F32),
        ),
        in_specs=[VMEM] * 4,
        out_specs=(VMEM, VMEM),
        scratch_shapes=[pltpu.VMEM((8, own), F32)],
        compiler_params=pltpu.CompilerParams(vmem_limit_bytes=4 << 20),
    )(sums, coef, cosine, sine)
    return (hidden, potential.reshape(own), field)


def solution(mesh):
    placed = (
        P(AXES, None),
        P(None, AXES),
        P(AXES, None),
        P(AXES),
        P(),
        P(),
        P(),
        P(),
    )
    return jax.shard_map(
        per_device,
        mesh=mesh,
        in_specs=placed,
        out_specs=(P(AXES, None), P(AXES), P(None, AXES)),
        check_vma=False,
    )
```

```python
import functools
import math

import jax
import jax.numpy as jnp
from jax import lax
from jax.experimental import pallas as pl
from jax.experimental.pallas import tpu as pltpu
from jax.sharding import PartitionSpec as P

LAYERS = 2
HALO = 64
AXES = ("brick", "kvec")
LANES = 128
F32 = jnp.float32
BF16 = jnp.bfloat16

VMEM = pl.BlockSpec(memory_space=pltpu.VMEM)
HBM = pl.BlockSpec(memory_space=pltpu.HBM)


def pieces(x):
    first = x.astype(BF16).astype(F32)
    rest = x - first
    second = rest.astype(BF16).astype(F32)
    return first, second, rest - second


def pack_kernel(
    feat_ref, pos_ref, neigh_ref, counts_ref, wave_ref, first_ref, last_ref, waves_ref,
    held_ref, sem,
):
    slots, own = neigh_ref.shape
    channels = feat_ref.shape[1]
    copy = pltpu.make_async_copy(wave_ref, waves_ref, sem)
    copy.start()
    held_ref[...] = pos_ref[...]
    rows = lax.broadcasted_iota(jnp.int32, (slots, own), 1)
    slot = lax.broadcasted_iota(jnp.int32, (slots, own), 0)
    delta = (neigh_ref[...] - HALO - rows).astype(F32)
    delta = jnp.where(slot < counts_ref[...], delta, 0.0)
    zero5 = jnp.zeros((5, own), F32)
    coords = [jnp.concatenate([p, zero5], axis=0) for p in pieces(pos_ref[...])]
    rest = jnp.zeros((LANES - slots - 24, own), F32)
    extra = jnp.concatenate([delta] + coords + [rest], axis=0).astype(BF16)
    half = own // 2
    for ref, start in ((first_ref, 0), (last_ref, half)):
        ref[:, :channels] = feat_ref[start : start + half, :]
        ref[:, channels:] = extra[:, start : start + half]
    copy.wait()


HALF_SINE = (4.438831262995637, -7.228964613368321, 3.149392241482131)


def horner(s, coefs):
    value = coefs[-1] * s + coefs[-2]
    for c in coefs[-3::-1]:
        value = value * s + c
    return value


def trig_kernel(
    pos_ref, wave_ref, w_in_ref, w_out_ref, w_charge_ref, cos_ref, sin_ref, coef_ref, w_in_out,
    w_out_out, w_charge_out, left_ref, even_ref, odd_ref, sems, *, tile, chunk, factor,
):
    own = pos_ref.shape[1]
    total = wave_ref.shape[1]
    copies = [
        pltpu.make_async_copy(source, target, sems.at[n])
        for n, (source, target) in enumerate(
            ((w_in_ref, w_in_out), (w_out_ref, w_out_out), (w_charge_ref, w_charge_out))
        )
    ]
    for copy in copies:
        copy.start()
    zero5 = jnp.zeros((5, own), F32)
    a, b, c = (jnp.concatenate([p, zero5], axis=0) for p in pieces(pos_ref[...]))
    left = jnp.concatenate([a, a, b, b, a, c] + [jnp.zeros((80, own), F32)], axis=0)
    left_ref[...] = left.T.astype(BF16)
    tail5 = jnp.zeros((5, tile), F32)
    count = total // tile
    group = 8

    def place(step):
        return pl.ds(pl.multiple_of(step * tile, tile), tile)

    def phase(step, out_ref):
        turns = wave_ref[:, place(step)] * (0.5 / math.pi)
        u, v, w = (jnp.concatenate([p, tail5], axis=0) for p in pieces(turns))
        right = jnp.concatenate([u, v, u, v, w, u] + [jnp.zeros((80, tile), F32)], axis=0)
        out_ref[...] = jnp.dot(left_ref[...], right.astype(BF16), preferred_element_type=F32)

    def evaluate(step, in_ref):
        span = place(step)
        for start in range(0, own, chunk):
            t = in_ref[start : start + chunk, :]
            r = t - jnp.round(t)
            x = r * horner(r * r, HALF_SINE)
            square = x * x
            rest = 2.000002 - square
            cos_ref[start : start + chunk, span] = (1.0 - square).astype(BF16)
            sin_ref[start : start + chunk, span] = (x * rest * lax.rsqrt(rest)).astype(BF16)

    def scale(step):
        waves = [wave_ref[:, place(step + n)] for n in range(group)]
        ksq = jnp.zeros((group, tile), F32)
        for c in range(3):
            part = jnp.concatenate([w[c : c + 1] for w in waves], axis=0)
            ksq = ksq + part * part
        coef = factor * jnp.exp(-0.1 * ksq) / ksq
        one = jnp.ones((1, tile), F32)
        for n, w in enumerate(waves):
            coef_ref[:, place(step + n)] = coef[n : n + 1] * jnp.concatenate(
                [one, w, one, w], axis=0
            )

    phase(0, even_ref)

    @pl.loop(0, count // group)
    def _(block):
        base = group * block
        scale(base)
        for step in range(0, group, 2):
            phase(base + step + 1, odd_ref)
            evaluate(base + step, even_ref)
            phase(jnp.minimum(base + step + 2, count - 1), even_ref)
            evaluate(base + step + 1, odd_ref)

    for copy in copies:
        copy.wait()


def silu(x):
    return x / (1.0 + jnp.exp(-x))


def layer_kernel(
    before_ref, first_ref, last_ref, after_ref, w_in_ref, w_out_ref, w_charge_ref, cos_ref,
    sin_ref, hidden_ref, sums_ref, feat_ref, mid_ref, matrix_ref, *, tile,
):
    parts = (before_ref, first_ref, last_ref, after_ref)
    half = before_ref.shape[0]
    channels = w_in_ref.shape[1]
    own = 2 * half
    for n, ref in enumerate(parts):
        feat_ref[n * half : (n + 1) * half, :] = ref[:, :channels]
    feat_ref[4 * half :, :] = jnp.zeros((HALO, channels), BF16)
    extras = [ref[:, channels:].astype(F32) for ref in parts]
    rows = [e[64:72] + e[72:80] + e[80:88] for e in extras]
    ext_rows = jnp.concatenate(rows + [jnp.zeros((8, LANES), F32)], axis=1)
    ext_cols = jnp.concatenate([r.T for r in rows], axis=0)
    lane = lax.broadcasted_iota(jnp.int32, (HALO, LANES), 1)
    deep = lax.broadcasted_iota(jnp.int32, (LANES, LANES), 0).astype(F32)
    deltas = [e[:64] for e in extras]
    ends = jnp.where(lane < HALO, deltas[3], deltas[0])
    hists = []
    for delta in (ends, deltas[1], deltas[2]):
        place = jnp.where(delta > 0, delta + 63.0, delta + 64.0)
        place = jnp.where(delta == 0, -1.0, place)
        hist = jnp.zeros((LANES, LANES), F32)
        for slot in range(64):
            hist = hist + jnp.where(deep == place[slot : slot + 1, :], 1.0, 0.0)
        hists.append(hist.T)
    hist_all = (hists[0][HALO:], hists[1][:HALO], hists[1][HALO:], hists[2][:HALO])
    hist_all = hist_all + (hists[2][HALO:], hists[0][:HALO])
    blocks = (own + 2 * HALO) // HALO
    zeros = jnp.zeros((HALO, LANES), F32)
    for block in range(blocks):
        base = HALO * (block + 1)
        hist = hist_all[block]
        low = jnp.concatenate([jnp.where(lane < 64, hist, 0.0), zeros], axis=1)
        high = jnp.concatenate([jnp.where(lane < 64, 0.0, hist), zeros], axis=1)
        counted = pltpu.roll(low, 0, 1, stride=1, stride_axis=0) + pltpu.roll(
            high, 1, 1, stride=1, stride_axis=0
        )
        dist = jnp.zeros((HALO, 2 * LANES), F32)
        for c in range(3):
            there = ext_rows[c : c + 1, HALO * block : HALO * block + 2 * LANES]
            diff = there - ext_cols[base : base + HALO, c : c + 1]
            dist = dist + diff * diff
        weight = counted / (1.0 + dist)
        upper = weight.astype(BF16)
        lower = (weight - upper.astype(F32)).astype(BF16)
        matrix_ref[block, :HALO, :] = upper
        matrix_ref[block, HALO:, :] = lower

    def advance(source_ref, layer, block_ids, row0, residual):
        messages = []
        for block in block_ids:
            start = HALO * (block - row0)
            out = jnp.dot(
                matrix_ref[block],
                source_ref[start : start + 2 * LANES, :],
                preferred_element_type=F32,
            )
            messages.append(out[:HALO] + out[HALO:])
        message = jnp.concatenate(messages, axis=0)
        scale = lax.rsqrt(jnp.mean(message * message, axis=-1, keepdims=True) + 1e-05)
        normed = (message * scale).astype(BF16)
        inner = silu(jnp.dot(normed, w_in_ref[layer], preferred_element_type=F32)).astype(BF16)
        update = jnp.dot(inner, w_out_ref[layer], preferred_element_type=F32)
        return (residual.astype(F32) + update).astype(BF16)

    grown = own + 2 * HALO
    mid_ref[:grown, :] = advance(
        feat_ref, 0, range(blocks), 0, feat_ref[HALO : HALO + grown, :]
    )
    mid_ref[grown:, :] = jnp.zeros((HALO, channels), BF16)
    final = advance(mid_ref, 1, range(1, blocks - 1), 1, mid_ref[HALO : HALO + own, :])
    hidden_ref[...] = final
    reader = jnp.concatenate(
        list(pieces(w_charge_ref[...])) + [jnp.zeros((5, channels), F32)], axis=0
    ).astype(BF16)
    read = lax.dot_general(
        reader, final, (((1,), (1,)), ((), ())), preferred_element_type=F32
    )
    charge = read[0:1] + read[1:2] + read[2:3]
    hi, mid, lo = pieces(charge)
    charges = jnp.concatenate([hi, mid, lo, jnp.zeros((5, own), F32)], axis=0).astype(BF16)

    share = sums_ref.shape[2]
    per = tile // share

    @pl.loop(0, sums_ref.shape[0] // per)
    def _(step):
        span = pl.ds(pl.multiple_of(step * tile, tile), tile)
        both = []
        for ref in (cos_ref, sin_ref):
            part = jnp.dot(charges, ref[:, span], preferred_element_type=F32)
            both.append(part[0:1] + part[1:2] + part[2:3])
        both = jnp.concatenate(both, axis=0).astype(BF16)
        for q in range(per):
            sums_ref[step * per + q] = both[:, q * share : (q + 1) * share]


def sum_kernel(parts_ref, out_ref):
    total = jnp.sum(parts_ref[...].astype(F32), axis=0, keepdims=True)
    out_ref[...] = jnp.broadcast_to(total, parts_ref.shape).astype(BF16)


def response_kernel(sums_ref, coef_ref, cos_ref, sin_ref, pot_ref, field_ref, acc_ref, *, tile):
    groups, _, share = sums_ref.shape
    per = tile // share
    row = lax.broadcasted_iota(jnp.int32, (8, share), 0)
    lead = row % 4 == 0
    upper = row < 4
    dims = (((1,), (1,)), ((), ()))
    acc_ref[...] = jnp.zeros_like(acc_ref)

    @pl.loop(0, groups // per)
    def _(step):
        span = pl.ds(pl.multiple_of(step * tile, tile), tile)
        coef = coef_ref[:, span]
        factors = ([], [])
        for q in range(per):
            scaled = coef[:, q * share : (q + 1) * share]
            sums = sums_ref[step * per + q].astype(F32)
            cosine = sums[0:1]
            sine = sums[1:2]
            for n, (top, other) in enumerate(((cosine, -sine), (sine, cosine))):
                full = scaled * jnp.where(lead, top, other)
                hi = full.astype(BF16).astype(F32)
                factors[n].append(jnp.where(upper, hi, full - hi))
        total = acc_ref[...]
        for n, ref in enumerate((cos_ref, sin_ref)):
            wide = jnp.concatenate(factors[n], axis=1).astype(BF16)
            total = total + lax.dot_general(
                wide, ref[:, span], dims, preferred_element_type=F32
            )
        acc_ref[...] = total

    result = acc_ref[:4] + acc_ref[4:]
    pot_ref[...] = result[0:1]
    field_ref[...] = result[1:4]


def shifted(x, step):
    devices = lax.axis_size(AXES)
    pairs = [(i, i + step) for i in range(devices) if 0 <= i + step < devices]
    return lax.ppermute(x, AXES, pairs)


def per_device(features, positions, neighbours, counts, w_in, w_out, w_charge, wave):
    own, channels = features.shape
    total = wave.shape[1]
    devices = lax.axis_size(AXES)
    half = own // 2
    width = channels + LANES
    share = total // devices
    factor = 4.0 / math.sqrt(own * devices * total)
    wide = 4096
    dma = pltpu.SemaphoreType.DMA
    w_charge = w_charge.reshape(1, channels)
    wave, w_in, w_out, w_charge = (
        pltpu.with_memory_space_constraint(x, pltpu.HBM) for x in (wave, w_in, w_out, w_charge)
    )

    edge = pltpu.VMEM((half, width), BF16)
    first, last, waves, held = pl.pallas_call(
        pack_kernel,
        out_shape=(edge, edge, pltpu.VMEM(wave.shape, F32), pltpu.VMEM(positions.shape, F32)),
        in_specs=[VMEM] * 4 + [HBM],
        out_specs=(VMEM,) * 4,
        scratch_shapes=[dma],
    )(features, positions, neighbours.T, counts.reshape(1, own), wave)
    before = shifted(last, 1)
    after = shifted(first, -1)

    table = pltpu.VMEM((own, total), BF16)
    kept = pltpu.VMEM(w_in.shape, BF16)
    cosine, sine, coef, w_first, w_second, w_read = pl.pallas_call(
        functools.partial(trig_kernel, tile=256, chunk=32, factor=factor),
        out_shape=(table, table, pltpu.VMEM((8, total), F32), kept, kept)
        + (pltpu.VMEM((1, channels), F32),),
        in_specs=[VMEM] * 2 + [HBM] * 3,
        out_specs=(VMEM,) * 6,
        scratch_shapes=[pltpu.VMEM((own, LANES), BF16)]
        + [pltpu.VMEM((own, 256), F32)] * 2
        + [dma((3,))],
        compiler_params=pltpu.CompilerParams(vmem_limit_bytes=16 << 20),
        cost_estimate=pl.CostEstimate(
            flops=own * total * 40, bytes_accessed=4 * own * total, transcendentals=0
        ),
    )(held, waves, w_in, w_out, w_charge)

    hidden, partial = pl.pallas_call(
        functools.partial(layer_kernel, tile=wide),
        out_shape=(
            jax.ShapeDtypeStruct((own, channels), BF16),
            jax.ShapeDtypeStruct((devices, 2, share), BF16),
        ),
        in_specs=[VMEM] * 9,
        out_specs=(VMEM, VMEM),
        scratch_shapes=[
            pltpu.VMEM((4 * half + HALO, channels), BF16),
            pltpu.VMEM((own + 3 * HALO, channels), BF16),
            pltpu.VMEM((own // HALO + 2, 2 * HALO, 2 * LANES), BF16),
        ],
        compiler_params=pltpu.CompilerParams(vmem_limit_bytes=16 << 20),
    )(before, first, last, after, w_first, w_second, w_read, cosine, sine)

    swapped = lax.all_to_all(partial, AXES, 0, 0, tiled=True)
    spread = pl.pallas_call(
        sum_kernel,
        out_shape=jax.ShapeDtypeStruct((devices, 2, share), BF16),
        in_specs=[VMEM],
        out_specs=VMEM,
        compiler_params=pltpu.CompilerParams(vmem_limit_bytes=4 << 20),
    )(swapped)
    near = lax.axis_size("kvec")
    sums = lax.all_to_all(spread[:near], "kvec", 0, 0, tiled=True)
    sums = jnp.broadcast_to(sums[None], (devices // near, near, 2, share))
    sums = lax.all_to_all(sums, "brick", 0, 0, tiled=True).reshape(devices, 2, share)

    cosine, sine = (pltpu.with_memory_space_constraint(x, pltpu.VMEM) for x in (cosine, sine))
    potential, field = pl.pallas_call(
        functools.partial(response_kernel, tile=wide),
        out_shape=(
            jax.ShapeDtypeStruct((1, own), F32),
            jax.ShapeDtypeStruct((3, own), F32),
        ),
        in_specs=[VMEM] * 4,
        out_specs=(VMEM, VMEM),
        scratch_shapes=[pltpu.VMEM((8, own), F32)],
        compiler_params=pltpu.CompilerParams(vmem_limit_bytes=4 << 20),
    )(sums, coef, cosine, sine)
    return (hidden, potential.reshape(own), field)


def solution(mesh):
    placed = (
        P(AXES, None),
        P(None, AXES),
        P(AXES, None),
        P(AXES),
        P(),
        P(),
        P(),
        P(),
    )
    return jax.shard_map(
        per_device,
        mesh=mesh,
        in_specs=placed,
        out_specs=(P(AXES, None), P(AXES), P(None, AXES)),
        check_vma=False,
    )
```

```python
import functools
import math

import jax
import jax.numpy as jnp
from jax import lax
from jax.experimental import pallas as pl
from jax.experimental.pallas import tpu as pltpu
from jax.sharding import PartitionSpec as P

LAYERS = 2
HALO = 64
AXES = ("brick", "kvec")
LANES = 128
F32 = jnp.float32
BF16 = jnp.bfloat16

VMEM = pl.BlockSpec(memory_space=pltpu.VMEM)
HBM = pl.BlockSpec(memory_space=pltpu.HBM)


def pieces(x):
    first = x.astype(BF16).astype(F32)
    rest = x - first
    second = rest.astype(BF16).astype(F32)
    return first, second, rest - second


def pack_kernel(
    feat_ref, pos_ref, neigh_ref, counts_ref, wave_ref, first_ref, last_ref, waves_ref,
    held_ref, sem,
):
    slots, own = neigh_ref.shape
    channels = feat_ref.shape[1]
    copy = pltpu.make_async_copy(wave_ref, waves_ref, sem)
    copy.start()
    held_ref[...] = pos_ref[...]
    rows = lax.broadcasted_iota(jnp.int32, (slots, own), 1)
    slot = lax.broadcasted_iota(jnp.int32, (slots, own), 0)
    delta = (neigh_ref[...] - HALO - rows).astype(F32)
    delta = jnp.where(slot < counts_ref[...], delta, 0.0)
    zero5 = jnp.zeros((5, own), F32)
    coords = [jnp.concatenate([p, zero5], axis=0) for p in pieces(pos_ref[...])]
    rest = jnp.zeros((LANES - slots - 24, own), F32)
    extra = jnp.concatenate([delta] + coords + [rest], axis=0).astype(BF16)
    half = own // 2
    for ref, start in ((first_ref, 0), (last_ref, half)):
        ref[:, :channels] = feat_ref[start : start + half, :]
        ref[:, channels:] = extra[:, start : start + half]
    copy.wait()


HALF_SINE = (4.438831262995637, -7.228964613368321, 3.149392241482131)


def horner(s, coefs):
    value = coefs[-1] * s + coefs[-2]
    for c in coefs[-3::-1]:
        value = value * s + c
    return value


def atom_pieces(pos_ref):
    a, b, c = pieces(pos_ref[...])
    own = pos_ref.shape[1]
    left = jnp.concatenate([a, a, b, b, a, c, jnp.zeros((14, own), F32)], axis=0)
    return left.astype(BF16)


def place(step, tile):
    return pl.ds(pl.multiple_of(step * tile, tile), tile)


def phase(wave, left_ref, out_ref):
    tile = wave.shape[1]
    u, v, w = pieces(wave * (0.5 / math.pi))
    right = jnp.concatenate([u, v, u, v, w, u, jnp.zeros((14, tile), F32)], axis=0)
    out_ref[...] = jnp.dot(right.T.astype(BF16), left_ref[...], preferred_element_type=F32)


def evaluate(in_ref, stores, chunk):
    for start in range(0, in_ref.shape[0], chunk):
        t = in_ref[start : start + chunk, :]
        r = t - jnp.round(t)
        x = r * horner(r * r, HALF_SINE)
        square = x * x
        rest = 2.000002 - square
        cosine = (1.0 - square).astype(BF16)
        sine = (x * rest * lax.rsqrt(rest)).astype(BF16)
        for store in stores:
            store(start, cosine, sine)


def into_table(cos_ref, sin_ref, step, tile, chunk):
    def store(start, cosine, sine):
        rows = pl.ds(pl.multiple_of(step * tile + start, chunk), chunk)
        cos_ref[rows, :] = cosine
        sin_ref[rows, :] = sine

    return store


def into_tile(tile_ref, chunk):
    def store(start, cosine, sine):
        tile_ref[0, start : start + chunk, :] = cosine
        tile_ref[1, start : start + chunk, :] = sine

    return store


def histogram(delta):
    place = jnp.where(delta > 0, delta + 63.0, delta + 64.0)
    place = jnp.where(delta == 0, -1.0, place)
    deep = lax.broadcasted_iota(jnp.int32, (LANES, LANES), 0).astype(F32)
    hist = jnp.zeros((LANES, LANES), F32)
    for slot in range(64):
        hist = hist + jnp.where(deep == place[slot : slot + 1, :], 1.0, 0.0)
    return hist.T


def early_kernel(
    pos_ref, wave_ref, first_ref, last_ref, w_in_ref, w_out_ref, w_charge_ref, cos_ref, sin_ref,
    coef_ref, hist_ref, w_in_out, w_out_out, w_charge_out, left_ref, even_ref, odd_ref, sems,
    *, tile, chunk, factor,
):
    copies = [
        pltpu.make_async_copy(source, target, sems.at[n])
        for n, (source, target) in enumerate(
            ((w_in_ref, w_in_out), (w_out_ref, w_out_out), (w_charge_ref, w_charge_out))
        )
    ]
    for copy in copies:
        copy.start()
    left_ref[...] = atom_pieces(pos_ref)
    channels = w_in_ref.shape[1]
    for n, ref in enumerate((first_ref, last_ref)):
        hist_ref[n * LANES : (n + 1) * LANES, :] = histogram(ref[:64, channels:].astype(F32))
    head = cos_ref.shape[0] // tile
    group = 8

    def scale(step):
        waves = [wave_ref[:, place(step + n, tile)] for n in range(group)]
        ksq = jnp.zeros((group, tile), F32)
        for c in range(3):
            part = jnp.concatenate([w[c : c + 1] for w in waves], axis=0)
            ksq = ksq + part * part
        coef = factor * jnp.exp(-0.1 * ksq) / ksq
        one = jnp.ones((1, tile), F32)
        for n, w in enumerate(waves):
            coef_ref[:, place(step + n, tile)] = coef[n : n + 1] * jnp.concatenate(
                [one, w, one, w], axis=0
            )

    def turn(step, out_ref):
        phase(wave_ref[:, place(step, tile)], left_ref, out_ref)

    turn(0, even_ref)

    @pl.loop(0, head // 4)
    def _(block):
        base = 4 * block
        scale(4 * base)
        scale(4 * base + group)
        for step in range(0, 4, 2):
            turn(base + step + 1, odd_ref)
            evaluate(even_ref, [into_table(cos_ref, sin_ref, base + step, tile, chunk)], chunk)
            turn(jnp.minimum(base + step + 2, head - 1), even_ref)
            evaluate(odd_ref, [into_table(cos_ref, sin_ref, base + step + 1, tile, chunk)], chunk)

    for copy in copies:
        copy.wait()


def silu(x):
    return x / (1.0 + jnp.exp(-x))


def layer_kernel(
    before_ref, first_ref, last_ref, after_ref, w_in_ref, w_out_ref, w_charge_ref, hist_ref,
    pos_ref, wave_ref, cos_head_ref, sin_head_ref, hidden_ref, sums_ref, cos_ref, sin_ref,
    feat_ref, mid_ref, matrix_ref, left_ref, charge_ref, even_ref, odd_ref, even_tile_ref,
    odd_tile_ref, *, tile, chunk,
):
    parts = (before_ref, first_ref, last_ref, after_ref)
    half = before_ref.shape[0]
    channels = w_in_ref.shape[1]
    own = 2 * half
    for n, ref in enumerate(parts):
        feat_ref[n * half : (n + 1) * half, :] = ref[:, :channels]
    feat_ref[4 * half :, :] = jnp.zeros((HALO, channels), BF16)
    extras = [ref[:, channels:].astype(F32) for ref in parts]
    rows = [e[64:72] + e[72:80] + e[80:88] for e in extras]
    ext_rows = jnp.concatenate(rows + [jnp.zeros((8, LANES), F32)], axis=1)
    ext_cols = jnp.concatenate([r.T for r in rows], axis=0)
    lane = lax.broadcasted_iota(jnp.int32, (HALO, LANES), 1)
    ends = histogram(jnp.where(lane < HALO, extras[3][:64], extras[0][:64]))
    inner = [hist_ref[n * HALO : (n + 1) * HALO, :] for n in range(own // HALO)]
    hist_all = [ends[HALO:]] + inner + [ends[:HALO]]
    blocks = (own + 2 * HALO) // HALO
    zeros = jnp.zeros((HALO, LANES), F32)
    for block in range(blocks):
        base = HALO * (block + 1)
        hist = hist_all[block]
        low = jnp.concatenate([jnp.where(lane < 64, hist, 0.0), zeros], axis=1)
        high = jnp.concatenate([jnp.where(lane < 64, 0.0, hist), zeros], axis=1)
        counted = pltpu.roll(low, 0, 1, stride=1, stride_axis=0) + pltpu.roll(
            high, 1, 1, stride=1, stride_axis=0
        )
        dist = jnp.zeros((HALO, 2 * LANES), F32)
        for c in range(3):
            there = ext_rows[c : c + 1, HALO * block : HALO * block + 2 * LANES]
            diff = there - ext_cols[base : base + HALO, c : c + 1]
            dist = dist + diff * diff
        weight = counted / (1.0 + dist)
        upper = weight.astype(BF16)
        lower = (weight - upper.astype(F32)).astype(BF16)
        matrix_ref[block, :HALO, :] = upper
        matrix_ref[block, HALO:, :] = lower

    def advance(source_ref, layer, block_ids, row0, residual):
        messages = []
        for block in block_ids:
            start = HALO * (block - row0)
            out = jnp.dot(
                matrix_ref[block],
                source_ref[start : start + 2 * LANES, :],
                preferred_element_type=F32,
            )
            messages.append(out[:HALO] + out[HALO:])
        message = jnp.concatenate(messages, axis=0)
        scale = lax.rsqrt(jnp.mean(message * message, axis=-1, keepdims=True) + 1e-05)
        normed = (message * scale).astype(BF16)
        inner = silu(jnp.dot(normed, w_in_ref[layer], preferred_element_type=F32)).astype(BF16)
        update = jnp.dot(inner, w_out_ref[layer], preferred_element_type=F32)
        return (residual.astype(F32) + update).astype(BF16)

    grown = own + 2 * HALO
    mid_ref[:grown, :] = advance(
        feat_ref, 0, range(blocks), 0, feat_ref[HALO : HALO + grown, :]
    )
    mid_ref[grown:, :] = jnp.zeros((HALO, channels), BF16)
    final = advance(mid_ref, 1, range(1, blocks - 1), 1, mid_ref[HALO : HALO + own, :])
    hidden_ref[...] = final
    reader = jnp.concatenate(
        list(pieces(w_charge_ref[...])) + [jnp.zeros((5, channels), F32)], axis=0
    ).astype(BF16)
    read = lax.dot_general(
        reader, final, (((1,), (1,)), ((), ())), preferred_element_type=F32
    )
    charge = read[0:1] + read[1:2] + read[2:3]
    hi, mid, lo = pieces(charge)
    charges = jnp.concatenate([hi, mid, lo, jnp.zeros((5, own), F32)], axis=0).astype(BF16)

    charge_ref[...] = charges
    left_ref[...] = atom_pieces(pos_ref)
    head = cos_head_ref.shape[0] // tile
    late = cos_ref.shape[0] // tile
    share = sums_ref.shape[2]
    per = 2 * tile // share
    dims = (((1,), (1,)), ((), ()))

    def turn(step, out_ref):
        phase(wave_ref[:, place(head + step, tile)], left_ref, out_ref)

    def added(table):
        part = lax.dot_general(charge_ref[...], table, dims, preferred_element_type=F32)
        return part[0:1] + part[1:2] + part[2:3]

    def keep(index, pair):
        for q in range(per):
            sums_ref[index * per + q] = pair[:, q * share : (q + 1) * share].astype(BF16)

    def joined(parts):
        return jnp.concatenate(
            [jnp.concatenate(list(row), axis=1) for row in zip(*parts)], axis=0
        )

    turn(0, even_ref)

    @pl.loop(0, head // 2)
    def _(block):
        parts = []
        for n in range(2):
            rows = place(2 * block + n, tile)
            parts.append((added(cos_head_ref[rows, :]), added(sin_head_ref[rows, :])))
        keep(block, joined(parts))
        for pair in range(3):
            step = 6 * block + 2 * pair
            turn(step + 1, odd_ref)
            evaluate(
                even_ref,
                [into_table(cos_ref, sin_ref, step, tile, chunk), into_tile(even_tile_ref, chunk)],
                chunk,
            )
            turn(jnp.minimum(step + 2, late - 1), even_ref)
            parts = [(added(even_tile_ref[0]), added(even_tile_ref[1]))]
            evaluate(
                odd_ref,
                [
                    into_table(cos_ref, sin_ref, step + 1, tile, chunk),
                    into_tile(odd_tile_ref, chunk),
                ],
                chunk,
            )
            parts.append((added(odd_tile_ref[0]), added(odd_tile_ref[1])))
            keep(head // 2 + 3 * block + pair, joined(parts))


def sum_kernel(parts_ref, out_ref):
    total = jnp.sum(parts_ref[...].astype(F32), axis=0, keepdims=True)
    out_ref[...] = jnp.broadcast_to(total, parts_ref.shape).astype(BF16)


def response_kernel(
    sums_ref, coef_ref, cos_head_ref, sin_head_ref, cos_ref, sin_ref, pot_ref, field_ref, *, tile
):
    share = sums_ref.shape[2]
    per = tile // share
    row = lax.broadcasted_iota(jnp.int32, (8, share), 0)
    lead = row % 4 == 0
    upper = row < 4
    totals = []
    segments = [(cos_head_ref, sin_head_ref, k) for k in range(0, cos_head_ref.shape[0], tile)]
    segments += [(cos_ref, sin_ref, k) for k in range(0, cos_ref.shape[0], tile)]
    for index, (cos_part, sin_part, start) in enumerate(segments):
        factors = ([], [])
        for q in range(index * per, (index + 1) * per):
            scaled = coef_ref[:, q * share : (q + 1) * share]
            sums = sums_ref[q].astype(F32)
            cosine = sums[0:1]
            sine = sums[1:2]
            for n, (top, other) in enumerate(((cosine, -sine), (sine, cosine))):
                full = scaled * jnp.where(lead, top, other)
                hi = full.astype(BF16).astype(F32)
                factors[n].append(jnp.where(upper, hi, full - hi))
        for n, ref in enumerate((cos_part, sin_part)):
            wide = jnp.concatenate(factors[n], axis=1).astype(BF16)
            totals.append(
                jnp.dot(wide, ref[start : start + tile, :], preferred_element_type=F32)
            )
    total = sum(totals[1:], totals[0])
    result = total[:4] + total[4:]
    pot_ref[...] = result[0:1]
    field_ref[...] = result[1:4]


def shifted(x, step):
    devices = lax.axis_size(AXES)
    pairs = [(i, i + step) for i in range(devices) if 0 <= i + step < devices]
    return lax.ppermute(x, AXES, pairs)


def per_device(features, positions, neighbours, counts, w_in, w_out, w_charge, wave):
    own, channels = features.shape
    total = wave.shape[1]
    devices = lax.axis_size(AXES)
    half = own // 2
    width = channels + LANES
    share = total // devices
    factor = 4.0 / math.sqrt(own * devices * total)
    dma = pltpu.SemaphoreType.DMA
    w_charge = w_charge.reshape(1, channels)
    wave, w_in, w_out, w_charge = (
        pltpu.with_memory_space_constraint(x, pltpu.HBM) for x in (wave, w_in, w_out, w_charge)
    )

    edge = pltpu.VMEM((half, width), BF16)
    first, last, waves, held = pl.pallas_call(
        pack_kernel,
        out_shape=(edge, edge, pltpu.VMEM(wave.shape, F32), pltpu.VMEM(positions.shape, F32)),
        in_specs=[VMEM] * 4 + [HBM],
        out_specs=(VMEM,) * 4,
        scratch_shapes=[dma],
    )(features, positions, neighbours.T, counts.reshape(1, own), wave)
    before = shifted(last, 1)
    after = shifted(first, -1)

    early = total // 4
    tile, chunk = 256, 32
    kept = pltpu.VMEM(w_in.shape, BF16)
    table = pltpu.VMEM((early, own), BF16)
    phases = [pltpu.VMEM((tile, own), F32)] * 2
    grant = pltpu.CompilerParams(vmem_limit_bytes=16 << 20)
    cos_head, sin_head, coef, hist, w_first, w_second, w_read = pl.pallas_call(
        functools.partial(early_kernel, tile=tile, chunk=chunk, factor=factor),
        out_shape=(
            table,
            table,
            pltpu.VMEM((8, total), F32),
            pltpu.VMEM((own, LANES), F32),
            kept,
            kept,
            pltpu.VMEM((1, channels), F32),
        ),
        in_specs=[VMEM] * 4 + [HBM] * 3,
        out_specs=(VMEM,) * 7,
        scratch_shapes=[pltpu.VMEM((32, own), BF16)] + phases + [dma((3,))],
        compiler_params=grant,
        cost_estimate=pl.CostEstimate(
            flops=own * early * 40, bytes_accessed=4 * own * early, transcendentals=0
        ),
    )(held, waves, first, last, w_in, w_out, w_charge)

    table = pltpu.VMEM((total - early, own), BF16)
    hidden, partial, cos_late, sin_late = pl.pallas_call(
        functools.partial(layer_kernel, tile=tile, chunk=chunk),
        out_shape=(
            jax.ShapeDtypeStruct((own, channels), BF16),
            jax.ShapeDtypeStruct((devices, 2, share), BF16),
            table,
            table,
        ),
        in_specs=[VMEM] * 12,
        out_specs=(VMEM,) * 4,
        scratch_shapes=[
            pltpu.VMEM((4 * half + HALO, channels), BF16),
            pltpu.VMEM((own + 3 * HALO, channels), BF16),
            pltpu.VMEM((own // HALO + 2, 2 * HALO, 2 * LANES), BF16),
            pltpu.VMEM((32, own), BF16),
            pltpu.VMEM((8, own), BF16),
        ]
        + phases
        + [pltpu.VMEM((2, tile, own), BF16)] * 2,
        compiler_params=grant,
    )(before, first, last, after, w_first, w_second, w_read, hist, held, waves, cos_head, sin_head)

    swapped = lax.all_to_all(partial, AXES, 0, 0, tiled=True)
    spread = pl.pallas_call(
        sum_kernel,
        out_shape=jax.ShapeDtypeStruct((devices, 2, share), BF16),
        in_specs=[VMEM],
        out_specs=VMEM,
        compiler_params=pltpu.CompilerParams(vmem_limit_bytes=4 << 20),
    )(swapped)
    sums = lax.all_to_all(spread, AXES, 0, 0, tiled=True)

    tables = [
        pltpu.with_memory_space_constraint(x, pltpu.VMEM)
        for x in (cos_head, sin_head, cos_late, sin_late)
    ]
    potential, field = pl.pallas_call(
        functools.partial(response_kernel, tile=4096),
        out_shape=(
            jax.ShapeDtypeStruct((1, own), F32),
            jax.ShapeDtypeStruct((3, own), F32),
        ),
        in_specs=[VMEM] * 6,
        out_specs=(VMEM, VMEM),
        compiler_params=pltpu.CompilerParams(vmem_limit_bytes=4 << 20),
    )(sums, coef, *tables)
    return (hidden, potential.reshape(own), field)


def solution(mesh):
    placed = (
        P(AXES, None),
        P(None, AXES),
        P(AXES, None),
        P(AXES),
        P(),
        P(),
        P(),
        P(),
    )
    return jax.shard_map(
        per_device,
        mesh=mesh,
        in_specs=placed,
        out_specs=(P(AXES, None), P(AXES), P(None, AXES)),
        check_vma=False,
    )
```

```python
import functools
import math

import jax
import jax.numpy as jnp
from jax import lax
from jax.experimental import pallas as pl
from jax.experimental.pallas import tpu as pltpu
from jax.sharding import PartitionSpec as P

LAYERS = 2
HALO = 64
AXES = ("brick", "kvec")
LANES = 128
F32 = jnp.float32
BF16 = jnp.bfloat16

VMEM = pl.BlockSpec(memory_space=pltpu.VMEM)
HBM = pl.BlockSpec(memory_space=pltpu.HBM)


def pieces(x):
    first = x.astype(BF16).astype(F32)
    rest = x - first
    second = rest.astype(BF16).astype(F32)
    return first, second, rest - second


def pack_kernel(
    feat_ref, pos_ref, neigh_ref, counts_ref, wave_ref, first_ref, last_ref, waves_ref,
    held_ref, sem,
):
    slots, own = neigh_ref.shape
    channels = feat_ref.shape[1]
    copy = pltpu.make_async_copy(wave_ref, waves_ref, sem)
    copy.start()
    held_ref[...] = pos_ref[...]
    rows = lax.broadcasted_iota(jnp.int32, (slots, own), 1)
    slot = lax.broadcasted_iota(jnp.int32, (slots, own), 0)
    delta = (neigh_ref[...] - HALO - rows).astype(F32)
    delta = jnp.where(slot < counts_ref[...], delta, 0.0)
    zero5 = jnp.zeros((5, own), F32)
    coords = [jnp.concatenate([p, zero5], axis=0) for p in pieces(pos_ref[...])]
    rest = jnp.zeros((LANES - slots - 24, own), F32)
    extra = jnp.concatenate([delta] + coords + [rest], axis=0).astype(BF16)
    half = own // 2
    for ref, start in ((first_ref, 0), (last_ref, half)):
        ref[:, :channels] = feat_ref[start : start + half, :]
        ref[:, channels:] = extra[:, start : start + half]
    copy.wait()


HALF_SINE = (4.438831262995637, -7.228964613368321, 3.149392241482131)


def horner(s, coefs):
    value = coefs[-1] * s + coefs[-2]
    for c in coefs[-3::-1]:
        value = value * s + c
    return value


def atom_pieces(pos_ref):
    a, b, c = pieces(pos_ref[...])
    own = pos_ref.shape[1]
    left = jnp.concatenate([a, a, b, b, a, c, jnp.zeros((14, own), F32)], axis=0)
    return left.astype(BF16)


def place(step, tile):
    return pl.ds(pl.multiple_of(step * tile, tile), tile)


def phase(wave, left_ref, out_ref):
    tile = wave.shape[1]
    u, v, w = pieces(wave * (0.5 / math.pi))
    right = jnp.concatenate([u, v, u, v, w, u, jnp.zeros((14, tile), F32)], axis=0)
    out_ref[...] = jnp.dot(right.T.astype(BF16), left_ref[...], preferred_element_type=F32)


def evaluate(in_ref, stores, chunk):
    for start in range(0, in_ref.shape[0], chunk):
        t = in_ref[start : start + chunk, :]
        r = t - jnp.round(t)
        x = r * horner(r * r, HALF_SINE)
        square = x * x
        rest = 2.000002 - square
        cosine = (1.0 - square).astype(BF16)
        sine = (x * rest * lax.rsqrt(rest)).astype(BF16)
        for store in stores:
            store(start, cosine, sine)


def into_table(cos_ref, sin_ref, step, tile, chunk):
    def store(start, cosine, sine):
        rows = pl.ds(pl.multiple_of(step * tile + start, chunk), chunk)
        cos_ref[rows, :] = cosine
        sin_ref[rows, :] = sine

    return store


def into_tile(tile_ref, chunk):
    def store(start, cosine, sine):
        tile_ref[0, start : start + chunk, :] = cosine
        tile_ref[1, start : start + chunk, :] = sine

    return store


def histogram(delta):
    place = jnp.where(delta > 0, delta + 63.0, delta + 64.0)
    place = jnp.where(delta == 0, -1.0, place)
    deep = lax.broadcasted_iota(jnp.int32, (LANES, LANES), 0).astype(F32).astype(BF16)
    one = jnp.ones((LANES, LANES), BF16)
    zero = jnp.zeros((LANES, LANES), BF16)
    hist = zero
    for slot in range(64):
        row = jnp.broadcast_to(place[slot : slot + 1, :], (16, LANES)).astype(BF16)
        hist = hist + jnp.where(deep == jnp.concatenate([row] * 8, axis=0), one, zero)
    return hist.astype(F32).T


def early_kernel(
    pos_ref, wave_ref, first_ref, last_ref, w_in_ref, w_out_ref, w_charge_ref, cos_ref, sin_ref,
    coef_ref, hist_ref, w_in_out, w_out_out, w_charge_out, left_ref, even_ref, odd_ref, sems,
    *, tile, chunk, factor,
):
    copies = [
        pltpu.make_async_copy(source, target, sems.at[n])
        for n, (source, target) in enumerate(
            ((w_in_ref, w_in_out), (w_out_ref, w_out_out), (w_charge_ref, w_charge_out))
        )
    ]
    for copy in copies:
        copy.start()
    left_ref[...] = atom_pieces(pos_ref)
    channels = w_in_ref.shape[1]
    for n, ref in enumerate((first_ref, last_ref)):
        hist_ref[n * LANES : (n + 1) * LANES, :] = histogram(ref[:64, channels:].astype(F32))
    head = cos_ref.shape[0] // tile
    group = 8

    def scale(step):
        waves = [wave_ref[:, place(step + n, tile)] for n in range(group)]
        ksq = jnp.zeros((group, tile), F32)
        for c in range(3):
            part = jnp.concatenate([w[c : c + 1] for w in waves], axis=0)
            ksq = ksq + part * part
        coef = factor * jnp.exp(-0.1 * ksq) / ksq
        one = jnp.ones((1, tile), F32)
        for n, w in enumerate(waves):
            coef_ref[:, place(step + n, tile)] = coef[n : n + 1] * jnp.concatenate(
                [one, w, one, w], axis=0
            )

    def turn(step, out_ref):
        phase(wave_ref[:, place(step, tile)], left_ref, out_ref)

    turn(0, even_ref)

    @pl.loop(0, head // 4)
    def _(block):
        base = 4 * block
        scale(4 * base)
        scale(4 * base + group)
        for step in range(0, 4, 2):
            turn(base + step + 1, odd_ref)
            evaluate(even_ref, [into_table(cos_ref, sin_ref, base + step, tile, chunk)], chunk)
            turn(jnp.minimum(base + step + 2, head - 1), even_ref)
            evaluate(odd_ref, [into_table(cos_ref, sin_ref, base + step + 1, tile, chunk)], chunk)

    for copy in copies:
        copy.wait()


def silu(x):
    return x / (1.0 + jnp.exp(-x))


def layer_kernel(
    before_ref, first_ref, last_ref, after_ref, w_in_ref, w_out_ref, w_charge_ref, hist_ref,
    pos_ref, wave_ref, cos_head_ref, sin_head_ref, hidden_ref, sums_ref, cos_ref, sin_ref,
    feat_ref, mid_ref, matrix_ref, left_ref, charge_ref, even_ref, odd_ref, even_tile_ref,
    odd_tile_ref, *, tile, chunk,
):
    parts = (before_ref, first_ref, last_ref, after_ref)
    half = before_ref.shape[0]
    channels = w_in_ref.shape[1]
    own = 2 * half
    for n, ref in enumerate(parts):
        feat_ref[n * half : (n + 1) * half, :] = ref[:, :channels]
    feat_ref[4 * half :, :] = jnp.zeros((HALO, channels), BF16)
    extras = [ref[:, channels:].astype(F32) for ref in parts]
    rows = [e[64:72] + e[72:80] + e[80:88] for e in extras]
    ext_rows = jnp.concatenate(rows + [jnp.zeros((8, LANES), F32)], axis=1)
    ext_cols = jnp.concatenate([r.T for r in rows], axis=0)
    lane = lax.broadcasted_iota(jnp.int32, (HALO, LANES), 1)
    ends = histogram(jnp.where(lane < HALO, extras[3][:64], extras[0][:64]))
    inner = [hist_ref[n * HALO : (n + 1) * HALO, :] for n in range(own // HALO)]
    hist_all = [ends[HALO:]] + inner + [ends[:HALO]]
    blocks = (own + 2 * HALO) // HALO
    zeros = jnp.zeros((HALO, LANES), F32)
    for block in range(blocks):
        base = HALO * (block + 1)
        hist = hist_all[block]
        low = jnp.concatenate([jnp.where(lane < 64, hist, 0.0), zeros], axis=1)
        high = jnp.concatenate([jnp.where(lane < 64, 0.0, hist), zeros], axis=1)
        counted = pltpu.roll(low, 0, 1, stride=1, stride_axis=0) + pltpu.roll(
            high, 1, 1, stride=1, stride_axis=0
        )
        dist = jnp.zeros((HALO, 2 * LANES), F32)
        for c in range(3):
            there = ext_rows[c : c + 1, HALO * block : HALO * block + 2 * LANES]
            diff = there - ext_cols[base : base + HALO, c : c + 1]
            dist = dist + diff * diff
        weight = counted / (1.0 + dist)
        upper = weight.astype(BF16)
        lower = (weight - upper.astype(F32)).astype(BF16)
        matrix_ref[block, :HALO, :] = upper
        matrix_ref[block, HALO:, :] = lower

    def advance(source_ref, layer, block_ids, row0, residual):
        messages = []
        for block in block_ids:
            start = HALO * (block - row0)
            out = jnp.dot(
                matrix_ref[block],
                source_ref[start : start + 2 * LANES, :],
                preferred_element_type=F32,
            )
            messages.append(out[:HALO] + out[HALO:])
        message = jnp.concatenate(messages, axis=0)
        scale = lax.rsqrt(jnp.mean(message * message, axis=-1, keepdims=True) + 1e-05)
        normed = (message * scale).astype(BF16)
        inner = silu(jnp.dot(normed, w_in_ref[layer], preferred_element_type=F32)).astype(BF16)
        update = jnp.dot(inner, w_out_ref[layer], preferred_element_type=F32)
        return (residual.astype(F32) + update).astype(BF16)

    grown = own + 2 * HALO
    mid_ref[:grown, :] = advance(
        feat_ref, 0, range(blocks), 0, feat_ref[HALO : HALO + grown, :]
    )
    mid_ref[grown:, :] = jnp.zeros((HALO, channels), BF16)
    final = advance(mid_ref, 1, range(1, blocks - 1), 1, mid_ref[HALO : HALO + own, :])
    hidden_ref[...] = final
    reader = jnp.concatenate(
        list(pieces(w_charge_ref[...])) + [jnp.zeros((5, channels), F32)], axis=0
    ).astype(BF16)
    read = lax.dot_general(
        reader, final, (((1,), (1,)), ((), ())), preferred_element_type=F32
    )
    charge = read[0:1] + read[1:2] + read[2:3]
    hi, mid, lo = pieces(charge)
    charges = jnp.concatenate([hi, mid, lo, jnp.zeros((5, own), F32)], axis=0).astype(BF16)

    charge_ref[...] = charges
    left_ref[...] = atom_pieces(pos_ref)
    head = cos_head_ref.shape[0] // tile
    late = cos_ref.shape[0] // tile
    share = sums_ref.shape[2]
    per = 2 * tile // share
    dims = (((1,), (1,)), ((), ()))

    def turn(step, out_ref):
        phase(wave_ref[:, place(head + step, tile)], left_ref, out_ref)

    def added(step, cos_tile, sin_tile, odd):
        rows = []
        for table in (cos_tile, sin_tile):
            part = lax.dot_general(charge_ref[...], table, dims, preferred_element_type=F32)
            rows.append(part[0:1] + part[1:2] + part[2:3])
        index = (step - odd) // 2 * per + odd * (per - 1)
        lanes = odd * (2 - per) * tile
        sums_ref[index, :, lanes : lanes + tile] = jnp.concatenate(rows, axis=0)

    turn(0, even_ref)

    @pl.loop(0, head // 2)
    def _(block):
        for n in range(2):
            step = 2 * block + n
            rows = place(step, tile)
            added(step, cos_head_ref[rows, :], sin_head_ref[rows, :], n)
        for pair in range(3):
            step = 6 * block + 2 * pair
            turn(step + 1, odd_ref)
            added(head + step - 1, odd_tile_ref[0], odd_tile_ref[1], 1)
            evaluate(
                even_ref,
                [into_table(cos_ref, sin_ref, step, tile, chunk), into_tile(even_tile_ref, chunk)],
                chunk,
            )
            turn(jnp.minimum(step + 2, late - 1), even_ref)
            added(head + step, even_tile_ref[0], even_tile_ref[1], 0)
            evaluate(
                odd_ref,
                [
                    into_table(cos_ref, sin_ref, step + 1, tile, chunk),
                    into_tile(odd_tile_ref, chunk),
                ],
                chunk,
            )

    added(head + late - 1, odd_tile_ref[0], odd_tile_ref[1], 1)


def sum_kernel(parts_ref, out_ref):
    total = jnp.sum(parts_ref[...].astype(F32), axis=0, keepdims=True)
    out_ref[...] = jnp.broadcast_to(total, parts_ref.shape).astype(BF16)


def response_kernel(
    sums_ref, coef_ref, cos_head_ref, sin_head_ref, cos_ref, sin_ref, pot_ref, field_ref, *, tile
):
    share = sums_ref.shape[2]
    per = tile // share
    row = lax.broadcasted_iota(jnp.int32, (8, share), 0)
    lead = row % 4 == 0
    upper = row < 4
    totals = []
    segments = [(cos_head_ref, sin_head_ref, k) for k in range(0, cos_head_ref.shape[0], tile)]
    segments += [(cos_ref, sin_ref, k) for k in range(0, cos_ref.shape[0], tile)]
    for index, (cos_part, sin_part, start) in enumerate(segments):
        factors = ([], [])
        for q in range(index * per, (index + 1) * per):
            scaled = coef_ref[:, q * share : (q + 1) * share]
            sums = sums_ref[q].astype(F32)
            cosine = sums[0:1]
            sine = sums[1:2]
            for n, (top, other) in enumerate(((cosine, -sine), (sine, cosine))):
                full = scaled * jnp.where(lead, top, other)
                hi = full.astype(BF16).astype(F32)
                factors[n].append(jnp.where(upper, hi, full - hi))
        for n, ref in enumerate((cos_part, sin_part)):
            wide = jnp.concatenate(factors[n], axis=1).astype(BF16)
            totals.append(
                jnp.dot(wide, ref[start : start + tile, :], preferred_element_type=F32)
            )
    total = sum(totals[1:], totals[0])
    result = total[:4] + total[4:]
    pot_ref[...] = result[0:1]
    field_ref[...] = result[1:4]


def shifted(x, step):
    devices = lax.axis_size(AXES)
    pairs = [(i, i + step) for i in range(devices) if 0 <= i + step < devices]
    return lax.ppermute(x, AXES, pairs)


def per_device(features, positions, neighbours, counts, w_in, w_out, w_charge, wave):
    own, channels = features.shape
    total = wave.shape[1]
    devices = lax.axis_size(AXES)
    half = own // 2
    width = channels + LANES
    share = total // devices
    factor = 4.0 / math.sqrt(own * devices * total)
    dma = pltpu.SemaphoreType.DMA
    w_charge = w_charge.reshape(1, channels)
    wave, w_in, w_out, w_charge = (
        pltpu.with_memory_space_constraint(x, pltpu.HBM) for x in (wave, w_in, w_out, w_charge)
    )

    edge = pltpu.VMEM((half, width), BF16)
    first, last, waves, held = pl.pallas_call(
        pack_kernel,
        out_shape=(edge, edge, pltpu.VMEM(wave.shape, F32), pltpu.VMEM(positions.shape, F32)),
        in_specs=[VMEM] * 4 + [HBM],
        out_specs=(VMEM,) * 4,
        scratch_shapes=[dma],
    )(features, positions, neighbours.T, counts.reshape(1, own), wave)
    before = shifted(last, 1)
    after = shifted(first, -1)

    early = total // 4
    tile, chunk = 256, 32
    kept = pltpu.VMEM(w_in.shape, BF16)
    table = pltpu.VMEM((early, own), BF16)
    phases = [pltpu.VMEM((tile, own), F32)] * 2
    grant = pltpu.CompilerParams(vmem_limit_bytes=16 << 20)
    cos_head, sin_head, coef, hist, w_first, w_second, w_read = pl.pallas_call(
        functools.partial(early_kernel, tile=tile, chunk=chunk, factor=factor),
        out_shape=(
            table,
            table,
            pltpu.VMEM((8, total), F32),
            pltpu.VMEM((own, LANES), F32),
            kept,
            kept,
            pltpu.VMEM((1, channels), F32),
        ),
        in_specs=[VMEM] * 4 + [HBM] * 3,
        out_specs=(VMEM,) * 7,
        scratch_shapes=[pltpu.VMEM((32, own), BF16)] + phases + [dma((3,))],
        compiler_params=grant,
        cost_estimate=pl.CostEstimate(
            flops=own * early * 40, bytes_accessed=4 * own * early, transcendentals=0
        ),
    )(held, waves, first, last, w_in, w_out, w_charge)

    table = pltpu.VMEM((total - early, own), BF16)
    hidden, partial, cos_late, sin_late = pl.pallas_call(
        functools.partial(layer_kernel, tile=tile, chunk=chunk),
        out_shape=(
            jax.ShapeDtypeStruct((own, channels), BF16),
            jax.ShapeDtypeStruct((devices, 2, share), F32),
            table,
            table,
        ),
        in_specs=[VMEM] * 12,
        out_specs=(VMEM,) * 4,
        scratch_shapes=[
            pltpu.VMEM((4 * half + HALO, channels), BF16),
            pltpu.VMEM((own + 3 * HALO, channels), BF16),
            pltpu.VMEM((own // HALO + 2, 2 * HALO, 2 * LANES), BF16),
            pltpu.VMEM((32, own), BF16),
            pltpu.VMEM((8, own), BF16),
        ]
        + phases
        + [pltpu.VMEM((2, tile, own), BF16)] * 2,
        compiler_params=grant,
    )(before, first, last, after, w_first, w_second, w_read, hist, held, waves, cos_head, sin_head)

    swapped = lax.all_to_all(partial.astype(BF16), AXES, 0, 0, tiled=True)
    spread = pl.pallas_call(
        sum_kernel,
        out_shape=jax.ShapeDtypeStruct((devices, 2, share), BF16),
        in_specs=[VMEM],
        out_specs=VMEM,
        compiler_params=pltpu.CompilerParams(vmem_limit_bytes=4 << 20),
    )(swapped)
    sums = lax.all_to_all(spread, AXES, 0, 0, tiled=True)

    tables = [
        pltpu.with_memory_space_constraint(x, pltpu.VMEM)
        for x in (cos_head, sin_head, cos_late, sin_late)
    ]
    potential, field = pl.pallas_call(
        functools.partial(response_kernel, tile=4096),
        out_shape=(
            jax.ShapeDtypeStruct((1, own), F32),
            jax.ShapeDtypeStruct((3, own), F32),
        ),
        in_specs=[VMEM] * 6,
        out_specs=(VMEM, VMEM),
        compiler_params=pltpu.CompilerParams(vmem_limit_bytes=4 << 20),
    )(sums, coef, *tables)
    return (hidden, potential.reshape(own), field)


def solution(mesh):
    placed = (
        P(AXES, None),
        P(None, AXES),
        P(AXES, None),
        P(AXES),
        P(),
        P(),
        P(),
        P(),
    )
    return jax.shard_map(
        per_device,
        mesh=mesh,
        in_specs=placed,
        out_specs=(P(AXES, None), P(AXES), P(None, AXES)),
        check_vma=False,
    )
```

```python
import functools
import math

import jax
import jax.numpy as jnp
from jax import lax
from jax.experimental import pallas as pl
from jax.experimental.pallas import tpu as pltpu
from jax.sharding import PartitionSpec as P

LAYERS = 2
HALO = 64
AXES = ("brick", "kvec")
LANES = 128
F32 = jnp.float32
BF16 = jnp.bfloat16

VMEM = pl.BlockSpec(memory_space=pltpu.VMEM)
HBM = pl.BlockSpec(memory_space=pltpu.HBM)


def pieces(x):
    first = x.astype(BF16).astype(F32)
    rest = x - first
    second = rest.astype(BF16).astype(F32)
    return first, second, rest - second


def pack_kernel(
    feat_ref, pos_ref, neigh_ref, counts_ref, wave_ref, first_ref, last_ref, waves_ref,
    held_ref, sem,
):
    slots, own = neigh_ref.shape
    channels = feat_ref.shape[1]
    copy = pltpu.make_async_copy(wave_ref, waves_ref, sem)
    copy.start()
    held_ref[...] = pos_ref[...]
    rows = lax.broadcasted_iota(jnp.int32, (slots, own), 1)
    slot = lax.broadcasted_iota(jnp.int32, (slots, own), 0)
    delta = (neigh_ref[...] - HALO - rows).astype(F32)
    delta = jnp.where(slot < counts_ref[...], delta, 0.0)
    zero5 = jnp.zeros((5, own), F32)
    coords = [jnp.concatenate([p, zero5], axis=0) for p in pieces(pos_ref[...])]
    rest = jnp.zeros((LANES - slots - 24, own), F32)
    extra = jnp.concatenate([delta] + coords + [rest], axis=0).astype(BF16)
    half = own // 2
    for ref, start in ((first_ref, 0), (last_ref, half)):
        ref[:, :channels] = feat_ref[start : start + half, :]
        ref[:, channels:] = extra[:, start : start + half]
    copy.wait()


HALF_SINE = (4.438831262995637, -7.228964613368321, 3.149392241482131)


def horner(s, coefs):
    value = coefs[-1] * s + coefs[-2]
    for c in coefs[-3::-1]:
        value = value * s + c
    return value


def atom_pieces(pos_ref):
    a, b, c = pieces(pos_ref[...])
    own = pos_ref.shape[1]
    left = jnp.concatenate([a, a, b, b, a, c, jnp.zeros((14, own), F32)], axis=0)
    return left.astype(BF16)


def place(step, tile):
    return pl.ds(pl.multiple_of(step * tile, tile), tile)


def phase(wave, left_ref, out_ref):
    tile = wave.shape[1]
    u, v, w = pieces(wave * (0.5 / math.pi))
    right = jnp.concatenate([u, v, u, v, w, u, jnp.zeros((14, tile), F32)], axis=0)
    out_ref[...] = jnp.dot(right.T.astype(BF16), left_ref[...], preferred_element_type=F32)


def evaluate(in_ref, stores, chunk):
    for start in range(0, in_ref.shape[0], chunk):
        t = in_ref[start : start + chunk, :]
        r = t - jnp.round(t)
        x = r * horner(r * r, HALF_SINE)
        square = x * x
        rest = 2.000002 - square
        cosine = (1.0 - square).astype(BF16)
        sine = (x * rest * lax.rsqrt(rest)).astype(BF16)
        for store in stores:
            store(start, cosine, sine)


def into_table(cos_ref, sin_ref, step, tile, chunk):
    def store(start, cosine, sine):
        rows = pl.ds(pl.multiple_of(step * tile + start, chunk), chunk)
        cos_ref[rows, :] = cosine
        sin_ref[rows, :] = sine

    return store


def into_tile(tile_ref, chunk):
    def store(start, cosine, sine):
        tile_ref[0, start : start + chunk, :] = cosine
        tile_ref[1, start : start + chunk, :] = sine

    return store


def histogram(delta):
    place = jnp.where(delta > 0, delta + 63.0, delta + 64.0)
    place = jnp.where(delta == 0, -1.0, place)
    deep = lax.broadcasted_iota(jnp.int32, (LANES, LANES), 0).astype(F32).astype(BF16)
    one = jnp.ones((LANES, LANES), BF16)
    zero = jnp.zeros((LANES, LANES), BF16)
    hist = zero
    for slot in range(64):
        row = jnp.broadcast_to(place[slot : slot + 1, :], (16, LANES)).astype(BF16)
        hist = hist + jnp.where(deep == jnp.concatenate([row] * 8, axis=0), one, zero)
    return hist.astype(F32).T


def early_kernel(
    pos_ref, wave_ref, first_ref, last_ref, w_in_ref, w_out_ref, w_charge_ref, cos_ref, sin_ref,
    coef_ref, hist_ref, w_in_out, w_out_out, w_charge_out, left_ref, even_ref, odd_ref, sems,
    *, tile, chunk, factor,
):
    copies = [
        pltpu.make_async_copy(source, target, sems.at[n])
        for n, (source, target) in enumerate(
            ((w_in_ref, w_in_out), (w_out_ref, w_out_out), (w_charge_ref, w_charge_out))
        )
    ]
    for copy in copies:
        copy.start()
    left_ref[...] = atom_pieces(pos_ref)
    channels = w_in_ref.shape[1]
    for n, ref in enumerate((first_ref, last_ref)):
        hist_ref[n * LANES : (n + 1) * LANES, :] = histogram(ref[:64, channels:].astype(F32))
    head = cos_ref.shape[0] // tile
    group = 8

    def scale(step):
        waves = [wave_ref[:, place(step + n, tile)] for n in range(group)]
        ksq = jnp.zeros((group, tile), F32)
        for c in range(3):
            part = jnp.concatenate([w[c : c + 1] for w in waves], axis=0)
            ksq = ksq + part * part
        coef = factor * jnp.exp(-0.1 * ksq) / ksq
        one = jnp.ones((1, tile), F32)
        for n, w in enumerate(waves):
            coef_ref[:, place(step + n, tile)] = coef[n : n + 1] * jnp.concatenate(
                [one, w, one, w], axis=0
            )

    def turn(step, out_ref):
        phase(wave_ref[:, place(step, tile)], left_ref, out_ref)

    turn(0, even_ref)

    @pl.loop(0, head // 4)
    def _(block):
        base = 4 * block
        scale(2 * base)
        for step in range(0, 4, 2):
            turn(base + step + 1, odd_ref)
            evaluate(even_ref, [into_table(cos_ref, sin_ref, base + step, tile, chunk)], chunk)
            turn(jnp.minimum(base + step + 2, head - 1), even_ref)
            evaluate(odd_ref, [into_table(cos_ref, sin_ref, base + step + 1, tile, chunk)], chunk)

    for copy in copies:
        copy.wait()


def silu(x):
    return x / (1.0 + jnp.exp(-x))


def layer_kernel(
    before_ref, first_ref, last_ref, after_ref, w_in_ref, w_out_ref, w_charge_ref, hist_ref,
    pos_ref, wave_ref, cos_head_ref, sin_head_ref, hidden_ref, sums_ref, cos_ref, sin_ref,
    feat_ref, mid_ref, matrix_ref, left_ref, charge_ref, even_ref, odd_ref, even_tile_ref,
    odd_tile_ref, *, tile, chunk,
):
    parts = (before_ref, first_ref, last_ref, after_ref)
    half = before_ref.shape[0]
    channels = w_in_ref.shape[1]
    own = 2 * half
    for n, ref in enumerate(parts):
        feat_ref[n * half : (n + 1) * half, :] = ref[:, :channels]
    feat_ref[4 * half :, :] = jnp.zeros((HALO, channels), BF16)
    extras = [ref[:, channels:].astype(F32) for ref in parts]
    rows = [e[64:72] + e[72:80] + e[80:88] for e in extras]
    ext_rows = jnp.concatenate(rows + [jnp.zeros((8, LANES), F32)], axis=1)
    ext_cols = jnp.concatenate([r.T for r in rows], axis=0)
    lane = lax.broadcasted_iota(jnp.int32, (HALO, LANES), 1)
    ends = histogram(jnp.where(lane < HALO, extras[3][:64], extras[0][:64]))
    inner = [hist_ref[n * HALO : (n + 1) * HALO, :] for n in range(own // HALO)]
    hist_all = [ends[HALO:]] + inner + [ends[:HALO]]
    blocks = (own + 2 * HALO) // HALO
    zeros = jnp.zeros((HALO, LANES), F32)
    for block in range(blocks):
        base = HALO * (block + 1)
        hist = hist_all[block]
        low = jnp.concatenate([jnp.where(lane < 64, hist, 0.0), zeros], axis=1)
        high = jnp.concatenate([jnp.where(lane < 64, 0.0, hist), zeros], axis=1)
        counted = pltpu.roll(low, 0, 1, stride=1, stride_axis=0) + pltpu.roll(
            high, 1, 1, stride=1, stride_axis=0
        )
        dist = jnp.zeros((HALO, 2 * LANES), F32)
        for c in range(3):
            there = ext_rows[c : c + 1, HALO * block : HALO * block + 2 * LANES]
            diff = there - ext_cols[base : base + HALO, c : c + 1]
            dist = dist + diff * diff
        weight = counted / (1.0 + dist)
        upper = weight.astype(BF16)
        lower = (weight - upper.astype(F32)).astype(BF16)
        matrix_ref[block, :HALO, :] = upper
        matrix_ref[block, HALO:, :] = lower

    def advance(source_ref, layer, block_ids, row0, residual):
        messages = []
        for block in block_ids:
            start = HALO * (block - row0)
            out = jnp.dot(
                matrix_ref[block],
                source_ref[start : start + 2 * LANES, :],
                preferred_element_type=F32,
            )
            messages.append(out[:HALO] + out[HALO:])
        message = jnp.concatenate(messages, axis=0)
        scale = lax.rsqrt(jnp.mean(message * message, axis=-1, keepdims=True) + 1e-05)
        normed = (message * scale).astype(BF16)
        inner = silu(jnp.dot(normed, w_in_ref[layer], preferred_element_type=F32)).astype(BF16)
        update = jnp.dot(inner, w_out_ref[layer], preferred_element_type=F32)
        return (residual.astype(F32) + update).astype(BF16)

    grown = own + 2 * HALO
    mid_ref[:grown, :] = advance(
        feat_ref, 0, range(blocks), 0, feat_ref[HALO : HALO + grown, :]
    )
    mid_ref[grown:, :] = jnp.zeros((HALO, channels), BF16)
    final = advance(mid_ref, 1, range(1, blocks - 1), 1, mid_ref[HALO : HALO + own, :])
    hidden_ref[...] = final
    reader = jnp.concatenate(
        list(pieces(w_charge_ref[...])) + [jnp.zeros((5, channels), F32)], axis=0
    ).astype(BF16)
    read = lax.dot_general(
        reader, final, (((1,), (1,)), ((), ())), preferred_element_type=F32
    )
    charge = read[0:1] + read[1:2] + read[2:3]
    hi, mid, lo = pieces(charge)
    charges = jnp.concatenate([hi, mid, lo, jnp.zeros((5, own), F32)], axis=0).astype(BF16)

    charge_ref[...] = charges
    left_ref[...] = atom_pieces(pos_ref)
    head = cos_head_ref.shape[0] // tile
    late = cos_ref.shape[0] // tile
    share = sums_ref.shape[2]
    per = 2 * tile // share
    dims = (((1,), (1,)), ((), ()))

    def turn(step, out_ref):
        phase(wave_ref[:, place(head + step, tile)], left_ref, out_ref)

    def added(step, cos_tile, sin_tile, odd):
        rows = []
        for table in (cos_tile, sin_tile):
            part = lax.dot_general(charge_ref[...], table, dims, preferred_element_type=F32)
            rows.append(part[0:1] + part[1:2] + part[2:3])
        index = (step - odd) // 2 * per + odd * (per - 1)
        lanes = odd * (2 - per) * tile
        sums_ref[index, :, lanes : lanes + tile] = jnp.concatenate(rows, axis=0)

    turn(0, even_ref)

    @pl.loop(0, late // 4)
    def _(block):
        for pair in range(2):
            step = 4 * block + 2 * pair
            for n in range(2):
                rows = place(step + n, tile)
                added(step + n, cos_head_ref[rows, :], sin_head_ref[rows, :], n)
            turn(step + 1, odd_ref)
            added(head + step - 1, odd_tile_ref[0], odd_tile_ref[1], 1)
            evaluate(
                even_ref,
                [into_table(cos_ref, sin_ref, step, tile, chunk), into_tile(even_tile_ref, chunk)],
                chunk,
            )
            turn(jnp.minimum(step + 2, late - 1), even_ref)
            added(head + step, even_tile_ref[0], even_tile_ref[1], 0)
            evaluate(
                odd_ref,
                [
                    into_table(cos_ref, sin_ref, step + 1, tile, chunk),
                    into_tile(odd_tile_ref, chunk),
                ],
                chunk,
            )

    added(head + late - 1, odd_tile_ref[0], odd_tile_ref[1], 1)


def sum_kernel(parts_ref, out_ref):
    total = jnp.sum(parts_ref[...].astype(F32), axis=0, keepdims=True)
    out_ref[...] = jnp.broadcast_to(total, parts_ref.shape).astype(BF16)


def response_kernel(
    sums_ref, coef_ref, cos_head_ref, sin_head_ref, cos_ref, sin_ref, pot_ref, field_ref, *, tile
):
    share = sums_ref.shape[2]
    per = tile // share
    row = lax.broadcasted_iota(jnp.int32, (8, share), 0)
    lead = row % 4 == 0
    upper = row < 4
    totals = []
    segments = [(cos_head_ref, sin_head_ref, k) for k in range(0, cos_head_ref.shape[0], tile)]
    segments += [(cos_ref, sin_ref, k) for k in range(0, cos_ref.shape[0], tile)]
    for index, (cos_part, sin_part, start) in enumerate(segments):
        factors = ([], [])
        for q in range(index * per, (index + 1) * per):
            scaled = coef_ref[:, q * share : (q + 1) * share]
            sums = sums_ref[q].astype(F32)
            cosine = sums[0:1]
            sine = sums[1:2]
            for n, (top, other) in enumerate(((cosine, -sine), (sine, cosine))):
                full = scaled * jnp.where(lead, top, other)
                hi = full.astype(BF16).astype(F32)
                factors[n].append(jnp.where(upper, hi, full - hi))
        for n, ref in enumerate((cos_part, sin_part)):
            wide = jnp.concatenate(factors[n], axis=1).astype(BF16)
            totals.append(
                jnp.dot(wide, ref[start : start + tile, :], preferred_element_type=F32)
            )
    total = sum(totals[1:], totals[0])
    result = total[:4] + total[4:]
    pot_ref[...] = result[0:1]
    field_ref[...] = result[1:4]


def shifted(x, step):
    devices = lax.axis_size(AXES)
    pairs = [(i, i + step) for i in range(devices) if 0 <= i + step < devices]
    return lax.ppermute(x, AXES, pairs)


def per_device(features, positions, neighbours, counts, w_in, w_out, w_charge, wave):
    own, channels = features.shape
    total = wave.shape[1]
    devices = lax.axis_size(AXES)
    half = own // 2
    width = channels + LANES
    share = total // devices
    factor = 4.0 / math.sqrt(own * devices * total)
    dma = pltpu.SemaphoreType.DMA
    w_charge = w_charge.reshape(1, channels)
    wave, w_in, w_out, w_charge = (
        pltpu.with_memory_space_constraint(x, pltpu.HBM) for x in (wave, w_in, w_out, w_charge)
    )

    edge = pltpu.VMEM((half, width), BF16)
    first, last, waves, held = pl.pallas_call(
        pack_kernel,
        out_shape=(edge, edge, pltpu.VMEM(wave.shape, F32), pltpu.VMEM(positions.shape, F32)),
        in_specs=[VMEM] * 4 + [HBM],
        out_specs=(VMEM,) * 4,
        scratch_shapes=[dma],
    )(features, positions, neighbours.T, counts.reshape(1, own), wave)
    before = shifted(last, 1)
    after = shifted(first, -1)

    early = total // 2
    tile, chunk = 256, 32
    kept = pltpu.VMEM(w_in.shape, BF16)
    table = pltpu.VMEM((early, own), BF16)
    phases = [pltpu.VMEM((tile, own), F32)] * 2
    grant = pltpu.CompilerParams(vmem_limit_bytes=16 << 20)
    cos_head, sin_head, coef, hist, w_first, w_second, w_read = pl.pallas_call(
        functools.partial(early_kernel, tile=tile, chunk=chunk, factor=factor),
        out_shape=(
            table,
            table,
            pltpu.VMEM((8, total), F32),
            pltpu.VMEM((own, LANES), F32),
            kept,
            kept,
            pltpu.VMEM((1, channels), F32),
        ),
        in_specs=[VMEM] * 4 + [HBM] * 3,
        out_specs=(VMEM,) * 7,
        scratch_shapes=[pltpu.VMEM((32, own), BF16)] + phases + [dma((3,))],
        compiler_params=grant,
        cost_estimate=pl.CostEstimate(
            flops=own * early * 40, bytes_accessed=4 * own * early, transcendentals=0
        ),
    )(held, waves, first, last, w_in, w_out, w_charge)

    table = pltpu.VMEM((total - early, own), BF16)
    hidden, partial, cos_late, sin_late = pl.pallas_call(
        functools.partial(layer_kernel, tile=tile, chunk=chunk),
        out_shape=(
            jax.ShapeDtypeStruct((own, channels), BF16),
            jax.ShapeDtypeStruct((devices, 2, share), F32),
            table,
            table,
        ),
        in_specs=[VMEM] * 12,
        out_specs=(VMEM,) * 4,
        scratch_shapes=[
            pltpu.VMEM((4 * half + HALO, channels), BF16),
            pltpu.VMEM((own + 3 * HALO, channels), BF16),
            pltpu.VMEM((own // HALO + 2, 2 * HALO, 2 * LANES), BF16),
            pltpu.VMEM((32, own), BF16),
            pltpu.VMEM((8, own), BF16),
        ]
        + phases
        + [pltpu.VMEM((2, tile, own), BF16)] * 2,
        compiler_params=grant,
    )(before, first, last, after, w_first, w_second, w_read, hist, held, waves, cos_head, sin_head)

    swapped = lax.all_to_all(partial.astype(BF16), AXES, 0, 0, tiled=True)
    spread = pl.pallas_call(
        sum_kernel,
        out_shape=jax.ShapeDtypeStruct((devices, 2, share), BF16),
        in_specs=[VMEM],
        out_specs=VMEM,
        compiler_params=pltpu.CompilerParams(vmem_limit_bytes=4 << 20),
    )(swapped)
    sums = lax.all_to_all(spread, AXES, 0, 0, tiled=True)

    tables = [
        pltpu.with_memory_space_constraint(x, pltpu.VMEM)
        for x in (cos_head, sin_head, cos_late, sin_late)
    ]
    potential, field = pl.pallas_call(
        functools.partial(response_kernel, tile=4096),
        out_shape=(
            jax.ShapeDtypeStruct((1, own), F32),
            jax.ShapeDtypeStruct((3, own), F32),
        ),
        in_specs=[VMEM] * 6,
        out_specs=(VMEM, VMEM),
        compiler_params=pltpu.CompilerParams(vmem_limit_bytes=4 << 20),
    )(sums, coef, *tables)
    return (hidden, potential.reshape(own), field)


def solution(mesh):
    placed = (
        P(AXES, None),
        P(None, AXES),
        P(AXES, None),
        P(AXES),
        P(),
        P(),
        P(),
        P(),
    )
    return jax.shard_map(
        per_device,
        mesh=mesh,
        in_specs=placed,
        out_specs=(P(AXES, None), P(AXES), P(None, AXES)),
        check_vma=False,
    )
```

```python
import functools
import math

import jax
import jax.numpy as jnp
from jax import lax
from jax.experimental import pallas as pl
from jax.experimental.pallas import tpu as pltpu
from jax.sharding import PartitionSpec as P

LAYERS = 2
HALO = 64
AXES = ("brick", "kvec")
LANES = 128
F32 = jnp.float32
BF16 = jnp.bfloat16

VMEM = pl.BlockSpec(memory_space=pltpu.VMEM)
HBM = pl.BlockSpec(memory_space=pltpu.HBM)


def pieces(x):
    first = x.astype(BF16).astype(F32)
    rest = x - first
    second = rest.astype(BF16).astype(F32)
    return first, second, rest - second


def pack_kernel(
    feat_ref, pos_ref, neigh_ref, counts_ref, wave_ref, first_ref, last_ref, waves_ref,
    held_ref, sem,
):
    slots, own = neigh_ref.shape
    channels = feat_ref.shape[1]
    copy = pltpu.make_async_copy(wave_ref, waves_ref, sem)
    copy.start()
    held_ref[...] = pos_ref[...]
    rows = lax.broadcasted_iota(jnp.int32, (slots, own), 1)
    slot = lax.broadcasted_iota(jnp.int32, (slots, own), 0)
    delta = (neigh_ref[...] - HALO - rows).astype(F32)
    delta = jnp.where(slot < counts_ref[...], delta, 0.0)
    zero5 = jnp.zeros((5, own), F32)
    coords = [jnp.concatenate([p, zero5], axis=0) for p in pieces(pos_ref[...])]
    rest = jnp.zeros((LANES - slots - 24, own), F32)
    extra = jnp.concatenate([delta] + coords + [rest], axis=0).astype(BF16)
    half = own // 2
    for ref, start in ((first_ref, 0), (last_ref, half)):
        ref[:, :channels] = feat_ref[start : start + half, :]
        ref[:, channels:] = extra[:, start : start + half]
    copy.wait()


HALF_SINE = (4.438831262995637, -7.228964613368321, 3.149392241482131)


def horner(s, coefs):
    value = coefs[-1] * s + coefs[-2]
    for c in coefs[-3::-1]:
        value = value * s + c
    return value


def atom_pieces(pos_ref):
    a, b, c = pieces(pos_ref[...])
    own = pos_ref.shape[1]
    left = jnp.concatenate([a, a, b, b, a, c, jnp.zeros((14, own), F32)], axis=0)
    return left.astype(BF16)


def place(step, tile):
    return pl.ds(pl.multiple_of(step * tile, tile), tile)


def phase(wave, left_ref, out_ref):
    tile = wave.shape[1]
    u, v, w = pieces(wave * (0.5 / math.pi))
    right = jnp.concatenate([u, v, u, v, w, u, jnp.zeros((14, tile), F32)], axis=0)
    out_ref[...] = jnp.dot(right.T.astype(BF16), left_ref[...], preferred_element_type=F32)


def evaluate(in_ref, stores, chunk):
    for start in range(0, in_ref.shape[0], chunk):
        t = in_ref[start : start + chunk, :]
        r = t - jnp.round(t)
        x = r * horner(r * r, HALF_SINE)
        square = x * x
        rest = 2.000002 - square
        cosine = (1.0 - square).astype(BF16)
        sine = (x * rest * lax.rsqrt(rest)).astype(BF16)
        for store in stores:
            store(start, cosine, sine)


def into_table(cos_ref, sin_ref, step, tile, chunk):
    def store(start, cosine, sine):
        rows = pl.ds(pl.multiple_of(step * tile + start, chunk), chunk)
        cos_ref[rows, :] = cosine
        sin_ref[rows, :] = sine

    return store


def into_tile(tile_ref, chunk):
    tile = tile_ref.shape[0] // 2

    def store(start, cosine, sine):
        tile_ref[start : start + chunk, :] = cosine
        tile_ref[tile + start : tile + start + chunk, :] = sine

    return store


def histogram(delta):
    place = jnp.where(delta > 0, delta + 63.0, delta + 64.0)
    place = jnp.where(delta == 0, -1.0, place)
    deep = lax.broadcasted_iota(jnp.int32, (LANES, LANES), 0).astype(F32).astype(BF16)
    one = jnp.ones((LANES, LANES), BF16)
    zero = jnp.zeros((LANES, LANES), BF16)
    hist = zero
    for slot in range(64):
        row = jnp.broadcast_to(place[slot : slot + 1, :], (16, LANES)).astype(BF16)
        hist = hist + jnp.where(deep == jnp.concatenate([row] * 8, axis=0), one, zero)
    return hist.astype(F32).T


def early_kernel(
    pos_ref, wave_ref, first_ref, last_ref, w_in_ref, w_out_ref, w_charge_ref, cos_ref, sin_ref,
    coef_ref, hist_ref, w_in_out, w_out_out, w_charge_out, left_ref, even_ref, odd_ref, sems,
    *, tile, chunk, factor,
):
    copies = [
        pltpu.make_async_copy(source, target, sems.at[n])
        for n, (source, target) in enumerate(
            ((w_in_ref, w_in_out), (w_out_ref, w_out_out), (w_charge_ref, w_charge_out))
        )
    ]
    for copy in copies:
        copy.start()
    left_ref[...] = atom_pieces(pos_ref)
    channels = w_in_ref.shape[1]
    for n, ref in enumerate((first_ref, last_ref)):
        hist_ref[n * LANES : (n + 1) * LANES, :] = histogram(ref[:64, channels:].astype(F32))
    head = cos_ref.shape[0] // tile
    group = 8
    width = 4 * tile // group

    def scale(step):
        waves = [wave_ref[:, place(4 * step + n, width)] for n in range(group)]
        ksq = jnp.zeros((group, width), F32)
        for c in range(3):
            part = jnp.concatenate([w[c : c + 1] for w in waves], axis=0)
            ksq = ksq + part * part
        coef = factor * jnp.exp(-0.1 * ksq) / ksq
        one = jnp.ones((1, width), F32)
        for n, w in enumerate(waves):
            coef_ref[:, place(4 * step + n, width)] = coef[n : n + 1] * jnp.concatenate(
                [one, w, one, w], axis=0
            )

    def turn(step, out_ref):
        phase(wave_ref[:, place(step, tile)], left_ref, out_ref)

    turn(0, even_ref)

    @pl.loop(0, head // 2)
    def _(block):
        step = 2 * block
        scale(step)
        turn(step + 1, odd_ref)
        evaluate(even_ref, [into_table(cos_ref, sin_ref, step, tile, chunk)], chunk)
        turn(jnp.minimum(step + 2, head - 1), even_ref)
        evaluate(odd_ref, [into_table(cos_ref, sin_ref, step + 1, tile, chunk)], chunk)

    for copy in copies:
        copy.wait()


def silu(x):
    return x / (1.0 + jnp.exp(-x))


def layer_kernel(
    before_ref, first_ref, last_ref, after_ref, w_in_ref, w_out_ref, w_charge_ref, hist_ref,
    pos_ref, wave_ref, cos_head_ref, sin_head_ref, hidden_ref, sums_ref, cos_ref, sin_ref,
    feat_ref, mid_ref, matrix_ref, left_ref, charge_ref, even_ref, odd_ref, even_tile_ref,
    odd_tile_ref, *, tile, chunk,
):
    parts = (before_ref, first_ref, last_ref, after_ref)
    half = before_ref.shape[0]
    channels = w_in_ref.shape[1]
    own = 2 * half
    for n, ref in enumerate(parts):
        feat_ref[n * half : (n + 1) * half, :] = ref[:, :channels]
    feat_ref[4 * half :, :] = jnp.zeros((HALO, channels), BF16)
    extras = [ref[:, channels:].astype(F32) for ref in parts]
    rows = [e[64:72] + e[72:80] + e[80:88] for e in extras]
    ext_rows = jnp.concatenate(rows + [jnp.zeros((8, LANES), F32)], axis=1)
    ext_cols = jnp.concatenate([r.T for r in rows], axis=0)
    lane = lax.broadcasted_iota(jnp.int32, (HALO, LANES), 1)
    ends = histogram(jnp.where(lane < HALO, extras[3][:64], extras[0][:64]))
    inner = [hist_ref[n * HALO : (n + 1) * HALO, :] for n in range(own // HALO)]
    hist_all = [ends[HALO:]] + inner + [ends[:HALO]]
    blocks = (own + 2 * HALO) // HALO
    zeros = jnp.zeros((HALO, LANES), F32)
    for block in range(blocks):
        base = HALO * (block + 1)
        hist = hist_all[block]
        low = jnp.concatenate([jnp.where(lane < 64, hist, 0.0), zeros], axis=1)
        high = jnp.concatenate([jnp.where(lane < 64, 0.0, hist), zeros], axis=1)
        counted = pltpu.roll(low, 0, 1, stride=1, stride_axis=0) + pltpu.roll(
            high, 1, 1, stride=1, stride_axis=0
        )
        dist = jnp.zeros((HALO, 2 * LANES), F32)
        for c in range(3):
            there = ext_rows[c : c + 1, HALO * block : HALO * block + 2 * LANES]
            diff = there - ext_cols[base : base + HALO, c : c + 1]
            dist = dist + diff * diff
        weight = counted / (1.0 + dist)
        upper = weight.astype(BF16)
        lower = (weight - upper.astype(F32)).astype(BF16)
        matrix_ref[block, :HALO, :] = upper
        matrix_ref[block, HALO:, :] = lower

    def advance(source_ref, layer, block_ids, row0, residual):
        messages = []
        for block in block_ids:
            start = HALO * (block - row0)
            out = jnp.dot(
                matrix_ref[block],
                source_ref[start : start + 2 * LANES, :],
                preferred_element_type=F32,
            )
            messages.append(out[:HALO] + out[HALO:])
        message = jnp.concatenate(messages, axis=0)
        scale = lax.rsqrt(jnp.mean(message * message, axis=-1, keepdims=True) + 1e-05)
        normed = (message * scale).astype(BF16)
        inner = silu(jnp.dot(normed, w_in_ref[layer], preferred_element_type=F32)).astype(BF16)
        update = jnp.dot(inner, w_out_ref[layer], preferred_element_type=F32)
        return (residual.astype(F32) + update).astype(BF16)

    grown = own + 2 * HALO
    mid_ref[:grown, :] = advance(
        feat_ref, 0, range(blocks), 0, feat_ref[HALO : HALO + grown, :]
    )
    mid_ref[grown:, :] = jnp.zeros((HALO, channels), BF16)
    final = advance(mid_ref, 1, range(1, blocks - 1), 1, mid_ref[HALO : HALO + own, :])
    hidden_ref[...] = final
    reader = jnp.concatenate(
        list(pieces(w_charge_ref[...])) + [jnp.zeros((5, channels), F32)], axis=0
    ).astype(BF16)
    read = lax.dot_general(
        reader, final, (((1,), (1,)), ((), ())), preferred_element_type=F32
    )
    charge = read[0:1] + read[1:2] + read[2:3]
    hi, mid, lo = pieces(charge)
    charges = jnp.concatenate([hi, mid, lo, jnp.zeros((5, own), F32)], axis=0).astype(BF16)

    charge_ref[...] = charges
    left_ref[...] = atom_pieces(pos_ref)
    head = cos_head_ref.shape[0] // tile
    late = cos_ref.shape[0] // tile
    share = sums_ref.shape[2]
    per = tile // share
    dims = (((1,), (1,)), ((), ()))

    def turn(step, out_ref):
        phase(wave_ref[:, place(head + step, tile)], left_ref, out_ref)

    def product(table):
        part = lax.dot_general(charge_ref[...], table, dims, preferred_element_type=F32)
        return part[0:1] + part[1:2] + part[2:3]

    def keep(step, cosine, sine):
        both = jnp.concatenate([cosine, sine], axis=0)
        for q in range(per):
            sums_ref[step * per + q] = both[:, q * share : (q + 1) * share]

    def added(step, tile_ref):
        both = product(tile_ref[...])
        keep(step, both[:, :tile], both[:, tile:])

    turn(0, even_ref)

    @pl.loop(0, late // 2)
    def _(block):
        step = 2 * block
        for n, (t_ref, next_ref, tile_ref, last_tile_ref) in enumerate(
            (
                (even_ref, odd_ref, even_tile_ref, odd_tile_ref),
                (odd_ref, even_ref, odd_tile_ref, even_tile_ref),
            )
        ):
            rows = place(step + n, tile)
            turn(jnp.minimum(step + n + 1, late - 1), next_ref)
            added(head + step + n - 1, last_tile_ref)
            keep(step + n, product(cos_head_ref[rows, :]), product(sin_head_ref[rows, :]))
            evaluate(
                t_ref,
                [into_table(cos_ref, sin_ref, step + n, tile, chunk), into_tile(tile_ref, chunk)],
                chunk,
            )

    added(head + late - 1, odd_tile_ref)


def sum_kernel(parts_ref, out_ref):
    total = jnp.sum(parts_ref[...].astype(F32), axis=0, keepdims=True)
    out_ref[...] = jnp.broadcast_to(total, parts_ref.shape).astype(BF16)


def response_kernel(
    sums_ref, coef_ref, cos_head_ref, sin_head_ref, cos_ref, sin_ref, pot_ref, field_ref, *, tile
):
    share = sums_ref.shape[2]
    per = tile // share
    row = lax.broadcasted_iota(jnp.int32, (8, share), 0)
    lead = row % 4 == 0
    upper = row < 4
    totals = []
    segments = [(cos_head_ref, sin_head_ref, k) for k in range(0, cos_head_ref.shape[0], tile)]
    segments += [(cos_ref, sin_ref, k) for k in range(0, cos_ref.shape[0], tile)]
    for index, (cos_part, sin_part, start) in enumerate(segments):
        factors = ([], [])
        for q in range(index * per, (index + 1) * per):
            scaled = coef_ref[:, q * share : (q + 1) * share]
            sums = sums_ref[q].astype(F32)
            cosine = sums[0:1]
            sine = sums[1:2]
            for n, (top, other) in enumerate(((cosine, -sine), (sine, cosine))):
                full = scaled * jnp.where(lead, top, other)
                hi = full.astype(BF16).astype(F32)
                factors[n].append(jnp.where(upper, hi, full - hi))
        for n, ref in enumerate((cos_part, sin_part)):
            wide = jnp.concatenate(factors[n], axis=1).astype(BF16)
            totals.append(
                jnp.dot(wide, ref[start : start + tile, :], preferred_element_type=F32)
            )
    total = sum(totals[1:], totals[0])
    result = total[:4] + total[4:]
    pot_ref[...] = result[0:1]
    field_ref[...] = result[1:4]


def shifted(x, step):
    devices = lax.axis_size(AXES)
    pairs = [(i, i + step) for i in range(devices) if 0 <= i + step < devices]
    return lax.ppermute(x, AXES, pairs)


def per_device(features, positions, neighbours, counts, w_in, w_out, w_charge, wave):
    own, channels = features.shape
    total = wave.shape[1]
    devices = lax.axis_size(AXES)
    half = own // 2
    width = channels + LANES
    share = total // devices
    factor = 4.0 / math.sqrt(own * devices * total)
    dma = pltpu.SemaphoreType.DMA
    w_charge = w_charge.reshape(1, channels)
    wave, w_in, w_out, w_charge = (
        pltpu.with_memory_space_constraint(x, pltpu.HBM) for x in (wave, w_in, w_out, w_charge)
    )

    edge = pltpu.VMEM((half, width), BF16)
    first, last, waves, held = pl.pallas_call(
        pack_kernel,
        out_shape=(edge, edge, pltpu.VMEM(wave.shape, F32), pltpu.VMEM(positions.shape, F32)),
        in_specs=[VMEM] * 4 + [HBM],
        out_specs=(VMEM,) * 4,
        scratch_shapes=[dma],
    )(features, positions, neighbours.T, counts.reshape(1, own), wave)
    before = shifted(last, 1)
    after = shifted(first, -1)

    early = total // 2
    tile, chunk = 512, 32
    kept = pltpu.VMEM(w_in.shape, BF16)
    table = pltpu.VMEM((early, own), BF16)
    phases = [pltpu.VMEM((tile, own), F32)] * 2
    grant = pltpu.CompilerParams(vmem_limit_bytes=16 << 20)
    cos_head, sin_head, coef, hist, w_first, w_second, w_read = pl.pallas_call(
        functools.partial(early_kernel, tile=tile, chunk=chunk, factor=factor),
        out_shape=(
            table,
            table,
            pltpu.VMEM((8, total), F32),
            pltpu.VMEM((own, LANES), F32),
            kept,
            kept,
            pltpu.VMEM((1, channels), F32),
        ),
        in_specs=[VMEM] * 4 + [HBM] * 3,
        out_specs=(VMEM,) * 7,
        scratch_shapes=[pltpu.VMEM((32, own), BF16)] + phases + [dma((3,))],
        compiler_params=grant,
        cost_estimate=pl.CostEstimate(
            flops=own * early * 40, bytes_accessed=4 * own * early, transcendentals=0
        ),
    )(held, waves, first, last, w_in, w_out, w_charge)

    table = pltpu.VMEM((total - early, own), BF16)
    hidden, partial, cos_late, sin_late = pl.pallas_call(
        functools.partial(layer_kernel, tile=tile, chunk=chunk),
        out_shape=(
            jax.ShapeDtypeStruct((own, channels), BF16),
            jax.ShapeDtypeStruct((devices, 2, share), F32),
            table,
            table,
        ),
        in_specs=[VMEM] * 12,
        out_specs=(VMEM,) * 4,
        scratch_shapes=[
            pltpu.VMEM((4 * half + HALO, channels), BF16),
            pltpu.VMEM((own + 3 * HALO, channels), BF16),
            pltpu.VMEM((own // HALO + 2, 2 * HALO, 2 * LANES), BF16),
            pltpu.VMEM((32, own), BF16),
            pltpu.VMEM((8, own), BF16),
        ]
        + phases
        + [pltpu.VMEM((2 * tile, own), BF16)] * 2,
        compiler_params=grant,
    )(before, first, last, after, w_first, w_second, w_read, hist, held, waves, cos_head, sin_head)

    swapped = lax.all_to_all(partial.astype(BF16), AXES, 0, 0, tiled=True)
    spread = pl.pallas_call(
        sum_kernel,
        out_shape=jax.ShapeDtypeStruct((devices, 2, share), BF16),
        in_specs=[VMEM],
        out_specs=VMEM,
        compiler_params=pltpu.CompilerParams(vmem_limit_bytes=4 << 20),
    )(swapped)
    sums = lax.all_to_all(spread, AXES, 0, 0, tiled=True)

    tables = [
        pltpu.with_memory_space_constraint(x, pltpu.VMEM)
        for x in (cos_head, sin_head, cos_late, sin_late)
    ]
    potential, field = pl.pallas_call(
        functools.partial(response_kernel, tile=4096),
        out_shape=(
            jax.ShapeDtypeStruct((1, own), F32),
            jax.ShapeDtypeStruct((3, own), F32),
        ),
        in_specs=[VMEM] * 6,
        out_specs=(VMEM, VMEM),
        compiler_params=pltpu.CompilerParams(vmem_limit_bytes=4 << 20),
    )(sums, coef, *tables)
    return (hidden, potential.reshape(own), field)


def solution(mesh):
    placed = (
        P(AXES, None),
        P(None, AXES),
        P(AXES, None),
        P(AXES),
        P(),
        P(),
        P(),
        P(),
    )
    return jax.shard_map(
        per_device,
        mesh=mesh,
        in_specs=placed,
        out_specs=(P(AXES, None), P(AXES), P(None, AXES)),
        check_vma=False,
    )
```

```python
import functools
import math

import jax
import jax.numpy as jnp
from jax import lax
from jax.experimental import pallas as pl
from jax.experimental.pallas import tpu as pltpu
from jax.sharding import PartitionSpec as P

LAYERS = 2
HALO = 64
AXES = ("brick", "kvec")
LANES = 128
F32 = jnp.float32
BF16 = jnp.bfloat16

VMEM = pl.BlockSpec(memory_space=pltpu.VMEM)
HBM = pl.BlockSpec(memory_space=pltpu.HBM)


def pieces(x):
    first = x.astype(BF16).astype(F32)
    rest = x - first
    second = rest.astype(BF16).astype(F32)
    return first, second, rest - second


def pack_kernel(
    feat_ref, pos_ref, neigh_ref, counts_ref, wave_ref, first_ref, last_ref, waves_ref,
    held_ref, sem,
):
    slots, own = neigh_ref.shape
    channels = feat_ref.shape[1]
    copy = pltpu.make_async_copy(wave_ref, waves_ref, sem)
    copy.start()
    held_ref[...] = pos_ref[...]
    rows = lax.broadcasted_iota(jnp.int32, (slots, own), 1)
    slot = lax.broadcasted_iota(jnp.int32, (slots, own), 0)
    delta = (neigh_ref[...] - HALO - rows).astype(F32)
    delta = jnp.where(slot < counts_ref[...], delta, 0.0)
    zero5 = jnp.zeros((5, own), F32)
    coords = [jnp.concatenate([p, zero5], axis=0) for p in pieces(pos_ref[...])]
    rest = jnp.zeros((LANES - slots - 24, own), F32)
    extra = jnp.concatenate([delta] + coords + [rest], axis=0).astype(BF16)
    half = own // 2
    for ref, start in ((first_ref, 0), (last_ref, half)):
        ref[:, :channels] = feat_ref[start : start + half, :]
        ref[:, channels:] = extra[:, start : start + half]
    copy.wait()


HALF_SINE = (4.438831262995637, -7.228964613368321, 3.149392241482131)


def horner(s, coefs):
    value = coefs[-1] * s + coefs[-2]
    for c in coefs[-3::-1]:
        value = value * s + c
    return value


def atom_pieces(pos_ref):
    a, b, c = pieces(pos_ref[...])
    own = pos_ref.shape[1]
    left = jnp.concatenate([a, a, b, b, a, c, jnp.zeros((14, own), F32)], axis=0)
    return left.astype(BF16)


def place(step, tile):
    return pl.ds(pl.multiple_of(step * tile, tile), tile)


def phase_pieces(wave, left_ref, out_ref, size):
    tile = wave.shape[1]
    u, v, w = pieces(wave * (0.5 / math.pi))
    right = jnp.concatenate([u, v, u, v, w, u, jnp.zeros((14, tile), F32)], axis=0)
    right = right.T.astype(BF16)

    def piece(start):
        out_ref[start : start + size, :] = jnp.dot(
            right[start : start + size], left_ref[...], preferred_element_type=F32
        )

    return [functools.partial(piece, start) for start in range(0, tile, size)]


def evaluate(in_ref, stores, chunk, woven):
    starts = range(0, in_ref.shape[0], chunk)
    for n, start in enumerate(starts):
        for turn, work in enumerate(woven):
            shift = 0 if turn % 2 else len(starts) - 1
            low, high = ((m * len(work) + shift) // len(starts) for m in (n, n + 1))
            for piece in work[low:high]:
                piece()
        t = in_ref[start : start + chunk, :]
        r = t - jnp.round(t)
        x = r * horner(r * r, HALF_SINE)
        square = x * x
        rest = 2.000002 - square
        cosine = (1.0 - square).astype(BF16)
        sine = (x * rest * lax.rsqrt(rest)).astype(BF16)
        for store in stores:
            store(start, cosine, sine)


def into_table(cos_ref, sin_ref, step, tile, chunk):
    def store(start, cosine, sine):
        rows = pl.ds(pl.multiple_of(step * tile + start, chunk), chunk)
        cos_ref[rows, :] = cosine
        sin_ref[rows, :] = sine

    return store


def into_tile(tile_ref, chunk):
    def store(start, cosine, sine):
        tile_ref[0, start : start + chunk, :] = cosine
        tile_ref[1, start : start + chunk, :] = sine

    return store


def histogram(delta):
    place = jnp.where(delta > 0, delta + 63.0, delta + 64.0)
    place = jnp.where(delta == 0, -1.0, place)
    deep = lax.broadcasted_iota(jnp.int32, (LANES, LANES), 0).astype(F32).astype(BF16)
    one = jnp.ones((LANES, LANES), BF16)
    zero = jnp.zeros((LANES, LANES), BF16)
    hist = zero
    for slot in range(64):
        row = jnp.broadcast_to(place[slot : slot + 1, :], (16, LANES)).astype(BF16)
        hist = hist + jnp.where(deep == jnp.concatenate([row] * 8, axis=0), one, zero)
    return hist.astype(F32).T


def early_kernel(
    pos_ref, wave_ref, first_ref, last_ref, w_in_ref, w_out_ref, w_charge_ref, cos_ref, sin_ref,
    coef_ref, hist_ref, w_in_out, w_out_out, w_charge_out, left_ref, even_ref, odd_ref, sems,
    *, tile, chunk, factor,
):
    copies = [
        pltpu.make_async_copy(source, target, sems.at[n])
        for n, (source, target) in enumerate(
            ((w_in_ref, w_in_out), (w_out_ref, w_out_out), (w_charge_ref, w_charge_out))
        )
    ]
    for copy in copies:
        copy.start()
    left_ref[...] = atom_pieces(pos_ref)
    channels = w_in_ref.shape[1]
    for n, ref in enumerate((first_ref, last_ref)):
        hist_ref[n * LANES : (n + 1) * LANES, :] = histogram(ref[:64, channels:].astype(F32))
    head = cos_ref.shape[0] // tile
    group = 8

    def scale(step):
        waves = [wave_ref[:, place(step + n, tile)] for n in range(group)]
        ksq = jnp.zeros((group, tile), F32)
        for c in range(3):
            part = jnp.concatenate([w[c : c + 1] for w in waves], axis=0)
            ksq = ksq + part * part
        coef = factor * jnp.exp(-0.1 * ksq) / ksq
        one = jnp.ones((1, tile), F32)
        for n, w in enumerate(waves):
            coef_ref[:, place(step + n, tile)] = coef[n : n + 1] * jnp.concatenate(
                [one, w, one, w], axis=0
            )

    def turn(step, out_ref):
        return phase_pieces(wave_ref[:, place(step, tile)], left_ref, out_ref, 64)

    for piece in turn(0, even_ref):
        piece()

    @pl.loop(0, head // 4)
    def _(block):
        base = 4 * block
        scale(2 * base)
        for n in range(4):
            now, later = (even_ref, odd_ref) if n % 2 == 0 else (odd_ref, even_ref)
            work = turn(jnp.minimum(base + n + 1, head - 1), later)
            evaluate(
                now, [into_table(cos_ref, sin_ref, base + n, tile, chunk)], chunk, [work]
            )

    for copy in copies:
        copy.wait()


def silu(x):
    return x / (1.0 + jnp.exp(-x))


def layer_kernel(
    before_ref, first_ref, last_ref, after_ref, w_in_ref, w_out_ref, w_charge_ref, hist_ref,
    pos_ref, wave_ref, cos_head_ref, sin_head_ref, hidden_ref, sums_ref, cos_ref, sin_ref,
    feat_ref, mid_ref, matrix_ref, left_ref, charge_ref, even_ref, odd_ref, even_tile_ref,
    odd_tile_ref, *, tile, chunk,
):
    parts = (before_ref, first_ref, last_ref, after_ref)
    half = before_ref.shape[0]
    channels = w_in_ref.shape[1]
    own = 2 * half
    for n, ref in enumerate(parts):
        feat_ref[n * half : (n + 1) * half, :] = ref[:, :channels]
    feat_ref[4 * half :, :] = jnp.zeros((HALO, channels), BF16)
    extras = [ref[:, channels:].astype(F32) for ref in parts]
    rows = [e[64:72] + e[72:80] + e[80:88] for e in extras]
    ext_rows = jnp.concatenate(rows + [jnp.zeros((8, LANES), F32)], axis=1)
    ext_cols = jnp.concatenate([r.T for r in rows], axis=0)
    lane = lax.broadcasted_iota(jnp.int32, (HALO, LANES), 1)
    ends = histogram(jnp.where(lane < HALO, extras[3][:64], extras[0][:64]))
    inner = [hist_ref[n * HALO : (n + 1) * HALO, :] for n in range(own // HALO)]
    hist_all = [ends[HALO:]] + inner + [ends[:HALO]]
    blocks = (own + 2 * HALO) // HALO
    zeros = jnp.zeros((HALO, LANES), F32)
    for block in range(blocks):
        base = HALO * (block + 1)
        hist = hist_all[block]
        low = jnp.concatenate([jnp.where(lane < 64, hist, 0.0), zeros], axis=1)
        high = jnp.concatenate([jnp.where(lane < 64, 0.0, hist), zeros], axis=1)
        counted = pltpu.roll(low, 0, 1, stride=1, stride_axis=0) + pltpu.roll(
            high, 1, 1, stride=1, stride_axis=0
        )
        dist = jnp.zeros((HALO, 2 * LANES), F32)
        for c in range(3):
            there = ext_rows[c : c + 1, HALO * block : HALO * block + 2 * LANES]
            diff = there - ext_cols[base : base + HALO, c : c + 1]
            dist = dist + diff * diff
        weight = counted / (1.0 + dist)
        upper = weight.astype(BF16)
        lower = (weight - upper.astype(F32)).astype(BF16)
        matrix_ref[block, :HALO, :] = upper
        matrix_ref[block, HALO:, :] = lower

    def advance(source_ref, layer, block_ids, row0, residual):
        messages = []
        for block in block_ids:
            start = HALO * (block - row0)
            out = jnp.dot(
                matrix_ref[block],
                source_ref[start : start + 2 * LANES, :],
                preferred_element_type=F32,
            )
            messages.append(out[:HALO] + out[HALO:])
        message = jnp.concatenate(messages, axis=0)
        scale = lax.rsqrt(jnp.mean(message * message, axis=-1, keepdims=True) + 1e-05)
        normed = (message * scale).astype(BF16)
        inner = silu(jnp.dot(normed, w_in_ref[layer], preferred_element_type=F32)).astype(BF16)
        update = jnp.dot(inner, w_out_ref[layer], preferred_element_type=F32)
        return (residual.astype(F32) + update).astype(BF16)

    grown = own + 2 * HALO
    mid_ref[:grown, :] = advance(
        feat_ref, 0, range(blocks), 0, feat_ref[HALO : HALO + grown, :]
    )
    mid_ref[grown:, :] = jnp.zeros((HALO, channels), BF16)
    final = advance(mid_ref, 1, range(1, blocks - 1), 1, mid_ref[HALO : HALO + own, :])
    hidden_ref[...] = final
    reader = jnp.concatenate(
        list(pieces(w_charge_ref[...])) + [jnp.zeros((5, channels), F32)], axis=0
    ).astype(BF16)
    read = lax.dot_general(
        reader, final, (((1,), (1,)), ((), ())), preferred_element_type=F32
    )
    charge = read[0:1] + read[1:2] + read[2:3]
    hi, mid, lo = pieces(charge)
    charges = jnp.concatenate([hi, mid, lo, jnp.zeros((5, own), F32)], axis=0).astype(BF16)

    charge_ref[...] = charges
    left_ref[...] = atom_pieces(pos_ref)
    head = cos_head_ref.shape[0] // tile
    late = cos_ref.shape[0] // tile
    share = sums_ref.shape[2]
    per = 2 * tile // share
    dims = (((1,), (1,)), ((), ()))

    def turn(step, out_ref):
        return phase_pieces(wave_ref[:, place(head + step, tile)], left_ref, out_ref, 64)

    def products(step, odd, tables):
        index = (step - odd) // 2 * per + odd * (per - 1)
        lanes = odd * (2 - per) * tile

        def piece(n, start):
            part = lax.dot_general(
                charge_ref[...], tables(n, start), dims, preferred_element_type=F32
            )
            part = part[0:1] + part[1:2] + part[2:3]
            sums_ref[index, n : n + 1, lanes + start : lanes + start + LANES] = part

        return [
            functools.partial(piece, n, start)
            for n in range(2)
            for start in range(0, tile, LANES)
        ]

    def late_table(tile_ref):
        return lambda n, start: tile_ref[n, start : start + LANES, :]

    def head_table(step):
        refs = (cos_head_ref, sin_head_ref)
        return lambda n, start: refs[n][
            pl.ds(pl.multiple_of(step * tile + start, LANES), LANES), :
        ]

    for piece in turn(0, even_ref):
        piece()

    @pl.loop(0, late // 4)
    def _(block):
        base = 4 * block
        slots = ((even_ref, even_tile_ref), (odd_ref, odd_tile_ref))
        for n in range(4):
            now, now_tile = slots[n % 2]
            later, last_tile = slots[1 - n % 2]
            step = base + n
            work = [
                turn(jnp.minimum(step + 1, late - 1), later),
                products(head + step - 1, 1 - n % 2, late_table(last_tile)),
                products(step, n % 2, head_table(step)),
            ]
            stores = [
                into_table(cos_ref, sin_ref, step, tile, chunk),
                into_tile(now_tile, chunk),
            ]
            evaluate(now, stores, chunk, work)

    for piece in products(head + late - 1, 1, late_table(odd_tile_ref)):
        piece()


def sum_kernel(parts_ref, out_ref):
    total = jnp.sum(parts_ref[...].astype(F32), axis=0, keepdims=True)
    out_ref[...] = jnp.broadcast_to(total, parts_ref.shape).astype(BF16)


def response_kernel(
    sums_ref, coef_ref, cos_head_ref, sin_head_ref, cos_ref, sin_ref, pot_ref, field_ref, *, tile
):
    share = sums_ref.shape[2]
    per = tile // share
    row = lax.broadcasted_iota(jnp.int32, (8, share), 0)
    lead = row % 4 == 0
    upper = row < 4
    totals = []
    segments = [(cos_head_ref, sin_head_ref, k) for k in range(0, cos_head_ref.shape[0], tile)]
    segments += [(cos_ref, sin_ref, k) for k in range(0, cos_ref.shape[0], tile)]
    for index, (cos_part, sin_part, start) in enumerate(segments):
        factors = ([], [])
        for q in range(index * per, (index + 1) * per):
            scaled = coef_ref[:, q * share : (q + 1) * share]
            sums = sums_ref[q].astype(F32)
            cosine = sums[0:1]
            sine = sums[1:2]
            for n, (top, other) in enumerate(((cosine, -sine), (sine, cosine))):
                full = scaled * jnp.where(lead, top, other)
                hi = full.astype(BF16).astype(F32)
                factors[n].append(jnp.where(upper, hi, full - hi))
        for n, ref in enumerate((cos_part, sin_part)):
            wide = jnp.concatenate(factors[n], axis=1).astype(BF16)
            totals.append(
                jnp.dot(wide, ref[start : start + tile, :], preferred_element_type=F32)
            )
    total = sum(totals[1:], totals[0])
    result = total[:4] + total[4:]
    pot_ref[...] = result[0:1]
    field_ref[...] = result[1:4]


def shifted(x, step):
    devices = lax.axis_size(AXES)
    pairs = [(i, i + step) for i in range(devices) if 0 <= i + step < devices]
    return lax.ppermute(x, AXES, pairs)


def per_device(features, positions, neighbours, counts, w_in, w_out, w_charge, wave):
    own, channels = features.shape
    total = wave.shape[1]
    devices = lax.axis_size(AXES)
    half = own // 2
    width = channels + LANES
    share = total // devices
    factor = 4.0 / math.sqrt(own * devices * total)
    dma = pltpu.SemaphoreType.DMA
    w_charge = w_charge.reshape(1, channels)
    wave, w_in, w_out, w_charge = (
        pltpu.with_memory_space_constraint(x, pltpu.HBM) for x in (wave, w_in, w_out, w_charge)
    )

    edge = pltpu.VMEM((half, width), BF16)
    first, last, waves, held = pl.pallas_call(
        pack_kernel,
        out_shape=(edge, edge, pltpu.VMEM(wave.shape, F32), pltpu.VMEM(positions.shape, F32)),
        in_specs=[VMEM] * 4 + [HBM],
        out_specs=(VMEM,) * 4,
        scratch_shapes=[dma],
    )(features, positions, neighbours.T, counts.reshape(1, own), wave)
    before = shifted(last, 1)
    after = shifted(first, -1)

    early = total // 2
    tile, chunk = 256, 32
    kept = pltpu.VMEM(w_in.shape, BF16)
    table = pltpu.VMEM((early, own), BF16)
    phases = [pltpu.VMEM((tile, own), F32)] * 2
    grant = pltpu.CompilerParams(vmem_limit_bytes=16 << 20)
    cos_head, sin_head, coef, hist, w_first, w_second, w_read = pl.pallas_call(
        functools.partial(early_kernel, tile=tile, chunk=chunk, factor=factor),
        out_shape=(
            table,
            table,
            pltpu.VMEM((8, total), F32),
            pltpu.VMEM((own, LANES), F32),
            kept,
            kept,
            pltpu.VMEM((1, channels), F32),
        ),
        in_specs=[VMEM] * 4 + [HBM] * 3,
        out_specs=(VMEM,) * 7,
        scratch_shapes=[pltpu.VMEM((32, own), BF16)] + phases + [dma((3,))],
        compiler_params=grant,
        cost_estimate=pl.CostEstimate(
            flops=own * early * 40, bytes_accessed=4 * own * early, transcendentals=0
        ),
    )(held, waves, first, last, w_in, w_out, w_charge)

    table = pltpu.VMEM((total - early, own), BF16)
    hidden, partial, cos_late, sin_late = pl.pallas_call(
        functools.partial(layer_kernel, tile=tile, chunk=chunk),
        out_shape=(
            jax.ShapeDtypeStruct((own, channels), BF16),
            jax.ShapeDtypeStruct((devices, 2, share), F32),
            table,
            table,
        ),
        in_specs=[VMEM] * 12,
        out_specs=(VMEM,) * 4,
        scratch_shapes=[
            pltpu.VMEM((4 * half + HALO, channels), BF16),
            pltpu.VMEM((own + 3 * HALO, channels), BF16),
            pltpu.VMEM((own // HALO + 2, 2 * HALO, 2 * LANES), BF16),
            pltpu.VMEM((32, own), BF16),
            pltpu.VMEM((8, own), BF16),
        ]
        + phases
        + [pltpu.VMEM((2, tile, own), BF16)] * 2,
        compiler_params=grant,
    )(before, first, last, after, w_first, w_second, w_read, hist, held, waves, cos_head, sin_head)

    swapped = lax.all_to_all(partial.astype(BF16), AXES, 0, 0, tiled=True)
    spread = pl.pallas_call(
        sum_kernel,
        out_shape=jax.ShapeDtypeStruct((devices, 2, share), BF16),
        in_specs=[VMEM],
        out_specs=VMEM,
        compiler_params=pltpu.CompilerParams(vmem_limit_bytes=4 << 20),
    )(swapped)
    sums = lax.all_to_all(spread, AXES, 0, 0, tiled=True)

    tables = [
        pltpu.with_memory_space_constraint(x, pltpu.VMEM)
        for x in (cos_head, sin_head, cos_late, sin_late)
    ]
    potential, field = pl.pallas_call(
        functools.partial(response_kernel, tile=4096),
        out_shape=(
            jax.ShapeDtypeStruct((1, own), F32),
            jax.ShapeDtypeStruct((3, own), F32),
        ),
        in_specs=[VMEM] * 6,
        out_specs=(VMEM, VMEM),
        compiler_params=pltpu.CompilerParams(vmem_limit_bytes=4 << 20),
    )(sums, coef, *tables)
    return (hidden, potential.reshape(own), field)


def solution(mesh):
    placed = (
        P(AXES, None),
        P(None, AXES),
        P(AXES, None),
        P(AXES),
        P(),
        P(),
        P(),
        P(),
    )
    return jax.shard_map(
        per_device,
        mesh=mesh,
        in_specs=placed,
        out_specs=(P(AXES, None), P(AXES), P(None, AXES)),
        check_vma=False,
    )
```

```python
import functools
import math

import jax
import jax.numpy as jnp
from jax import lax
from jax.experimental import pallas as pl
from jax.experimental.pallas import tpu as pltpu
from jax.sharding import PartitionSpec as P

LAYERS = 2
HALO = 64
AXES = ("brick", "kvec")
LANES = 128
F32 = jnp.float32
BF16 = jnp.bfloat16

VMEM = pl.BlockSpec(memory_space=pltpu.VMEM)
HBM = pl.BlockSpec(memory_space=pltpu.HBM)


def pieces(x):
    first = x.astype(BF16).astype(F32)
    rest = x - first
    second = rest.astype(BF16).astype(F32)
    return first, second, rest - second


def pack_kernel(
    feat_ref, pos_ref, neigh_ref, counts_ref, wave_ref, first_ref, last_ref, waves_ref,
    held_ref, sem,
):
    slots, own = neigh_ref.shape
    channels = feat_ref.shape[1]
    copy = pltpu.make_async_copy(wave_ref, waves_ref, sem)
    copy.start()
    held_ref[...] = pos_ref[...]
    rows = lax.broadcasted_iota(jnp.int32, (slots, own), 1)
    slot = lax.broadcasted_iota(jnp.int32, (slots, own), 0)
    delta = (neigh_ref[...] - HALO - rows).astype(F32)
    delta = jnp.where(slot < counts_ref[...], delta, 0.0)
    zero5 = jnp.zeros((5, own), F32)
    coords = [jnp.concatenate([p, zero5], axis=0) for p in pieces(pos_ref[...])]
    rest = jnp.zeros((LANES - slots - 24, own), F32)
    extra = jnp.concatenate([delta] + coords + [rest], axis=0).astype(BF16)
    half = own // 2
    for ref, start in ((first_ref, 0), (last_ref, half)):
        ref[:, :channels] = feat_ref[start : start + half, :]
        ref[:, channels:] = extra[:, start : start + half]
    copy.wait()


HALF_SINE = (4.438831262995637, -7.228964613368321, 3.149392241482131)


def horner(s, coefs):
    value = coefs[-1] * s + coefs[-2]
    for c in coefs[-3::-1]:
        value = value * s + c
    return value


def atom_pieces(pos_ref):
    a, b, c = pieces(pos_ref[...])
    own = pos_ref.shape[1]
    left = jnp.concatenate([a, a, b, b, a, c, jnp.zeros((LANES - 18, own), F32)], axis=0)
    return left.T.astype(BF16)[:, :32]


def place(step, tile):
    return pl.ds(pl.multiple_of(step * tile, tile), tile)


def phase(wave, left_ref, out_ref):
    tile = wave.shape[1]
    u, v, w = pieces(wave * (0.5 / math.pi))
    right = jnp.concatenate([u, v, u, v, w, u, jnp.zeros((14, tile), F32)], axis=0)
    out_ref[...] = jnp.dot(left_ref[...], right.astype(BF16), preferred_element_type=F32)


def evaluate(in_ref, stores, chunk):
    for start in range(0, in_ref.shape[0], chunk):
        t = in_ref[start : start + chunk, :]
        r = t - jnp.round(t)
        x = r * horner(r * r, HALF_SINE)
        square = x * x
        rest = 2.000002 - square
        cosine = (1.0 - square).astype(BF16)
        sine = (x * rest * lax.rsqrt(rest)).astype(BF16)
        for store in stores:
            store(start, cosine, sine)


def into_table(cos_ref, sin_ref, step, tile, chunk):
    def store(start, cosine, sine):
        cos_ref[start : start + chunk, place(step, tile)] = cosine
        sin_ref[start : start + chunk, place(step, tile)] = sine

    return store


def into_tile(tile_ref, chunk):
    def store(start, cosine, sine):
        tile_ref[0, start : start + chunk, :] = cosine
        tile_ref[1, start : start + chunk, :] = sine

    return store


def histogram(delta):
    place = jnp.where(delta > 0, delta + 63.0, delta + 64.0)
    place = jnp.where(delta == 0, -1.0, place)
    deep = lax.broadcasted_iota(jnp.int32, (LANES, LANES), 0).astype(F32).astype(BF16)
    one = jnp.ones((LANES, LANES), BF16)
    zero = jnp.zeros((LANES, LANES), BF16)
    hist = zero
    for slot in range(64):
        row = jnp.broadcast_to(place[slot : slot + 1, :], (16, LANES)).astype(BF16)
        hist = hist + jnp.where(deep == jnp.concatenate([row] * 8, axis=0), one, zero)
    return hist.astype(F32).T


def early_kernel(
    pos_ref, wave_ref, first_ref, last_ref, w_in_ref, w_out_ref, w_charge_ref, cos_ref, sin_ref,
    hist_ref, w_in_out, w_out_out, w_charge_out, left_ref, even_ref, odd_ref, sems,
    *, tile, chunk,
):
    copies = [
        pltpu.make_async_copy(source, target, sems.at[n])
        for n, (source, target) in enumerate(
            ((w_in_ref, w_in_out), (w_out_ref, w_out_out), (w_charge_ref, w_charge_out))
        )
    ]
    for copy in copies:
        copy.start()
    left_ref[...] = atom_pieces(pos_ref)
    channels = w_in_ref.shape[1]
    for n, ref in enumerate((first_ref, last_ref)):
        hist_ref[n * LANES : (n + 1) * LANES, :] = histogram(ref[:64, channels:].astype(F32))
    head = cos_ref.shape[1] // tile

    def turn(step, out_ref):
        phase(wave_ref[:, place(step, tile)], left_ref, out_ref)

    turn(0, even_ref)

    @pl.loop(0, head // 4)
    def _(block):
        base = 4 * block
        for step in range(0, 4, 2):
            turn(base + step + 1, odd_ref)
            evaluate(even_ref, [into_table(cos_ref, sin_ref, base + step, tile, chunk)], chunk)
            turn(jnp.minimum(base + step + 2, head - 1), even_ref)
            evaluate(odd_ref, [into_table(cos_ref, sin_ref, base + step + 1, tile, chunk)], chunk)

    for copy in copies:
        copy.wait()


def silu(x):
    return x / (1.0 + jnp.exp(-x))


def layer_kernel(
    before_ref, first_ref, last_ref, after_ref, w_in_ref, w_out_ref, w_charge_ref, hist_ref,
    pos_ref, wave_ref, cos_head_ref, sin_head_ref, hidden_ref, sums_ref, cos_ref, sin_ref,
    coef_ref, feat_ref, mid_ref, matrix_ref, left_ref, charge_ref, even_ref, odd_ref, even_tile_ref,
    odd_tile_ref, *, tile, chunk, factor,
):
    parts = (before_ref, first_ref, last_ref, after_ref)
    half = before_ref.shape[0]
    channels = w_in_ref.shape[1]
    own = 2 * half
    for n, ref in enumerate(parts):
        feat_ref[n * half : (n + 1) * half, :] = ref[:, :channels]
    feat_ref[4 * half :, :] = jnp.zeros((HALO, channels), BF16)
    extras = [ref[:, channels:].astype(F32) for ref in parts]
    rows = [e[64:72] + e[72:80] + e[80:88] for e in extras]
    ext_rows = jnp.concatenate(rows + [jnp.zeros((8, LANES), F32)], axis=1)
    ext_cols = jnp.concatenate([r.T for r in rows], axis=0)
    lane = lax.broadcasted_iota(jnp.int32, (HALO, LANES), 1)
    ends = histogram(jnp.where(lane < HALO, extras[3][:64], extras[0][:64]))
    inner = [hist_ref[n * HALO : (n + 1) * HALO, :] for n in range(own // HALO)]
    hist_all = [ends[HALO:]] + inner + [ends[:HALO]]
    blocks = (own + 2 * HALO) // HALO
    zeros = jnp.zeros((HALO, LANES), F32)
    for block in range(blocks):
        base = HALO * (block + 1)
        hist = hist_all[block]
        low = jnp.concatenate([jnp.where(lane < 64, hist, 0.0), zeros], axis=1)
        high = jnp.concatenate([jnp.where(lane < 64, 0.0, hist), zeros], axis=1)
        counted = pltpu.roll(low, 0, 1, stride=1, stride_axis=0) + pltpu.roll(
            high, 1, 1, stride=1, stride_axis=0
        )
        dist = jnp.zeros((HALO, 2 * LANES), F32)
        for c in range(3):
            there = ext_rows[c : c + 1, HALO * block : HALO * block + 2 * LANES]
            diff = there - ext_cols[base : base + HALO, c : c + 1]
            dist = dist + diff * diff
        weight = counted / (1.0 + dist)
        upper = weight.astype(BF16)
        lower = (weight - upper.astype(F32)).astype(BF16)
        matrix_ref[block, :HALO, :] = upper
        matrix_ref[block, HALO:, :] = lower

    def advance(source_ref, layer, block_ids, row0, residual):
        messages = []
        for block in block_ids:
            start = HALO * (block - row0)
            out = jnp.dot(
                matrix_ref[block],
                source_ref[start : start + 2 * LANES, :],
                preferred_element_type=F32,
            )
            messages.append(out[:HALO] + out[HALO:])
        message = jnp.concatenate(messages, axis=0)
        scale = lax.rsqrt(jnp.mean(message * message, axis=-1, keepdims=True) + 1e-05)
        normed = (message * scale).astype(BF16)
        inner = silu(jnp.dot(normed, w_in_ref[layer], preferred_element_type=F32)).astype(BF16)
        update = jnp.dot(inner, w_out_ref[layer], preferred_element_type=F32)
        return (residual.astype(F32) + update).astype(BF16)

    grown = own + 2 * HALO
    mid_ref[:grown, :] = advance(
        feat_ref, 0, range(blocks), 0, feat_ref[HALO : HALO + grown, :]
    )
    mid_ref[grown:, :] = jnp.zeros((HALO, channels), BF16)
    final = advance(mid_ref, 1, range(1, blocks - 1), 1, mid_ref[HALO : HALO + own, :])
    hidden_ref[...] = final
    reader = jnp.concatenate(
        list(pieces(w_charge_ref[...])) + [jnp.zeros((5, channels), F32)], axis=0
    ).astype(BF16)
    read = lax.dot_general(
        reader, final, (((1,), (1,)), ((), ())), preferred_element_type=F32
    )
    charge = read[0:1] + read[1:2] + read[2:3]
    hi, mid, lo = pieces(charge)
    charges = jnp.concatenate([hi, mid, lo, jnp.zeros((5, own), F32)], axis=0).astype(BF16)

    charge_ref[...] = charges
    left_ref[...] = atom_pieces(pos_ref)
    head = cos_head_ref.shape[1] // tile
    late = cos_ref.shape[1] // tile
    share = sums_ref.shape[2]
    per = 2 * tile // share
    group = 8

    def scale(step):
        waves = [wave_ref[:, place(step + n, tile)] for n in range(group)]
        ksq = jnp.zeros((group, tile), F32)
        for c in range(3):
            part = jnp.concatenate([w[c : c + 1] for w in waves], axis=0)
            ksq = ksq + part * part
        coef = factor * jnp.exp(-0.1 * ksq) / ksq
        one = jnp.ones((1, tile), F32)
        for n, w in enumerate(waves):
            coef_ref[:, place(step + n, tile)] = coef[n : n + 1] * jnp.concatenate(
                [one, w, one, w], axis=0
            )

    def turn(step, out_ref):
        phase(wave_ref[:, place(head + step, tile)], left_ref, out_ref)

    def added(step, cos_tile, sin_tile, odd):
        index = (step - odd) // 2 * per + odd * (per - 1)
        lanes = odd * (2 - per) * tile
        for n, table in enumerate((cos_tile, sin_tile)):
            part = jnp.dot(charge_ref[...], table, preferred_element_type=F32)
            part = part[0:1] + part[1:2] + part[2:3]
            sums_ref[index, n : n + 1, lanes : lanes + tile] = part

    turn(0, even_ref)

    @pl.loop(0, late // 4)
    def _(block):
        base = 4 * block
        slots = ((even_ref, even_tile_ref), (odd_ref, odd_tile_ref))
        for n in range(4):
            now, now_tile = slots[n % 2]
            later, last_tile = slots[1 - n % 2]
            step = base + n
            turn(jnp.minimum(step + 1, late - 1), later)
            added(head + step - 1, last_tile[0], last_tile[1], 1 - n % 2)
            for m in range(3 * n, 3 * n + 3):
                span = place(3 * base + m, tile)
                added(3 * base + m, cos_head_ref[:, span], sin_head_ref[:, span], m % 2)
            if n % 2 == 0:
                scale(4 * base + 4 * n)
            stores = [
                into_table(cos_ref, sin_ref, step, tile, chunk),
                into_tile(now_tile, chunk),
            ]
            evaluate(now, stores, chunk)

    added(head + late - 1, odd_tile_ref[0], odd_tile_ref[1], 1)


def sum_kernel(parts_ref, out_ref):
    total = jnp.sum(parts_ref[...].astype(F32), axis=0, keepdims=True)
    out_ref[...] = jnp.broadcast_to(total, parts_ref.shape).astype(BF16)


def response_kernel(
    sums_ref, coef_ref, cos_head_ref, sin_head_ref, cos_ref, sin_ref, pot_ref, field_ref, *, tile
):
    share = sums_ref.shape[2]
    row = lax.broadcasted_iota(jnp.int32, (8, share), 0)
    lead = row % 4 == 0
    upper = row < 4
    totals = [None] * 4
    dims = (((1,), (1,)), ((), ()))
    head = cos_head_ref.shape[1]
    for q in range(sums_ref.shape[0]):
        scaled = coef_ref[:, q * share : (q + 1) * share]
        sums = sums_ref[q].astype(F32)
        cosine = sums[0:1]
        sine = sums[1:2]
        early = q * share < head
        offset = q * share - (0 if early else head)
        refs = (cos_head_ref, sin_head_ref) if early else (cos_ref, sin_ref)
        for n, (top, other) in enumerate(((cosine, -sine), (sine, cosine))):
            full = scaled * jnp.where(lead, top, other)
            hi = full.astype(BF16).astype(F32)
            wide = jnp.where(upper, hi, full - hi).astype(BF16)
            for start in range(0, share, tile):
                part = lax.dot_general(
                    wide[:, start : start + tile],
                    refs[n][:, offset + start : offset + start + tile],
                    dims,
                    preferred_element_type=F32,
                )
                spot = (2 * start // tile + n) % 4
                totals[spot] = part if totals[spot] is None else totals[spot] + part
    totals = [t for t in totals if t is not None]
    total = sum(totals[1:], totals[0])
    result = total[:4] + total[4:]
    pot_ref[...] = result[0:1]
    field_ref[...] = result[1:4]


def shifted(x, step):
    devices = lax.axis_size(AXES)
    pairs = [(i, i + step) for i in range(devices) if 0 <= i + step < devices]
    return lax.ppermute(x, AXES, pairs)


def per_device(features, positions, neighbours, counts, w_in, w_out, w_charge, wave):
    own, channels = features.shape
    total = wave.shape[1]
    devices = lax.axis_size(AXES)
    half = own // 2
    width = channels + LANES
    share = total // devices
    factor = 4.0 / math.sqrt(own * devices * total)
    dma = pltpu.SemaphoreType.DMA
    w_charge = w_charge.reshape(1, channels)
    wave, w_in, w_out, w_charge = (
        pltpu.with_memory_space_constraint(x, pltpu.HBM) for x in (wave, w_in, w_out, w_charge)
    )

    edge = pltpu.VMEM((half, width), BF16)
    first, last, waves, held = pl.pallas_call(
        pack_kernel,
        out_shape=(edge, edge, pltpu.VMEM(wave.shape, F32), pltpu.VMEM(positions.shape, F32)),
        in_specs=[VMEM] * 4 + [HBM],
        out_specs=(VMEM,) * 4,
        scratch_shapes=[dma],
    )(features, positions, neighbours.T, counts.reshape(1, own), wave)
    before = shifted(last, 1)
    after = shifted(first, -1)

    early = 3 * total // 4
    tile, chunk = 256, 32
    kept = pltpu.VMEM(w_in.shape, BF16)
    table = pltpu.VMEM((own, early), BF16)
    phases = [pltpu.VMEM((own, tile), F32)] * 2
    grant = pltpu.CompilerParams(vmem_limit_bytes=16 << 20)
    cos_head, sin_head, hist, w_first, w_second, w_read = pl.pallas_call(
        functools.partial(early_kernel, tile=tile, chunk=chunk),
        out_shape=(
            table,
            table,
            pltpu.VMEM((own, LANES), F32),
            kept,
            kept,
            pltpu.VMEM((1, channels), F32),
        ),
        in_specs=[VMEM] * 4 + [HBM] * 3,
        out_specs=(VMEM,) * 6,
        scratch_shapes=[pltpu.VMEM((own, 32), BF16)] + phases + [dma((3,))],
        compiler_params=grant,
        cost_estimate=pl.CostEstimate(
            flops=own * early * 40, bytes_accessed=4 * own * early, transcendentals=0
        ),
    )(held, waves, first, last, w_in, w_out, w_charge)

    table = pltpu.VMEM((own, total - early), BF16)
    hidden, partial, cos_late, sin_late, coef = pl.pallas_call(
        functools.partial(layer_kernel, tile=tile, chunk=chunk, factor=factor),
        out_shape=(
            jax.ShapeDtypeStruct((own, channels), BF16),
            jax.ShapeDtypeStruct((devices, 2, share), F32),
            table,
            table,
            pltpu.VMEM((8, total), F32),
        ),
        in_specs=[VMEM] * 12,
        out_specs=(VMEM,) * 5,
        scratch_shapes=[
            pltpu.VMEM((4 * half + HALO, channels), BF16),
            pltpu.VMEM((own + 3 * HALO, channels), BF16),
            pltpu.VMEM((own // HALO + 2, 2 * HALO, 2 * LANES), BF16),
            pltpu.VMEM((own, 32), BF16),
            pltpu.VMEM((8, own), BF16),
        ]
        + phases
        + [pltpu.VMEM((2, own, tile), BF16)] * 2,
        compiler_params=grant,
    )(before, first, last, after, w_first, w_second, w_read, hist, held, waves, cos_head, sin_head)

    swapped = lax.all_to_all(partial.astype(BF16), AXES, 0, 0, tiled=True)
    spread = pl.pallas_call(
        sum_kernel,
        out_shape=jax.ShapeDtypeStruct((devices, 2, share), BF16),
        in_specs=[VMEM],
        out_specs=VMEM,
        compiler_params=pltpu.CompilerParams(vmem_limit_bytes=4 << 20),
    )(swapped)
    sums = lax.all_to_all(spread, AXES, 0, 0, tiled=True)

    tables = [
        pltpu.with_memory_space_constraint(x, pltpu.VMEM)
        for x in (cos_head, sin_head, cos_late, sin_late)
    ]
    potential, field = pl.pallas_call(
        functools.partial(response_kernel, tile=tile),
        out_shape=(
            jax.ShapeDtypeStruct((1, own), F32),
            jax.ShapeDtypeStruct((3, own), F32),
        ),
        in_specs=[VMEM] * 6,
        out_specs=(VMEM, VMEM),
        compiler_params=pltpu.CompilerParams(vmem_limit_bytes=4 << 20),
    )(sums, coef, *tables)
    return (hidden, potential.reshape(own), field)


def solution(mesh):
    placed = (
        P(AXES, None),
        P(None, AXES),
        P(AXES, None),
        P(AXES),
        P(),
        P(),
        P(),
        P(),
    )
    return jax.shard_map(
        per_device,
        mesh=mesh,
        in_specs=placed,
        out_specs=(P(AXES, None), P(AXES), P(None, AXES)),
        check_vma=False,
    )
```

```python
import functools
import math

import jax
import jax.numpy as jnp
from jax import lax
from jax.experimental import pallas as pl
from jax.experimental.pallas import tpu as pltpu
from jax.sharding import PartitionSpec as P

LAYERS = 2
HALO = 64
AXES = ("brick", "kvec")
LANES = 128
F32 = jnp.float32
BF16 = jnp.bfloat16

VMEM = pl.BlockSpec(memory_space=pltpu.VMEM)
HBM = pl.BlockSpec(memory_space=pltpu.HBM)


def pieces(x):
    first = x.astype(BF16).astype(F32)
    rest = x - first
    second = rest.astype(BF16).astype(F32)
    return first, second, rest - second


def pack_kernel(
    feat_ref, pos_ref, neigh_ref, counts_ref, wave_ref, first_ref, last_ref, waves_ref,
    held_ref, sem,
):
    slots, own = neigh_ref.shape
    channels = feat_ref.shape[1]
    copy = pltpu.make_async_copy(wave_ref, waves_ref, sem)
    copy.start()
    held_ref[...] = pos_ref[...]
    rows = lax.broadcasted_iota(jnp.int32, (slots, own), 1)
    slot = lax.broadcasted_iota(jnp.int32, (slots, own), 0)
    delta = (neigh_ref[...] - HALO - rows).astype(F32)
    delta = jnp.where(slot < counts_ref[...], delta, 0.0)
    zero5 = jnp.zeros((5, own), F32)
    coords = [jnp.concatenate([p, zero5], axis=0) for p in pieces(pos_ref[...])]
    rest = jnp.zeros((LANES - slots - 24, own), F32)
    extra = jnp.concatenate([delta] + coords + [rest], axis=0).astype(BF16)
    half = own // 2
    for ref, start in ((first_ref, 0), (last_ref, half)):
        ref[:, :channels] = feat_ref[start : start + half, :]
        ref[:, channels:] = extra[:, start : start + half]
    copy.wait()


HALF_SINE = (4.438831262995637, -7.228964613368321, 3.149392241482131)


def horner(s, coefs):
    value = coefs[-1] * s + coefs[-2]
    for c in coefs[-3::-1]:
        value = value * s + c
    return value


def atom_pieces(pos_ref):
    a, b, c = pieces(pos_ref[...])
    own = pos_ref.shape[1]
    left = jnp.concatenate([a, a, b, b, a, c, jnp.zeros((14, own), F32)], axis=0)
    return left.astype(BF16)


def place(step, tile):
    return pl.ds(pl.multiple_of(step * tile, tile), tile)


def phase(wave, left_ref, out_ref):
    tile = wave.shape[1]
    u, v, w = pieces(wave * (0.5 / math.pi))
    right = jnp.concatenate([u, v, u, v, w, u, jnp.zeros((14, tile), F32)], axis=0)
    out_ref[...] = jnp.dot(right.T.astype(BF16), left_ref[...], preferred_element_type=F32)


def evaluate(in_ref, stores, chunk):
    for start in range(0, in_ref.shape[0], chunk):
        t = in_ref[start : start + chunk, :]
        r = t - jnp.round(t)
        x = r * horner(r * r, HALF_SINE)
        square = x * x
        rest = 2.000002 - square
        cosine = (1.0 - square).astype(BF16)
        sine = (x * rest * lax.rsqrt(rest)).astype(BF16)
        for store in stores:
            store(start, cosine, sine)


def into_table(cos_ref, sin_ref, step, tile, chunk):
    def store(start, cosine, sine):
        rows = pl.ds(pl.multiple_of(step * tile + start, chunk), chunk)
        cos_ref[rows, :] = cosine
        sin_ref[rows, :] = sine

    return store


def into_tile(tile_ref, chunk):
    def store(start, cosine, sine):
        tile_ref[0, start : start + chunk, :] = cosine
        tile_ref[1, start : start + chunk, :] = sine

    return store


def histogram(delta):
    place = jnp.where(delta > 0, delta + 63.0, delta + 64.0)
    place = jnp.where(delta == 0, -1.0, place)
    deep = lax.broadcasted_iota(jnp.int32, (LANES, LANES), 0).astype(F32).astype(BF16)
    one = jnp.ones((LANES, LANES), BF16)
    zero = jnp.zeros((LANES, LANES), BF16)
    hist = zero
    for slot in range(64):
        row = jnp.broadcast_to(place[slot : slot + 1, :], (16, LANES)).astype(BF16)
        hist = hist + jnp.where(deep == jnp.concatenate([row] * 8, axis=0), one, zero)
    return hist.astype(F32).T


def early_kernel(
    pos_ref, wave_ref, first_ref, last_ref, w_in_ref, w_out_ref, w_charge_ref, cos_ref, sin_ref,
    coef_ref, hist_ref, w_in_out, w_out_out, w_charge_out, left_ref, even_ref, odd_ref, sems,
    *, tile, chunk, factor,
):
    copies = [
        pltpu.make_async_copy(source, target, sems.at[n])
        for n, (source, target) in enumerate(
            ((w_in_ref, w_in_out), (w_out_ref, w_out_out), (w_charge_ref, w_charge_out))
        )
    ]
    for copy in copies:
        copy.start()
    left_ref[...] = atom_pieces(pos_ref)
    channels = w_in_ref.shape[1]
    for n, ref in enumerate((first_ref, last_ref)):
        hist_ref[n * LANES : (n + 1) * LANES, :] = histogram(ref[:64, channels:].astype(F32))
    head = cos_ref.shape[0] // tile
    group = 8

    def scale(step):
        waves = [wave_ref[:, place(step + n, tile)] for n in range(group)]
        ksq = jnp.zeros((group, tile), F32)
        for c in range(3):
            part = jnp.concatenate([w[c : c + 1] for w in waves], axis=0)
            ksq = ksq + part * part
        coef = factor * jnp.exp(-0.1 * ksq) / ksq
        one = jnp.ones((1, tile), F32)
        for n, w in enumerate(waves):
            coef_ref[:, place(step + n, tile)] = coef[n : n + 1] * jnp.concatenate(
                [one, w, one, w], axis=0
            )

    def turn(step, out_ref):
        phase(wave_ref[:, place(step, tile)], left_ref, out_ref)

    scale(0)
    turn(0, even_ref)

    @pl.loop(0, head // 4)
    def _(block):
        base = 4 * block
        scale(2 * base + group)
        for step in range(0, 4, 2):
            turn(base + step + 1, odd_ref)
            evaluate(even_ref, [into_table(cos_ref, sin_ref, base + step, tile, chunk)], chunk)
            turn(jnp.minimum(base + step + 2, head - 1), even_ref)
            evaluate(odd_ref, [into_table(cos_ref, sin_ref, base + step + 1, tile, chunk)], chunk)

    for copy in copies:
        copy.wait()


def silu(x):
    return x / (1.0 + jnp.exp(-x))


def layer_kernel(
    before_ref, first_ref, last_ref, after_ref, w_in_ref, w_out_ref, w_charge_ref, hist_ref,
    pos_ref, wave_ref, cos_head_ref, sin_head_ref, hidden_ref, sums_ref, cos_ref, sin_ref,
    feat_ref, mid_ref, matrix_ref, left_ref, charge_ref, even_ref, odd_ref, even_tile_ref,
    odd_tile_ref, *, tile, chunk,
):
    parts = (before_ref, first_ref, last_ref, after_ref)
    half = before_ref.shape[0]
    channels = w_in_ref.shape[1]
    own = 2 * half
    for n, ref in enumerate(parts):
        feat_ref[n * half : (n + 1) * half, :] = ref[:, :channels]
    feat_ref[4 * half :, :] = jnp.zeros((HALO, channels), BF16)
    extras = [ref[:, channels:].astype(F32) for ref in parts]
    rows = [e[64:72] + e[72:80] + e[80:88] for e in extras]
    ext_rows = jnp.concatenate(rows + [jnp.zeros((8, LANES), F32)], axis=1)
    ext_cols = jnp.concatenate([r.T for r in rows], axis=0)
    lane = lax.broadcasted_iota(jnp.int32, (HALO, LANES), 1)
    ends = histogram(jnp.where(lane < HALO, extras[3][:64], extras[0][:64]))
    inner = [hist_ref[n * HALO : (n + 1) * HALO, :] for n in range(own // HALO)]
    hist_all = [ends[HALO:]] + inner + [ends[:HALO]]
    blocks = (own + 2 * HALO) // HALO
    zeros = jnp.zeros((HALO, LANES), F32)
    for block in range(blocks):
        base = HALO * (block + 1)
        hist = hist_all[block]
        low = jnp.concatenate([jnp.where(lane < 64, hist, 0.0), zeros], axis=1)
        high = jnp.concatenate([jnp.where(lane < 64, 0.0, hist), zeros], axis=1)
        counted = pltpu.roll(low, 0, 1, stride=1, stride_axis=0) + pltpu.roll(
            high, 1, 1, stride=1, stride_axis=0
        )
        dist = jnp.zeros((HALO, 2 * LANES), F32)
        for c in range(3):
            there = ext_rows[c : c + 1, HALO * block : HALO * block + 2 * LANES]
            diff = there - ext_cols[base : base + HALO, c : c + 1]
            dist = dist + diff * diff
        weight = counted / (1.0 + dist)
        upper = weight.astype(BF16)
        lower = (weight - upper.astype(F32)).astype(BF16)
        matrix_ref[block, :HALO, :] = upper
        matrix_ref[block, HALO:, :] = lower

    left_ref[...] = atom_pieces(pos_ref)
    head = cos_head_ref.shape[0] // tile
    late = cos_ref.shape[0] // tile
    filled = 8
    slots = (even_ref, odd_ref)

    def turn(step, out_ref):
        phase(wave_ref[:, place(head + step, tile)], left_ref, out_ref)

    def filler(step):
        turn(step + 1, slots[(step + 1) % 2])
        evaluate(
            slots[step % 2], [into_table(cos_ref, sin_ref, step, tile, chunk)], chunk
        )

    turn(0, even_ref)

    def advance(source_ref, layer, block_ids, row0, residual):
        messages = []
        for block in block_ids:
            start = HALO * (block - row0)
            out = jnp.dot(
                matrix_ref[block],
                source_ref[start : start + 2 * LANES, :],
                preferred_element_type=F32,
            )
            messages.append(out[:HALO] + out[HALO:])
        filler(4 * layer)
        message = jnp.concatenate(messages, axis=0)
        scale = lax.rsqrt(jnp.mean(message * message, axis=-1, keepdims=True) + 1e-05)
        filler(4 * layer + 1)
        normed = (message * scale).astype(BF16)
        inner = jnp.dot(normed, w_in_ref[layer], preferred_element_type=F32)
        filler(4 * layer + 2)
        inner = silu(inner).astype(BF16)
        update = jnp.dot(inner, w_out_ref[layer], preferred_element_type=F32)
        filler(4 * layer + 3)
        return (residual.astype(F32) + update).astype(BF16)

    grown = own + 2 * HALO
    mid_ref[:grown, :] = advance(
        feat_ref, 0, range(blocks), 0, feat_ref[HALO : HALO + grown, :]
    )
    mid_ref[grown:, :] = jnp.zeros((HALO, channels), BF16)
    final = advance(mid_ref, 1, range(1, blocks - 1), 1, mid_ref[HALO : HALO + own, :])
    hidden_ref[...] = final
    reader = jnp.concatenate(
        list(pieces(w_charge_ref[...])) + [jnp.zeros((5, channels), F32)], axis=0
    ).astype(BF16)
    read = lax.dot_general(
        reader, final, (((1,), (1,)), ((), ())), preferred_element_type=F32
    )
    charge = read[0:1] + read[1:2] + read[2:3]
    hi, mid, lo = pieces(charge)
    charges = jnp.concatenate([hi, mid, lo, jnp.zeros((5, own), F32)], axis=0).astype(BF16)

    charge_ref[...] = charges
    share = sums_ref.shape[2]
    per = 2 * tile // share
    dims = (((1,), (1,)), ((), ()))

    def added(step, cos_tile, sin_tile, odd):
        rows = []
        for table in (cos_tile, sin_tile):
            part = lax.dot_general(charge_ref[...], table, dims, preferred_element_type=F32)
            rows.append(part[0:1] + part[1:2] + part[2:3])
        index = (step - odd) // 2 * per + odd * (per - 1)
        lanes = odd * (2 - per) * tile
        sums_ref[index, :, lanes : lanes + tile] = jnp.concatenate(rows, axis=0)

    for step in range(filled - 1):
        rows = place(step, tile)
        added(head + step, cos_ref[rows, :], sin_ref[rows, :], step % 2)

    @pl.loop(0, (late - filled) // 4)
    def _(block):
        for pair in range(2):
            early = 4 * block + 2 * pair
            step = early + filled
            for n in range(2):
                rows = place(early + n, tile)
                added(early + n, cos_head_ref[rows, :], sin_head_ref[rows, :], n)
            turn(step + 1, odd_ref)
            added(head + step - 1, odd_tile_ref[0], odd_tile_ref[1], 1)
            evaluate(
                even_ref,
                [into_table(cos_ref, sin_ref, step, tile, chunk), into_tile(even_tile_ref, chunk)],
                chunk,
            )
            turn(jnp.minimum(step + 2, late - 1), even_ref)
            added(head + step, even_tile_ref[0], even_tile_ref[1], 0)
            evaluate(
                odd_ref,
                [
                    into_table(cos_ref, sin_ref, step + 1, tile, chunk),
                    into_tile(odd_tile_ref, chunk),
                ],
                chunk,
            )

    rows = place(filled - 1, tile)
    added(head + filled - 1, cos_ref[rows, :], sin_ref[rows, :], 1)
    added(head + late - 1, odd_tile_ref[0], odd_tile_ref[1], 1)


def sum_kernel(parts_ref, out_ref):
    total = jnp.sum(parts_ref[...].astype(F32), axis=0, keepdims=True)
    out_ref[...] = jnp.broadcast_to(total, parts_ref.shape).astype(BF16)


def response_kernel(
    sums_ref, coef_ref, cos_head_ref, sin_head_ref, cos_ref, sin_ref, pot_ref, field_ref, *, tile
):
    share = sums_ref.shape[2]
    per = tile // share
    row = lax.broadcasted_iota(jnp.int32, (8, share), 0)
    lead = row % 4 == 0
    upper = row < 4
    totals = []
    segments = [(cos_head_ref, sin_head_ref, k) for k in range(0, cos_head_ref.shape[0], tile)]
    segments += [(cos_ref, sin_ref, k) for k in range(0, cos_ref.shape[0], tile)]
    for index, (cos_part, sin_part, start) in enumerate(segments):
        factors = ([], [])
        for q in range(index * per, (index + 1) * per):
            scaled = coef_ref[:, q * share : (q + 1) * share]
            sums = sums_ref[q].astype(F32)
            cosine = sums[0:1]
            sine = sums[1:2]
            for n, (top, other) in enumerate(((cosine, -sine), (sine, cosine))):
                full = scaled * jnp.where(lead, top, other)
                hi = full.astype(BF16).astype(F32)
                factors[n].append(jnp.where(upper, hi, full - hi))
        for n, ref in enumerate((cos_part, sin_part)):
            wide = jnp.concatenate(factors[n], axis=1).astype(BF16)
            totals.append(
                jnp.dot(wide, ref[start : start + tile, :], preferred_element_type=F32)
            )
    total = sum(totals[1:], totals[0])
    result = total[:4] + total[4:]
    pot_ref[...] = result[0:1]
    field_ref[...] = result[1:4]


def shifted(x, step):
    devices = lax.axis_size(AXES)
    pairs = [(i, i + step) for i in range(devices) if 0 <= i + step < devices]
    return lax.ppermute(x, AXES, pairs)


def per_device(features, positions, neighbours, counts, w_in, w_out, w_charge, wave):
    own, channels = features.shape
    total = wave.shape[1]
    devices = lax.axis_size(AXES)
    half = own // 2
    width = channels + LANES
    share = total // devices
    factor = 4.0 / math.sqrt(own * devices * total)
    dma = pltpu.SemaphoreType.DMA
    w_charge = w_charge.reshape(1, channels)
    wave, w_in, w_out, w_charge = (
        pltpu.with_memory_space_constraint(x, pltpu.HBM) for x in (wave, w_in, w_out, w_charge)
    )

    edge = pltpu.VMEM((half, width), BF16)
    first, last, waves, held = pl.pallas_call(
        pack_kernel,
        out_shape=(edge, edge, pltpu.VMEM(wave.shape, F32), pltpu.VMEM(positions.shape, F32)),
        in_specs=[VMEM] * 4 + [HBM],
        out_specs=(VMEM,) * 4,
        scratch_shapes=[dma],
    )(features, positions, neighbours.T, counts.reshape(1, own), wave)
    before = shifted(last, 1)
    after = shifted(first, -1)

    tile, chunk = 256, 32
    early = (total - 8 * tile) // 2
    kept = pltpu.VMEM(w_in.shape, BF16)
    table = pltpu.VMEM((early, own), BF16)
    phases = [pltpu.VMEM((tile, own), F32)] * 2
    grant = pltpu.CompilerParams(vmem_limit_bytes=16 << 20)
    cos_head, sin_head, coef, hist, w_first, w_second, w_read = pl.pallas_call(
        functools.partial(early_kernel, tile=tile, chunk=chunk, factor=factor),
        out_shape=(
            table,
            table,
            pltpu.VMEM((8, total), F32),
            pltpu.VMEM((own, LANES), F32),
            kept,
            kept,
            pltpu.VMEM((1, channels), F32),
        ),
        in_specs=[VMEM] * 4 + [HBM] * 3,
        out_specs=(VMEM,) * 7,
        scratch_shapes=[pltpu.VMEM((32, own), BF16)] + phases + [dma((3,))],
        compiler_params=grant,
        cost_estimate=pl.CostEstimate(
            flops=own * early * 40, bytes_accessed=4 * own * early, transcendentals=0
        ),
    )(held, waves, first, last, w_in, w_out, w_charge)

    table = pltpu.VMEM((total - early, own), BF16)
    hidden, partial, cos_late, sin_late = pl.pallas_call(
        functools.partial(layer_kernel, tile=tile, chunk=chunk),
        out_shape=(
            jax.ShapeDtypeStruct((own, channels), BF16),
            jax.ShapeDtypeStruct((devices, 2, share), F32),
            table,
            table,
        ),
        in_specs=[VMEM] * 12,
        out_specs=(VMEM,) * 4,
        scratch_shapes=[
            pltpu.VMEM((4 * half + HALO, channels), BF16),
            pltpu.VMEM((own + 3 * HALO, channels), BF16),
            pltpu.VMEM((own // HALO + 2, 2 * HALO, 2 * LANES), BF16),
            pltpu.VMEM((32, own), BF16),
            pltpu.VMEM((8, own), BF16),
        ]
        + phases
        + [pltpu.VMEM((2, tile, own), BF16)] * 2,
        compiler_params=grant,
    )(before, first, last, after, w_first, w_second, w_read, hist, held, waves, cos_head, sin_head)

    swapped = lax.all_to_all(partial.astype(BF16), AXES, 0, 0, tiled=True)
    spread = pl.pallas_call(
        sum_kernel,
        out_shape=jax.ShapeDtypeStruct((devices, 2, share), BF16),
        in_specs=[VMEM],
        out_specs=VMEM,
        compiler_params=pltpu.CompilerParams(vmem_limit_bytes=4 << 20),
    )(swapped)
    sums = lax.all_to_all(spread, AXES, 0, 0, tiled=True)

    tables = [
        pltpu.with_memory_space_constraint(x, pltpu.VMEM)
        for x in (cos_head, sin_head, cos_late, sin_late)
    ]
    potential, field = pl.pallas_call(
        functools.partial(response_kernel, tile=1024),
        out_shape=(
            jax.ShapeDtypeStruct((1, own), F32),
            jax.ShapeDtypeStruct((3, own), F32),
        ),
        in_specs=[VMEM] * 6,
        out_specs=(VMEM, VMEM),
        compiler_params=pltpu.CompilerParams(vmem_limit_bytes=4 << 20),
    )(sums, coef, *tables)
    return (hidden, potential.reshape(own), field)


def solution(mesh):
    placed = (
        P(AXES, None),
        P(None, AXES),
        P(AXES, None),
        P(AXES),
        P(),
        P(),
        P(),
        P(),
    )
    return jax.shard_map(
        per_device,
        mesh=mesh,
        in_specs=placed,
        out_specs=(P(AXES, None), P(AXES), P(None, AXES)),
        check_vma=False,
    )
```

```python
import functools
import math

import jax
import jax.numpy as jnp
from jax import lax
from jax.experimental import pallas as pl
from jax.experimental.pallas import tpu as pltpu
from jax.sharding import PartitionSpec as P

LAYERS = 2
HALO = 64
AXES = ("brick", "kvec")
LANES = 128
F32 = jnp.float32
BF16 = jnp.bfloat16

VMEM = pl.BlockSpec(memory_space=pltpu.VMEM)
HBM = pl.BlockSpec(memory_space=pltpu.HBM)


def pieces(x):
    first = x.astype(BF16).astype(F32)
    rest = x - first
    second = rest.astype(BF16).astype(F32)
    return first, second, rest - second


def pack_kernel(
    feat_ref, pos_ref, neigh_ref, counts_ref, first_ref, last_ref, held_ref, slots_ref, used_ref,
    sems,
):
    slots, own = neigh_ref.shape
    channels = feat_ref.shape[1]
    half = own // 2
    copies = [
        pltpu.make_async_copy(source, target, sems.at[n])
        for n, (source, target) in enumerate(
            (
                (neigh_ref, slots_ref),
                (pos_ref, held_ref),
                (counts_ref, used_ref),
                (feat_ref.at[:half, :], first_ref.at[:, :channels]),
                (feat_ref.at[half:, :], last_ref.at[:, :channels]),
            )
        )
    ]
    for copy in copies:
        copy.start()
    rows = lax.broadcasted_iota(jnp.int32, (slots, own), 1)
    slot = lax.broadcasted_iota(jnp.int32, (slots, own), 0)
    for copy in copies:
        copy.wait()
    delta = (slots_ref[...] - HALO - rows).astype(F32)
    delta = jnp.where(slot < used_ref[...], delta, 0.0)
    zero5 = jnp.zeros((5, own), F32)
    coords = [jnp.concatenate([p, zero5], axis=0) for p in pieces(held_ref[...])]
    rest = jnp.zeros((LANES - slots - 24, own), F32)
    extra = jnp.concatenate([delta] + coords + [rest], axis=0).astype(BF16)
    first_ref[:, channels:] = extra[:, :half]
    last_ref[:, channels:] = extra[:, half:]


HALF_SINE = (4.438831262995637, -7.228964613368321, 3.149392241482131)


def horner(s, coefs):
    value = coefs[-1] * s + coefs[-2]
    for c in coefs[-3::-1]:
        value = value * s + c
    return value


def atom_pieces(pos_ref):
    a, b, c = pieces(pos_ref[...])
    own = pos_ref.shape[1]
    left = jnp.concatenate([a, a, b, b, a, c, jnp.zeros((14, own), F32)], axis=0)
    return left.astype(BF16)


def place(step, tile):
    return pl.ds(pl.multiple_of(step * tile, tile), tile)


def phase(wave, left_ref, out_ref):
    tile = wave.shape[1]
    u, v, w = pieces(wave * (0.5 / math.pi))
    right = jnp.concatenate([u, v, u, v, w, u, jnp.zeros((14, tile), F32)], axis=0)
    out_ref[...] = jnp.dot(right.T.astype(BF16), left_ref[...], preferred_element_type=F32)


def evaluate(in_ref, stores, chunk):
    for start in range(0, in_ref.shape[0], chunk):
        t = in_ref[start : start + chunk, :]
        r = t - jnp.round(t)
        x = r * horner(r * r, HALF_SINE)
        square = x * x
        rest = 2.000002 - square
        cosine = (1.0 - square).astype(BF16)
        sine = (x * rest * lax.rsqrt(rest)).astype(BF16)
        for store in stores:
            store(start, cosine, sine)


def into_table(cos_ref, sin_ref, step, tile, chunk):
    def store(start, cosine, sine):
        rows = pl.ds(pl.multiple_of(step * tile + start, chunk), chunk)
        cos_ref[rows, :] = cosine
        sin_ref[rows, :] = sine

    return store


def into_tile(tile_ref, chunk):
    def store(start, cosine, sine):
        tile_ref[0, start : start + chunk, :] = cosine
        tile_ref[1, start : start + chunk, :] = sine

    return store


def histogram(delta):
    place = jnp.where(delta > 0, delta + 63.0, delta + 64.0)
    place = jnp.where(delta == 0, -1.0, place)
    deep = lax.broadcasted_iota(jnp.int32, (LANES, LANES), 0).astype(F32).astype(BF16)
    one = jnp.ones((LANES, LANES), BF16)
    zero = jnp.zeros((LANES, LANES), BF16)
    hist = zero
    for slot in range(64):
        row = jnp.broadcast_to(place[slot : slot + 1, :], (16, LANES)).astype(BF16)
        hist = hist + jnp.where(deep == jnp.concatenate([row] * 8, axis=0), one, zero)
    return hist.astype(F32).T


def early_kernel(
    pos_ref, source_ref, first_ref, last_ref, w_in_ref, w_out_ref, w_charge_ref, cos_ref, sin_ref,
    coef_ref, hist_ref, wave_ref, w_in_out, w_out_out, w_charge_out, left_ref, even_ref, odd_ref, sems,
    *, tile, chunk, factor,
):
    copies = [
        pltpu.make_async_copy(source, target, sems.at[n])
        for n, (source, target) in enumerate(
            (
                (source_ref, wave_ref),
                (w_in_ref, w_in_out),
                (w_out_ref, w_out_out),
                (w_charge_ref, w_charge_out),
            )
        )
    ]
    for copy in copies:
        copy.start()
    left_ref[...] = atom_pieces(pos_ref)
    channels = w_in_ref.shape[1]
    for n, ref in enumerate((first_ref, last_ref)):
        hist_ref[n * LANES : (n + 1) * LANES, :] = histogram(ref[:64, channels:].astype(F32))
    head = cos_ref.shape[0] // tile
    group = 8

    def scale(step):
        waves = [wave_ref[:, place(step + n, tile)] for n in range(group)]
        ksq = jnp.zeros((group, tile), F32)
        for c in range(3):
            part = jnp.concatenate([w[c : c + 1] for w in waves], axis=0)
            ksq = ksq + part * part
        coef = factor * jnp.exp(-0.1 * ksq) / ksq
        one = jnp.ones((1, tile), F32)
        for n, w in enumerate(waves):
            coef_ref[:, place(step + n, tile)] = coef[n : n + 1] * jnp.concatenate(
                [one, w, one, w], axis=0
            )

    def turn(step, out_ref):
        phase(wave_ref[:, place(step, tile)], left_ref, out_ref)

    copies[0].wait()
    scale(0)
    turn(0, even_ref)

    @pl.loop(0, head // 4)
    def _(block):
        base = 4 * block
        scale(2 * base + group)
        for step in range(0, 4, 2):
            turn(base + step + 1, odd_ref)
            evaluate(even_ref, [into_table(cos_ref, sin_ref, base + step, tile, chunk)], chunk)
            turn(jnp.minimum(base + step + 2, head - 1), even_ref)
            evaluate(odd_ref, [into_table(cos_ref, sin_ref, base + step + 1, tile, chunk)], chunk)

    for copy in copies[1:]:
        copy.wait()


def silu(x):
    return x / (1.0 + jnp.exp(-x))


def layer_kernel(
    before_ref, first_ref, last_ref, after_ref, w_in_ref, w_out_ref, w_charge_ref, hist_ref,
    pos_ref, wave_ref, cos_head_ref, sin_head_ref, hidden_ref, sums_ref, cos_ref, sin_ref,
    feat_ref, mid_ref, matrix_ref, left_ref, charge_ref, even_ref, odd_ref, even_tile_ref,
    odd_tile_ref, final_ref, sem, *, tile, chunk,
):
    parts = (before_ref, first_ref, last_ref, after_ref)
    half = before_ref.shape[0]
    channels = w_in_ref.shape[1]
    own = 2 * half
    for n, ref in enumerate(parts):
        feat_ref[n * half : (n + 1) * half, :] = ref[:, :channels]
    feat_ref[4 * half :, :] = jnp.zeros((HALO, channels), BF16)
    extras = [ref[:, channels:].astype(F32) for ref in parts]
    rows = [e[64:72] + e[72:80] + e[80:88] for e in extras]
    ext_rows = jnp.concatenate(rows + [jnp.zeros((8, LANES), F32)], axis=1)
    ext_cols = jnp.concatenate([r.T for r in rows], axis=0)
    lane = lax.broadcasted_iota(jnp.int32, (HALO, LANES), 1)
    ends = histogram(jnp.where(lane < HALO, extras[3][:64], extras[0][:64]))
    inner = [hist_ref[n * HALO : (n + 1) * HALO, :] for n in range(own // HALO)]
    hist_all = [ends[HALO:]] + inner + [ends[:HALO]]
    blocks = (own + 2 * HALO) // HALO
    zeros = jnp.zeros((HALO, LANES), F32)
    for block in range(blocks):
        base = HALO * (block + 1)
        hist = hist_all[block]
        low = jnp.concatenate([jnp.where(lane < 64, hist, 0.0), zeros], axis=1)
        high = jnp.concatenate([jnp.where(lane < 64, 0.0, hist), zeros], axis=1)
        counted = pltpu.roll(low, 0, 1, stride=1, stride_axis=0) + pltpu.roll(
            high, 1, 1, stride=1, stride_axis=0
        )
        dist = jnp.zeros((HALO, 2 * LANES), F32)
        for c in range(3):
            there = ext_rows[c : c + 1, HALO * block : HALO * block + 2 * LANES]
            diff = there - ext_cols[base : base + HALO, c : c + 1]
            dist = dist + diff * diff
        weight = counted / (1.0 + dist)
        upper = weight.astype(BF16)
        lower = (weight - upper.astype(F32)).astype(BF16)
        matrix_ref[block, :HALO, :] = upper
        matrix_ref[block, HALO:, :] = lower

    left_ref[...] = atom_pieces(pos_ref)
    head = cos_head_ref.shape[0] // tile
    late = cos_ref.shape[0] // tile
    filled = 8
    slots = (even_ref, odd_ref)

    def turn(step, out_ref):
        phase(wave_ref[:, place(head + step, tile)], left_ref, out_ref)

    def filler(step):
        turn(step + 1, slots[(step + 1) % 2])
        evaluate(
            slots[step % 2], [into_table(cos_ref, sin_ref, step, tile, chunk)], chunk
        )

    turn(0, even_ref)

    def advance(source_ref, layer, block_ids, row0, residual):
        messages = []
        for block in block_ids:
            start = HALO * (block - row0)
            out = jnp.dot(
                matrix_ref[block],
                source_ref[start : start + 2 * LANES, :],
                preferred_element_type=F32,
            )
            messages.append(out[:HALO] + out[HALO:])
        filler(4 * layer)
        message = jnp.concatenate(messages, axis=0)
        scale = lax.rsqrt(jnp.mean(message * message, axis=-1, keepdims=True) + 1e-05)
        filler(4 * layer + 1)
        normed = (message * scale).astype(BF16)
        inner = jnp.dot(normed, w_in_ref[layer], preferred_element_type=F32)
        filler(4 * layer + 2)
        inner = silu(inner).astype(BF16)
        update = jnp.dot(inner, w_out_ref[layer], preferred_element_type=F32)
        filler(4 * layer + 3)
        return (residual.astype(F32) + update).astype(BF16)

    grown = own + 2 * HALO
    mid_ref[:grown, :] = advance(
        feat_ref, 0, range(blocks), 0, feat_ref[HALO : HALO + grown, :]
    )
    mid_ref[grown:, :] = jnp.zeros((HALO, channels), BF16)
    final = advance(mid_ref, 1, range(1, blocks - 1), 1, mid_ref[HALO : HALO + own, :])
    final_ref[...] = final
    leave = pltpu.make_async_copy(final_ref, hidden_ref, sem)
    leave.start()
    reader = jnp.concatenate(
        list(pieces(w_charge_ref[...])) + [jnp.zeros((5, channels), F32)], axis=0
    ).astype(BF16)
    read = lax.dot_general(
        reader, final, (((1,), (1,)), ((), ())), preferred_element_type=F32
    )
    charge = read[0:1] + read[1:2] + read[2:3]
    hi, mid, lo = pieces(charge)
    charges = jnp.concatenate([hi, mid, lo, jnp.zeros((5, own), F32)], axis=0).astype(BF16)

    charge_ref[...] = charges
    share = sums_ref.shape[2]
    per = 2 * tile // share
    dims = (((1,), (1,)), ((), ()))

    def added(step, cos_tile, sin_tile, odd):
        rows = []
        for table in (cos_tile, sin_tile):
            part = lax.dot_general(charge_ref[...], table, dims, preferred_element_type=F32)
            rows.append(part[0:1] + part[1:2] + part[2:3])
        index = (step - odd) // 2 * per + odd * (per - 1)
        lanes = odd * (2 - per) * tile
        sums_ref[index, :, lanes : lanes + tile] = jnp.concatenate(rows, axis=0)

    for step in range(filled - 1):
        rows = place(step, tile)
        added(head + step, cos_ref[rows, :], sin_ref[rows, :], step % 2)

    @pl.loop(0, (late - filled) // 4)
    def _(block):
        for pair in range(2):
            early = 4 * block + 2 * pair
            step = early + filled
            for n in range(2):
                rows = place(early + n, tile)
                added(early + n, cos_head_ref[rows, :], sin_head_ref[rows, :], n)
            turn(step + 1, odd_ref)
            added(head + step - 1, odd_tile_ref[0], odd_tile_ref[1], 1)
            evaluate(
                even_ref,
                [into_table(cos_ref, sin_ref, step, tile, chunk), into_tile(even_tile_ref, chunk)],
                chunk,
            )
            turn(jnp.minimum(step + 2, late - 1), even_ref)
            added(head + step, even_tile_ref[0], even_tile_ref[1], 0)
            evaluate(
                odd_ref,
                [
                    into_table(cos_ref, sin_ref, step + 1, tile, chunk),
                    into_tile(odd_tile_ref, chunk),
                ],
                chunk,
            )

    rows = place(filled - 1, tile)
    added(head + filled - 1, cos_ref[rows, :], sin_ref[rows, :], 1)
    added(head + late - 1, odd_tile_ref[0], odd_tile_ref[1], 1)
    leave.wait()


def sum_kernel(parts_ref, out_ref):
    total = jnp.sum(parts_ref[...].astype(F32), axis=0, keepdims=True)
    out_ref[...] = jnp.broadcast_to(total, parts_ref.shape).astype(BF16)


def response_kernel(
    sums_ref, coef_ref, cos_head_ref, sin_head_ref, cos_ref, sin_ref, pot_ref, field_ref, *, tile
):
    share = sums_ref.shape[2]
    per = tile // share
    row = lax.broadcasted_iota(jnp.int32, (8, share), 0)
    lead = row % 4 == 0
    upper = row < 4
    totals = []
    segments = [(cos_head_ref, sin_head_ref, k) for k in range(0, cos_head_ref.shape[0], tile)]
    segments += [(cos_ref, sin_ref, k) for k in range(0, cos_ref.shape[0], tile)]
    for index, (cos_part, sin_part, start) in enumerate(segments):
        factors = ([], [])
        for q in range(index * per, (index + 1) * per):
            scaled = coef_ref[:, q * share : (q + 1) * share]
            sums = sums_ref[q].astype(F32)
            cosine = sums[0:1]
            sine = sums[1:2]
            for n, (top, other) in enumerate(((cosine, -sine), (sine, cosine))):
                full = scaled * jnp.where(lead, top, other)
                hi = full.astype(BF16).astype(F32)
                factors[n].append(jnp.where(upper, hi, full - hi))
        for n, ref in enumerate((cos_part, sin_part)):
            wide = jnp.concatenate(factors[n], axis=1).astype(BF16)
            totals.append(
                jnp.dot(wide, ref[start : start + tile, :], preferred_element_type=F32)
            )
    total = sum(totals[1:], totals[0])
    result = total[:4] + total[4:]
    pot_ref[...] = result[0:1]
    field_ref[...] = result[1:4]


def shifted(x, step):
    devices = lax.axis_size(AXES)
    pairs = [(i, i + step) for i in range(devices) if 0 <= i + step < devices]
    return lax.ppermute(x, AXES, pairs)


def per_device(features, positions, neighbours, counts, w_in, w_out, w_charge, wave):
    own, channels = features.shape
    total = wave.shape[1]
    devices = lax.axis_size(AXES)
    half = own // 2
    width = channels + LANES
    share = total // devices
    factor = 4.0 / math.sqrt(own * devices * total)
    dma = pltpu.SemaphoreType.DMA
    w_charge = w_charge.reshape(1, channels)
    in_hbm = functools.partial(pltpu.with_memory_space_constraint, memory_space=pltpu.HBM)
    wave, w_in, w_out, w_charge = (in_hbm(x) for x in (wave, w_in, w_out, w_charge))

    edge = pltpu.VMEM((half, width), BF16)
    first, last, held = pl.pallas_call(
        pack_kernel,
        out_shape=(edge, edge, pltpu.VMEM(positions.shape, F32)),
        in_specs=[HBM] * 4,
        out_specs=(VMEM,) * 3,
        scratch_shapes=[
            pltpu.VMEM(neighbours.shape[::-1], jnp.int32),
            pltpu.VMEM((1, own), jnp.int32),
            dma((5,)),
        ],
    )(*(in_hbm(x) for x in (features, positions, neighbours.T, counts.reshape(1, own))))
    before = shifted(last, 1)
    after = shifted(first, -1)

    tile, chunk = 256, 32
    early = (total - 8 * tile) // 2
    kept = pltpu.VMEM(w_in.shape, BF16)
    table = pltpu.VMEM((early, own), BF16)
    phases = [pltpu.VMEM((tile, own), F32)] * 2
    grant = pltpu.CompilerParams(vmem_limit_bytes=16 << 20)
    cos_head, sin_head, coef, hist, waves, w_first, w_second, w_read = pl.pallas_call(
        functools.partial(early_kernel, tile=tile, chunk=chunk, factor=factor),
        out_shape=(
            table,
            table,
            pltpu.VMEM((8, total), F32),
            pltpu.VMEM((own, LANES), F32),
            pltpu.VMEM(wave.shape, F32),
            kept,
            kept,
            pltpu.VMEM((1, channels), F32),
        ),
        in_specs=[VMEM, HBM, VMEM, VMEM] + [HBM] * 3,
        out_specs=(VMEM,) * 8,
        scratch_shapes=[pltpu.VMEM((32, own), BF16)] + phases + [dma((4,))],
        compiler_params=grant,
        cost_estimate=pl.CostEstimate(
            flops=own * early * 40, bytes_accessed=4 * own * early, transcendentals=0
        ),
    )(held, wave, first, last, w_in, w_out, w_charge)

    table = pltpu.VMEM((total - early, own), BF16)
    hidden, partial, cos_late, sin_late = pl.pallas_call(
        functools.partial(layer_kernel, tile=tile, chunk=chunk),
        out_shape=(
            jax.ShapeDtypeStruct((own, channels), BF16),
            jax.ShapeDtypeStruct((devices, 2, share), F32),
            table,
            table,
        ),
        in_specs=[VMEM] * 12,
        out_specs=(HBM,) + (VMEM,) * 3,
        scratch_shapes=[
            pltpu.VMEM((4 * half + HALO, channels), BF16),
            pltpu.VMEM((own + 3 * HALO, channels), BF16),
            pltpu.VMEM((own // HALO + 2, 2 * HALO, 2 * LANES), BF16),
            pltpu.VMEM((32, own), BF16),
            pltpu.VMEM((8, own), BF16),
        ]
        + phases
        + [pltpu.VMEM((2, tile, own), BF16)] * 2
        + [pltpu.VMEM((own, channels), BF16), dma],
        compiler_params=grant,
    )(before, first, last, after, w_first, w_second, w_read, hist, held, waves, cos_head, sin_head)

    swapped = lax.all_to_all(partial.astype(BF16), AXES, 0, 0, tiled=True)
    spread = pl.pallas_call(
        sum_kernel,
        out_shape=jax.ShapeDtypeStruct((devices, 2, share), BF16),
        in_specs=[VMEM],
        out_specs=VMEM,
        compiler_params=pltpu.CompilerParams(vmem_limit_bytes=4 << 20),
    )(swapped)
    sums = lax.all_to_all(spread, AXES, 0, 0, tiled=True)

    tables = [
        pltpu.with_memory_space_constraint(x, pltpu.VMEM)
        for x in (cos_head, sin_head, cos_late, sin_late)
    ]
    potential, field = pl.pallas_call(
        functools.partial(response_kernel, tile=1024),
        out_shape=(
            jax.ShapeDtypeStruct((1, own), F32),
            jax.ShapeDtypeStruct((3, own), F32),
        ),
        in_specs=[VMEM] * 6,
        out_specs=(VMEM, VMEM),
        compiler_params=pltpu.CompilerParams(vmem_limit_bytes=4 << 20),
    )(sums, coef, *tables)
    return (hidden, potential.reshape(own), field)


def solution(mesh):
    placed = (
        P(AXES, None),
        P(None, AXES),
        P(AXES, None),
        P(AXES),
        P(),
        P(),
        P(),
        P(),
    )
    return jax.shard_map(
        per_device,
        mesh=mesh,
        in_specs=placed,
        out_specs=(P(AXES, None), P(AXES), P(None, AXES)),
        check_vma=False,
    )
```

```python
import functools
import math

import jax
import jax.numpy as jnp
from jax import lax
from jax.experimental import pallas as pl
from jax.experimental.pallas import tpu as pltpu
from jax.sharding import PartitionSpec as P

LAYERS = 2
HALO = 64
AXES = ("brick", "kvec")
LANES = 128
F32 = jnp.float32
BF16 = jnp.bfloat16

VMEM = pl.BlockSpec(memory_space=pltpu.VMEM)
HBM = pl.BlockSpec(memory_space=pltpu.HBM)


def pieces(x):
    first = x.astype(BF16).astype(F32)
    rest = x - first
    second = rest.astype(BF16).astype(F32)
    return first, second, rest - second


def even_device():
    index = lax.axis_index("brick") * lax.axis_size("kvec") + lax.axis_index("kvec")
    return index % 2 == 0


def chosen(even, one, other):
    return jnp.where(even, one.astype(F32), other.astype(F32)).astype(BF16)


def pack_kernel(
    feat_ref, pos_ref, neigh_ref, counts_ref, wave_ref, first_ref, last_ref, near_ref, far_ref,
    held_ref, waves_ref, slots_ref, used_ref, sems,
):
    slots, own = neigh_ref.shape
    channels = feat_ref.shape[1]
    half = own // 2
    copies = [
        pltpu.make_async_copy(source, target, sems.at[n])
        for n, (source, target) in enumerate(
            (
                (neigh_ref, slots_ref),
                (pos_ref, held_ref),
                (counts_ref, used_ref),
                (feat_ref.at[:half, :], first_ref.at[:, :channels]),
                (feat_ref.at[half:, :], last_ref.at[:, :channels]),
                (wave_ref, waves_ref),
            )
        )
    ]
    for copy in copies:
        copy.start()
    rows = lax.broadcasted_iota(jnp.int32, (slots, own), 1)
    slot = lax.broadcasted_iota(jnp.int32, (slots, own), 0)
    for copy in copies[:-1]:
        copy.wait()
    delta = (slots_ref[...] - HALO - rows).astype(F32)
    delta = jnp.where(slot < used_ref[...], delta, 0.0)
    zero5 = jnp.zeros((5, own), F32)
    coords = [jnp.concatenate([p, zero5], axis=0) for p in pieces(held_ref[...])]
    rest = jnp.zeros((LANES - slots - 24, own), F32)
    extra = jnp.concatenate([delta] + coords + [rest], axis=0).astype(BF16)
    first_ref[:, channels:] = extra[:, :half]
    last_ref[:, channels:] = extra[:, half:]
    even = even_device()
    near_ref[...] = chosen(even, last_ref[...], first_ref[...])
    far_ref[...] = chosen(even, first_ref[...], last_ref[...])
    copies[-1].wait()


HALF_SINE = (4.438831262995637, -7.228964613368321, 3.149392241482131)


def horner(s, coefs):
    value = coefs[-1] * s + coefs[-2]
    for c in coefs[-3::-1]:
        value = value * s + c
    return value


def atom_pieces(pos_ref):
    a, b, c = pieces(pos_ref[...])
    own = pos_ref.shape[1]
    left = jnp.concatenate([a, a, b, b, a, c, jnp.zeros((14, own), F32)], axis=0)
    return left.astype(BF16)


def place(step, tile):
    return pl.ds(pl.multiple_of(step * tile, tile), tile)


def phase(wave, left_ref, out_ref):
    tile = wave.shape[1]
    u, v, w = pieces(wave * (0.5 / math.pi))
    right = jnp.concatenate([u, v, u, v, w, u, jnp.zeros((14, tile), F32)], axis=0)
    out_ref[...] = jnp.dot(right.T.astype(BF16), left_ref[...], preferred_element_type=F32)


def evaluate(in_ref, stores, chunk):
    for start in range(0, in_ref.shape[0], chunk):
        t = in_ref[start : start + chunk, :]
        r = t - jnp.round(t)
        x = r * horner(r * r, HALF_SINE)
        square = x * x
        rest = 2.000002 - square
        cosine = (1.0 - square).astype(BF16)
        sine = (x * rest * lax.rsqrt(rest)).astype(BF16)
        for store in stores:
            store(start, cosine, sine)


def into_table(cos_ref, sin_ref, step, tile, chunk):
    def store(start, cosine, sine):
        rows = pl.ds(pl.multiple_of(step * tile + start, chunk), chunk)
        cos_ref[rows, :] = cosine
        sin_ref[rows, :] = sine

    return store


def into_tile(tile_ref, chunk):
    def store(start, cosine, sine):
        tile_ref[0, start : start + chunk, :] = cosine
        tile_ref[1, start : start + chunk, :] = sine

    return store


def histogram(delta):
    place = jnp.where(delta > 0, delta + 63.0, delta + 64.0)
    place = jnp.where(delta == 0, -1.0, place)
    deep = lax.broadcasted_iota(jnp.int32, (LANES, LANES), 0).astype(F32).astype(BF16)
    one = jnp.ones((LANES, LANES), BF16)
    zero = jnp.zeros((LANES, LANES), BF16)
    hist = zero
    for slot in range(64):
        row = jnp.broadcast_to(place[slot : slot + 1, :], (16, LANES)).astype(BF16)
        hist = hist + jnp.where(deep == jnp.concatenate([row] * 8, axis=0), one, zero)
    return hist.astype(F32).T


def early_kernel(
    pos_ref, wave_ref, first_ref, last_ref, w_in_ref, w_out_ref, w_charge_ref, cos_ref, sin_ref,
    coef_ref, hist_ref, w_in_out, w_out_out, w_charge_out, left_ref, even_ref, odd_ref, sems,
    *, tile, chunk, factor,
):
    copies = [
        pltpu.make_async_copy(source, target, sems.at[n])
        for n, (source, target) in enumerate(
            (
                (w_in_ref, w_in_out),
                (w_out_ref, w_out_out),
                (w_charge_ref, w_charge_out),
            )
        )
    ]
    for copy in copies:
        copy.start()
    left_ref[...] = atom_pieces(pos_ref)
    channels = w_in_ref.shape[1]
    for n, ref in enumerate((first_ref, last_ref)):
        hist_ref[n * LANES : (n + 1) * LANES, :] = histogram(ref[:64, channels:].astype(F32))
    head = cos_ref.shape[0] // tile
    group = 8

    def scale(step):
        waves = [wave_ref[:, place(step + n, tile)] for n in range(group)]
        ksq = jnp.zeros((group, tile), F32)
        for c in range(3):
            part = jnp.concatenate([w[c : c + 1] for w in waves], axis=0)
            ksq = ksq + part * part
        coef = factor * jnp.exp(-0.1 * ksq) / ksq
        one = jnp.ones((1, tile), F32)
        for n, w in enumerate(waves):
            coef_ref[:, place(step + n, tile)] = coef[n : n + 1] * jnp.concatenate(
                [one, w, one, w], axis=0
            )

    def turn(step, out_ref):
        phase(wave_ref[:, place(step, tile)], left_ref, out_ref)

    scale(0)
    turn(0, even_ref)

    @pl.loop(0, head // 4)
    def _(block):
        base = 4 * block
        scale(2 * base + group)
        for step in range(0, 4, 2):
            turn(base + step + 1, odd_ref)
            evaluate(even_ref, [into_table(cos_ref, sin_ref, base + step, tile, chunk)], chunk)
            turn(jnp.minimum(base + step + 2, head - 1), even_ref)
            evaluate(odd_ref, [into_table(cos_ref, sin_ref, base + step + 1, tile, chunk)], chunk)

    for copy in copies:
        copy.wait()


def silu(x):
    return x / (1.0 + jnp.exp(-x))


def layer_kernel(
    near_ref, first_ref, last_ref, far_ref, w_in_ref, w_out_ref, w_charge_ref, hist_ref,
    pos_ref, wave_ref, cos_head_ref, sin_head_ref, hidden_ref, sums_ref, cos_ref, sin_ref,
    feat_ref, mid_ref, matrix_ref, left_ref, charge_ref, even_ref, odd_ref, even_tile_ref,
    odd_tile_ref, final_ref, before_ref, after_ref, sem, *, tile, chunk,
):
    even = even_device()
    before_ref[...] = chosen(even, far_ref[...], near_ref[...])
    after_ref[...] = chosen(even, near_ref[...], far_ref[...])
    parts = (before_ref, first_ref, last_ref, after_ref)
    half = before_ref.shape[0]
    channels = w_in_ref.shape[1]
    own = 2 * half
    for n, ref in enumerate(parts):
        feat_ref[n * half : (n + 1) * half, :] = ref[:, :channels]
    feat_ref[4 * half :, :] = jnp.zeros((HALO, channels), BF16)
    extras = [ref[:, channels:].astype(F32) for ref in parts]
    rows = [e[64:72] + e[72:80] + e[80:88] for e in extras]
    ext_rows = jnp.concatenate(rows + [jnp.zeros((8, LANES), F32)], axis=1)
    ext_cols = jnp.concatenate([r.T for r in rows], axis=0)
    lane = lax.broadcasted_iota(jnp.int32, (HALO, LANES), 1)
    ends = histogram(jnp.where(lane < HALO, extras[3][:64], extras[0][:64]))
    inner = [hist_ref[n * HALO : (n + 1) * HALO, :] for n in range(own // HALO)]
    hist_all = [ends[HALO:]] + inner + [ends[:HALO]]
    blocks = (own + 2 * HALO) // HALO
    zeros = jnp.zeros((HALO, LANES), F32)
    for block in range(blocks):
        base = HALO * (block + 1)
        hist = hist_all[block]
        low = jnp.concatenate([jnp.where(lane < 64, hist, 0.0), zeros], axis=1)
        high = jnp.concatenate([jnp.where(lane < 64, 0.0, hist), zeros], axis=1)
        counted = pltpu.roll(low, 0, 1, stride=1, stride_axis=0) + pltpu.roll(
            high, 1, 1, stride=1, stride_axis=0
        )
        dist = jnp.zeros((HALO, 2 * LANES), F32)
        for c in range(3):
            there = ext_rows[c : c + 1, HALO * block : HALO * block + 2 * LANES]
            diff = there - ext_cols[base : base + HALO, c : c + 1]
            dist = dist + diff * diff
        weight = counted / (1.0 + dist)
        upper = weight.astype(BF16)
        lower = (weight - upper.astype(F32)).astype(BF16)
        matrix_ref[block, :HALO, :] = upper
        matrix_ref[block, HALO:, :] = lower

    left_ref[...] = atom_pieces(pos_ref)
    head = cos_head_ref.shape[0] // tile
    late = cos_ref.shape[0] // tile
    filled = 8
    slots = (even_ref, odd_ref)

    def turn(step, out_ref):
        phase(wave_ref[:, place(head + step, tile)], left_ref, out_ref)

    def filler(step):
        turn(step + 1, slots[(step + 1) % 2])
        evaluate(
            slots[step % 2], [into_table(cos_ref, sin_ref, step, tile, chunk)], chunk
        )

    turn(0, even_ref)

    def advance(source_ref, layer, block_ids, row0, residual):
        messages = []
        for block in block_ids:
            start = HALO * (block - row0)
            out = jnp.dot(
                matrix_ref[block],
                source_ref[start : start + 2 * LANES, :],
                preferred_element_type=F32,
            )
            messages.append(out[:HALO] + out[HALO:])
        filler(4 * layer)
        message = jnp.concatenate(messages, axis=0)
        scale = lax.rsqrt(jnp.mean(message * message, axis=-1, keepdims=True) + 1e-05)
        filler(4 * layer + 1)
        normed = (message * scale).astype(BF16)
        inner = jnp.dot(normed, w_in_ref[layer], preferred_element_type=F32)
        filler(4 * layer + 2)
        inner = silu(inner).astype(BF16)
        update = jnp.dot(inner, w_out_ref[layer], preferred_element_type=F32)
        filler(4 * layer + 3)
        return (residual.astype(F32) + update).astype(BF16)

    grown = own + 2 * HALO
    mid_ref[:grown, :] = advance(
        feat_ref, 0, range(blocks), 0, feat_ref[HALO : HALO + grown, :]
    )
    mid_ref[grown:, :] = jnp.zeros((HALO, channels), BF16)
    final = advance(mid_ref, 1, range(1, blocks - 1), 1, mid_ref[HALO : HALO + own, :])
    final_ref[...] = final
    leave = pltpu.make_async_copy(final_ref, hidden_ref, sem)
    leave.start()
    reader = jnp.concatenate(
        list(pieces(w_charge_ref[...])) + [jnp.zeros((5, channels), F32)], axis=0
    ).astype(BF16)
    read = lax.dot_general(
        reader, final, (((1,), (1,)), ((), ())), preferred_element_type=F32
    )
    charge = read[0:1] + read[1:2] + read[2:3]
    hi, mid, lo = pieces(charge)
    charges = jnp.concatenate([hi, mid, lo, jnp.zeros((5, own), F32)], axis=0).astype(BF16)

    charge_ref[...] = charges
    share = sums_ref.shape[2]
    per = 2 * tile // share
    dims = (((1,), (1,)), ((), ()))

    def added(step, cos_tile, sin_tile, odd):
        rows = []
        for table in (cos_tile, sin_tile):
            part = lax.dot_general(charge_ref[...], table, dims, preferred_element_type=F32)
            rows.append(part[0:1] + part[1:2] + part[2:3])
        index = (step - odd) // 2 * per + odd * (per - 1)
        lanes = odd * (2 - per) * tile
        sums_ref[index, :, lanes : lanes + tile] = jnp.concatenate(rows, axis=0)

    for step in range(filled - 1):
        rows = place(step, tile)
        added(head + step, cos_ref[rows, :], sin_ref[rows, :], step % 2)

    @pl.loop(0, (late - filled) // 4)
    def _(block):
        for pair in range(2):
            early = 4 * block + 2 * pair
            step = early + filled
            for n in range(2):
                rows = place(early + n, tile)
                added(early + n, cos_head_ref[rows, :], sin_head_ref[rows, :], n)
            turn(step + 1, odd_ref)
            added(head + step - 1, odd_tile_ref[0], odd_tile_ref[1], 1)
            evaluate(
                even_ref,
                [into_table(cos_ref, sin_ref, step, tile, chunk), into_tile(even_tile_ref, chunk)],
                chunk,
            )
            turn(jnp.minimum(step + 2, late - 1), even_ref)
            added(head + step, even_tile_ref[0], even_tile_ref[1], 0)
            evaluate(
                odd_ref,
                [
                    into_table(cos_ref, sin_ref, step + 1, tile, chunk),
                    into_tile(odd_tile_ref, chunk),
                ],
                chunk,
            )

    rows = place(filled - 1, tile)
    added(head + filled - 1, cos_ref[rows, :], sin_ref[rows, :], 1)
    added(head + late - 1, odd_tile_ref[0], odd_tile_ref[1], 1)
    leave.wait()


def sum_kernel(parts_ref, out_ref):
    total = jnp.sum(parts_ref[...].astype(F32), axis=0, keepdims=True)
    out_ref[...] = jnp.broadcast_to(total, parts_ref.shape).astype(BF16)


def response_kernel(
    sums_ref, coef_ref, cos_head_ref, sin_head_ref, cos_ref, sin_ref, pot_ref, field_ref, *, tile
):
    share = sums_ref.shape[2]
    per = tile // share
    row = lax.broadcasted_iota(jnp.int32, (8, share), 0)
    lead = row % 4 == 0
    upper = row < 4
    totals = []
    segments = [(cos_head_ref, sin_head_ref, k) for k in range(0, cos_head_ref.shape[0], tile)]
    segments += [(cos_ref, sin_ref, k) for k in range(0, cos_ref.shape[0], tile)]
    for index, (cos_part, sin_part, start) in enumerate(segments):
        factors = ([], [])
        for q in range(index * per, (index + 1) * per):
            scaled = coef_ref[:, q * share : (q + 1) * share]
            sums = sums_ref[q].astype(F32)
            cosine = sums[0:1]
            sine = sums[1:2]
            for n, (top, other) in enumerate(((cosine, -sine), (sine, cosine))):
                full = scaled * jnp.where(lead, top, other)
                hi = full.astype(BF16).astype(F32)
                factors[n].append(jnp.where(upper, hi, full - hi))
        for n, ref in enumerate((cos_part, sin_part)):
            wide = jnp.concatenate(factors[n], axis=1).astype(BF16)
            totals.append(
                jnp.dot(wide, ref[start : start + tile, :], preferred_element_type=F32)
            )
    total = sum(totals[1:], totals[0])
    result = total[:4] + total[4:]
    pot_ref[...] = result[0:1]
    field_ref[...] = result[1:4]


def exchanged(x, start):
    devices = lax.axis_size(AXES)
    pairs = [(i, i + 1) for i in range(start, devices - 1, 2)]
    return lax.ppermute(x, AXES, pairs + [(j, i) for i, j in pairs])


def per_device(features, positions, neighbours, counts, w_in, w_out, w_charge, wave):
    own, channels = features.shape
    total = wave.shape[1]
    devices = lax.axis_size(AXES)
    half = own // 2
    width = channels + LANES
    share = total // devices
    factor = 4.0 / math.sqrt(own * devices * total)
    dma = pltpu.SemaphoreType.DMA
    w_charge = w_charge.reshape(1, channels)
    in_hbm = functools.partial(pltpu.with_memory_space_constraint, memory_space=pltpu.HBM)
    wave, w_in, w_out, w_charge = (in_hbm(x) for x in (wave, w_in, w_out, w_charge))

    edge = pltpu.VMEM((half, width), BF16)
    first, last, near, far, held, waves = pl.pallas_call(
        pack_kernel,
        out_shape=(edge,) * 4
        + (pltpu.VMEM(positions.shape, F32), pltpu.VMEM(wave.shape, F32)),
        in_specs=[HBM] * 5,
        out_specs=(VMEM,) * 6,
        scratch_shapes=[
            pltpu.VMEM(neighbours.shape[::-1], jnp.int32),
            pltpu.VMEM((1, own), jnp.int32),
            dma((6,)),
        ],
    )(*(in_hbm(x) for x in (features, positions, neighbours.T, counts.reshape(1, own))), wave)
    near = exchanged(near, 0)
    far = exchanged(far, 1)

    tile, chunk = 256, 32
    early = (total - 8 * tile) // 2
    kept = pltpu.VMEM(w_in.shape, BF16)
    table = pltpu.VMEM((early, own), BF16)
    phases = [pltpu.VMEM((tile, own), F32)] * 2
    grant = pltpu.CompilerParams(vmem_limit_bytes=16 << 20)
    cos_head, sin_head, coef, hist, w_first, w_second, w_read = pl.pallas_call(
        functools.partial(early_kernel, tile=tile, chunk=chunk, factor=factor),
        out_shape=(
            table,
            table,
            pltpu.VMEM((8, total), F32),
            pltpu.VMEM((own, LANES), F32),
            kept,
            kept,
            pltpu.VMEM((1, channels), F32),
        ),
        in_specs=[VMEM] * 4 + [HBM] * 3,
        out_specs=(VMEM,) * 7,
        scratch_shapes=[pltpu.VMEM((32, own), BF16)] + phases + [dma((3,))],
        compiler_params=grant,
        cost_estimate=pl.CostEstimate(
            flops=own * early * 40, bytes_accessed=4 * own * early, transcendentals=0
        ),
    )(held, waves, first, last, w_in, w_out, w_charge)

    table = pltpu.VMEM((total - early, own), BF16)
    hidden, partial, cos_late, sin_late = pl.pallas_call(
        functools.partial(layer_kernel, tile=tile, chunk=chunk),
        out_shape=(
            jax.ShapeDtypeStruct((own, channels), BF16),
            jax.ShapeDtypeStruct((devices, 2, share), F32),
            table,
            table,
        ),
        in_specs=[VMEM] * 12,
        out_specs=(HBM,) + (VMEM,) * 3,
        scratch_shapes=[
            pltpu.VMEM((4 * half + HALO, channels), BF16),
            pltpu.VMEM((own + 3 * HALO, channels), BF16),
            pltpu.VMEM((own // HALO + 2, 2 * HALO, 2 * LANES), BF16),
            pltpu.VMEM((32, own), BF16),
            pltpu.VMEM((8, own), BF16),
        ]
        + phases
        + [pltpu.VMEM((2, tile, own), BF16)] * 2
        + [pltpu.VMEM((own, channels), BF16)]
        + [pltpu.VMEM((half, width), BF16)] * 2
        + [dma],
        compiler_params=grant,
    )(near, first, last, far, w_first, w_second, w_read, hist, held, waves, cos_head, sin_head)

    swapped = lax.all_to_all(partial.astype(BF16), AXES, 0, 0, tiled=True)
    spread = pl.pallas_call(
        sum_kernel,
        out_shape=jax.ShapeDtypeStruct((devices, 2, share), BF16),
        in_specs=[VMEM],
        out_specs=VMEM,
        compiler_params=pltpu.CompilerParams(vmem_limit_bytes=4 << 20),
    )(swapped)
    sums = lax.all_to_all(spread, AXES, 0, 0, tiled=True)

    tables = [
        pltpu.with_memory_space_constraint(x, pltpu.VMEM)
        for x in (cos_head, sin_head, cos_late, sin_late)
    ]
    potential, field = pl.pallas_call(
        functools.partial(response_kernel, tile=1024),
        out_shape=(
            jax.ShapeDtypeStruct((1, own), F32),
            jax.ShapeDtypeStruct((3, own), F32),
        ),
        in_specs=[VMEM] * 6,
        out_specs=(VMEM, VMEM),
        compiler_params=pltpu.CompilerParams(vmem_limit_bytes=4 << 20),
    )(sums, coef, *tables)
    return (hidden, potential.reshape(own), field)


def solution(mesh):
    placed = (
        P(AXES, None),
        P(None, AXES),
        P(AXES, None),
        P(AXES),
        P(),
        P(),
        P(),
        P(),
    )
    return jax.shard_map(
        per_device,
        mesh=mesh,
        in_specs=placed,
        out_specs=(P(AXES, None), P(AXES), P(None, AXES)),
        check_vma=False,
    )
```

```python
import functools
import math

import jax
import jax.numpy as jnp
from jax import lax
from jax.experimental import pallas as pl
from jax.experimental.pallas import tpu as pltpu
from jax.sharding import PartitionSpec as P

LAYERS = 2
HALO = 64
AXES = ("brick", "kvec")
LANES = 128
F32 = jnp.float32
BF16 = jnp.bfloat16

VMEM = pl.BlockSpec(memory_space=pltpu.VMEM)
HBM = pl.BlockSpec(memory_space=pltpu.HBM)


def pieces(x):
    first = x.astype(BF16).astype(F32)
    rest = x - first
    second = rest.astype(BF16).astype(F32)
    return first, second, rest - second


def even_device():
    index = lax.axis_index("brick") * lax.axis_size("kvec") + lax.axis_index("kvec")
    return index % 2 == 0


def chosen(even, one, other):
    return jnp.where(even, one.astype(F32), other.astype(F32)).astype(BF16)


def pack_kernel(
    feat_ref, pos_ref, neigh_ref, counts_ref, wave_ref, first_ref, last_ref, near_ref,
    held_ref, waves_ref, slots_ref, used_ref, sems,
):
    slots, own = neigh_ref.shape
    channels = feat_ref.shape[1]
    half = own // 2
    copies = [
        pltpu.make_async_copy(source, target, sems.at[n])
        for n, (source, target) in enumerate(
            (
                (neigh_ref, slots_ref),
                (pos_ref, held_ref),
                (counts_ref, used_ref),
                (feat_ref.at[:half, :], first_ref.at[:, :channels]),
                (feat_ref.at[half:, :], last_ref.at[:, :channels]),
                (wave_ref, waves_ref),
            )
        )
    ]
    for copy in copies:
        copy.start()
    rows = lax.broadcasted_iota(jnp.int32, (slots, own), 1)
    slot = lax.broadcasted_iota(jnp.int32, (slots, own), 0)
    for copy in copies[:-1]:
        copy.wait()
    delta = (slots_ref[...] - HALO - rows).astype(F32)
    delta = jnp.where(slot < used_ref[...], delta, 0.0)
    zero5 = jnp.zeros((5, own), F32)
    coords = [jnp.concatenate([p, zero5], axis=0) for p in pieces(held_ref[...])]
    rest = jnp.zeros((LANES - slots - 24, own), F32)
    extra = jnp.concatenate([delta] + coords + [rest], axis=0).astype(BF16)
    first_ref[:, channels:] = extra[:, :half]
    last_ref[:, channels:] = extra[:, half:]
    near_ref[...] = chosen(even_device(), last_ref[...], first_ref[...])
    copies[-1].wait()


HALF_SINE = (4.438831262995637, -7.228964613368321, 3.149392241482131)


def horner(s, coefs):
    value = coefs[-1] * s + coefs[-2]
    for c in coefs[-3::-1]:
        value = value * s + c
    return value


def atom_pieces(pos_ref):
    a, b, c = pieces(pos_ref[...])
    own = pos_ref.shape[1]
    left = jnp.concatenate([a, a, b, b, a, c, jnp.zeros((14, own), F32)], axis=0)
    return left.astype(BF16)


def place(step, tile):
    return pl.ds(pl.multiple_of(step * tile, tile), tile)


def phase(wave, left_ref, out_ref):
    tile = wave.shape[1]
    u, v, w = pieces(wave * (0.5 / math.pi))
    right = jnp.concatenate([u, v, u, v, w, u, jnp.zeros((14, tile), F32)], axis=0)
    out_ref[...] = jnp.dot(right.T.astype(BF16), left_ref[...], preferred_element_type=F32)


def evaluate(in_ref, stores, chunk):
    for start in range(0, in_ref.shape[0], chunk):
        t = in_ref[start : start + chunk, :]
        r = t - jnp.round(t)
        x = r * horner(r * r, HALF_SINE)
        square = x * x
        rest = 2.000002 - square
        cosine = (1.0 - square).astype(BF16)
        sine = (x * rest * lax.rsqrt(rest)).astype(BF16)
        for store in stores:
            store(start, cosine, sine)


def into_table(cos_ref, sin_ref, step, tile, chunk):
    def store(start, cosine, sine):
        rows = pl.ds(pl.multiple_of(step * tile + start, chunk), chunk)
        cos_ref[rows, :] = cosine
        sin_ref[rows, :] = sine

    return store


def into_tile(tile_ref, chunk):
    def store(start, cosine, sine):
        tile_ref[0, start : start + chunk, :] = cosine
        tile_ref[1, start : start + chunk, :] = sine

    return store


def histogram(delta):
    place = jnp.where(delta > 0, delta + 63.0, delta + 64.0)
    place = jnp.where(delta == 0, -1.0, place)
    deep = lax.broadcasted_iota(jnp.int32, (LANES, LANES), 0).astype(F32).astype(BF16)
    one = jnp.ones((LANES, LANES), BF16)
    zero = jnp.zeros((LANES, LANES), BF16)
    hist = zero
    for slot in range(64):
        row = jnp.broadcast_to(place[slot : slot + 1, :], (16, LANES)).astype(BF16)
        hist = hist + jnp.where(deep == jnp.concatenate([row] * 8, axis=0), one, zero)
    return hist.astype(F32).T


def prepare_kernel(wave_ref, first_ref, last_ref, far_ref, coef_ref, hist_ref, *, tile, factor):
    channels = first_ref.shape[1] - LANES
    far_ref[...] = chosen(even_device(), first_ref[...], last_ref[...])
    for n, ref in enumerate((first_ref, last_ref)):
        hist_ref[n * LANES : (n + 1) * LANES, :] = histogram(ref[:64, channels:].astype(F32))
    group = 8

    def scale(step):
        waves = [wave_ref[:, place(step + n, tile)] for n in range(group)]
        ksq = jnp.zeros((group, tile), F32)
        for c in range(3):
            part = jnp.concatenate([w[c : c + 1] for w in waves], axis=0)
            ksq = ksq + part * part
        coef = factor * jnp.exp(-0.1 * ksq) / ksq
        one = jnp.ones((1, tile), F32)
        for n, w in enumerate(waves):
            coef_ref[:, place(step + n, tile)] = coef[n : n + 1] * jnp.concatenate(
                [one, w, one, w], axis=0
            )

    @pl.loop(0, wave_ref.shape[1] // (2 * group * tile))
    def _(block):
        scale(2 * group * block)
        scale(2 * group * block + group)


def early_kernel(
    pos_ref, wave_ref, w_in_ref, w_out_ref, w_charge_ref, cos_ref, sin_ref,
    w_in_out, w_out_out, w_charge_out, left_ref, even_ref, odd_ref, sems,
    *, tile, chunk,
):
    copies = [
        pltpu.make_async_copy(source, target, sems.at[n])
        for n, (source, target) in enumerate(
            (
                (w_in_ref, w_in_out),
                (w_out_ref, w_out_out),
                (w_charge_ref, w_charge_out),
            )
        )
    ]
    for copy in copies:
        copy.start()
    left_ref[...] = atom_pieces(pos_ref)
    head = cos_ref.shape[0] // tile
    def turn(step, out_ref):
        phase(wave_ref[:, place(step, tile)], left_ref, out_ref)

    turn(0, even_ref)

    @pl.loop(0, head // 4)
    def _(block):
        base = 4 * block
        for step in range(0, 4, 2):
            turn(base + step + 1, odd_ref)
            evaluate(even_ref, [into_table(cos_ref, sin_ref, base + step, tile, chunk)], chunk)
            turn(jnp.minimum(base + step + 2, head - 1), even_ref)
            evaluate(odd_ref, [into_table(cos_ref, sin_ref, base + step + 1, tile, chunk)], chunk)

    for copy in copies:
        copy.wait()


def silu(x):
    return x / (1.0 + jnp.exp(-x))


def layer_kernel(
    near_ref, first_ref, last_ref, far_ref, w_in_ref, w_out_ref, w_charge_ref, hist_ref,
    pos_ref, wave_ref, cos_head_ref, sin_head_ref, hidden_ref, sums_ref, cos_ref, sin_ref,
    feat_ref, mid_ref, matrix_ref, left_ref, charge_ref, even_ref, odd_ref, even_tile_ref,
    odd_tile_ref, final_ref, before_ref, after_ref, sem, *, tile, chunk,
):
    even = even_device()
    before_ref[...] = chosen(even, far_ref[...], near_ref[...])
    after_ref[...] = chosen(even, near_ref[...], far_ref[...])
    parts = (before_ref, first_ref, last_ref, after_ref)
    half = before_ref.shape[0]
    channels = w_in_ref.shape[1]
    own = 2 * half
    for n, ref in enumerate(parts):
        feat_ref[n * half : (n + 1) * half, :] = ref[:, :channels]
    feat_ref[4 * half :, :] = jnp.zeros((HALO, channels), BF16)
    extras = [ref[:, channels:].astype(F32) for ref in parts]
    rows = [e[64:72] + e[72:80] + e[80:88] for e in extras]
    ext_rows = jnp.concatenate(rows + [jnp.zeros((8, LANES), F32)], axis=1)
    ext_cols = jnp.concatenate([r.T for r in rows], axis=0)
    lane = lax.broadcasted_iota(jnp.int32, (HALO, LANES), 1)
    ends = histogram(jnp.where(lane < HALO, extras[3][:64], extras[0][:64]))
    inner = [hist_ref[n * HALO : (n + 1) * HALO, :] for n in range(own // HALO)]
    hist_all = [ends[HALO:]] + inner + [ends[:HALO]]
    blocks = (own + 2 * HALO) // HALO
    zeros = jnp.zeros((HALO, LANES), F32)
    for block in range(blocks):
        base = HALO * (block + 1)
        hist = hist_all[block]
        low = jnp.concatenate([jnp.where(lane < 64, hist, 0.0), zeros], axis=1)
        high = jnp.concatenate([jnp.where(lane < 64, 0.0, hist), zeros], axis=1)
        counted = pltpu.roll(low, 0, 1, stride=1, stride_axis=0) + pltpu.roll(
            high, 1, 1, stride=1, stride_axis=0
        )
        dist = jnp.zeros((HALO, 2 * LANES), F32)
        for c in range(3):
            there = ext_rows[c : c + 1, HALO * block : HALO * block + 2 * LANES]
            diff = there - ext_cols[base : base + HALO, c : c + 1]
            dist = dist + diff * diff
        weight = counted / (1.0 + dist)
        upper = weight.astype(BF16)
        lower = (weight - upper.astype(F32)).astype(BF16)
        matrix_ref[block, :HALO, :] = upper
        matrix_ref[block, HALO:, :] = lower

    left_ref[...] = atom_pieces(pos_ref)
    head = cos_head_ref.shape[0] // tile
    late = cos_ref.shape[0] // tile
    filled = 8
    slots = (even_ref, odd_ref)

    def turn(step, out_ref):
        phase(wave_ref[:, place(head + step, tile)], left_ref, out_ref)

    def filler(step):
        turn(step + 1, slots[(step + 1) % 2])
        evaluate(
            slots[step % 2], [into_table(cos_ref, sin_ref, step, tile, chunk)], chunk
        )

    turn(0, even_ref)

    def advance(source_ref, layer, block_ids, row0, residual):
        messages = []
        for block in block_ids:
            start = HALO * (block - row0)
            out = jnp.dot(
                matrix_ref[block],
                source_ref[start : start + 2 * LANES, :],
                preferred_element_type=F32,
            )
            messages.append(out[:HALO] + out[HALO:])
        filler(4 * layer)
        message = jnp.concatenate(messages, axis=0)
        scale = lax.rsqrt(jnp.mean(message * message, axis=-1, keepdims=True) + 1e-05)
        filler(4 * layer + 1)
        normed = (message * scale).astype(BF16)
        inner = jnp.dot(normed, w_in_ref[layer], preferred_element_type=F32)
        filler(4 * layer + 2)
        inner = silu(inner).astype(BF16)
        update = jnp.dot(inner, w_out_ref[layer], preferred_element_type=F32)
        filler(4 * layer + 3)
        return (residual.astype(F32) + update).astype(BF16)

    grown = own + 2 * HALO
    mid_ref[:grown, :] = advance(
        feat_ref, 0, range(blocks), 0, feat_ref[HALO : HALO + grown, :]
    )
    mid_ref[grown:, :] = jnp.zeros((HALO, channels), BF16)
    final = advance(mid_ref, 1, range(1, blocks - 1), 1, mid_ref[HALO : HALO + own, :])
    final_ref[...] = final
    leave = pltpu.make_async_copy(final_ref, hidden_ref, sem)
    leave.start()
    reader = jnp.concatenate(
        list(pieces(w_charge_ref[...])) + [jnp.zeros((5, channels), F32)], axis=0
    ).astype(BF16)
    read = lax.dot_general(
        reader, final, (((1,), (1,)), ((), ())), preferred_element_type=F32
    )
    charge = read[0:1] + read[1:2] + read[2:3]
    hi, mid, lo = pieces(charge)
    charges = jnp.concatenate([hi, mid, lo, jnp.zeros((5, own), F32)], axis=0).astype(BF16)

    charge_ref[...] = charges
    share = sums_ref.shape[2]
    per = 2 * tile // share
    dims = (((1,), (1,)), ((), ()))

    def added(step, cos_tile, sin_tile, odd):
        rows = []
        for table in (cos_tile, sin_tile):
            part = lax.dot_general(charge_ref[...], table, dims, preferred_element_type=F32)
            rows.append(part[0:1] + part[1:2] + part[2:3])
        index = (step - odd) // 2 * per + odd * (per - 1)
        lanes = odd * (2 - per) * tile
        sums_ref[index, :, lanes : lanes + tile] = jnp.concatenate(rows, axis=0)

    for step in range(filled - 1):
        rows = place(step, tile)
        added(head + step, cos_ref[rows, :], sin_ref[rows, :], step % 2)

    @pl.loop(0, (late - filled) // 4)
    def _(block):
        for pair in range(2):
            early = 4 * block + 2 * pair
            step = early + filled
            for n in range(2):
                rows = place(early + n, tile)
                added(early + n, cos_head_ref[rows, :], sin_head_ref[rows, :], n)
            turn(step + 1, odd_ref)
            added(head + step - 1, odd_tile_ref[0], odd_tile_ref[1], 1)
            evaluate(
                even_ref,
                [into_table(cos_ref, sin_ref, step, tile, chunk), into_tile(even_tile_ref, chunk)],
                chunk,
            )
            turn(jnp.minimum(step + 2, late - 1), even_ref)
            added(head + step, even_tile_ref[0], even_tile_ref[1], 0)
            evaluate(
                odd_ref,
                [
                    into_table(cos_ref, sin_ref, step + 1, tile, chunk),
                    into_tile(odd_tile_ref, chunk),
                ],
                chunk,
            )

    rows = place(filled - 1, tile)
    added(head + filled - 1, cos_ref[rows, :], sin_ref[rows, :], 1)
    added(head + late - 1, odd_tile_ref[0], odd_tile_ref[1], 1)
    leave.wait()


def sum_kernel(parts_ref, out_ref):
    total = jnp.sum(parts_ref[...].astype(F32), axis=0, keepdims=True)
    out_ref[...] = jnp.broadcast_to(total, parts_ref.shape).astype(BF16)


def response_kernel(
    sums_ref, coef_ref, cos_head_ref, sin_head_ref, cos_ref, sin_ref, pot_ref, field_ref, *, tile
):
    share = sums_ref.shape[2]
    per = tile // share
    row = lax.broadcasted_iota(jnp.int32, (8, share), 0)
    lead = row % 4 == 0
    upper = row < 4
    totals = []
    segments = [(cos_head_ref, sin_head_ref, k) for k in range(0, cos_head_ref.shape[0], tile)]
    segments += [(cos_ref, sin_ref, k) for k in range(0, cos_ref.shape[0], tile)]
    for index, (cos_part, sin_part, start) in enumerate(segments):
        factors = ([], [])
        for q in range(index * per, (index + 1) * per):
            scaled = coef_ref[:, q * share : (q + 1) * share]
            sums = sums_ref[q].astype(F32)
            cosine = sums[0:1]
            sine = sums[1:2]
            for n, (top, other) in enumerate(((cosine, -sine), (sine, cosine))):
                full = scaled * jnp.where(lead, top, other)
                hi = full.astype(BF16).astype(F32)
                factors[n].append(jnp.where(upper, hi, full - hi))
        for n, ref in enumerate((cos_part, sin_part)):
            wide = jnp.concatenate(factors[n], axis=1).astype(BF16)
            totals.append(
                jnp.dot(wide, ref[start : start + tile, :], preferred_element_type=F32)
            )
    total = sum(totals[1:], totals[0])
    result = total[:4] + total[4:]
    pot_ref[...] = result[0:1]
    field_ref[...] = result[1:4]


def exchanged(x, start):
    devices = lax.axis_size(AXES)
    pairs = [(i, i + 1) for i in range(start, devices - 1, 2)]
    return lax.ppermute(x, AXES, pairs + [(j, i) for i, j in pairs])


def per_device(features, positions, neighbours, counts, w_in, w_out, w_charge, wave):
    own, channels = features.shape
    total = wave.shape[1]
    devices = lax.axis_size(AXES)
    half = own // 2
    width = channels + LANES
    share = total // devices
    factor = 4.0 / math.sqrt(own * devices * total)
    dma = pltpu.SemaphoreType.DMA
    w_charge = w_charge.reshape(1, channels)
    in_hbm = functools.partial(pltpu.with_memory_space_constraint, memory_space=pltpu.HBM)
    wave, w_in, w_out, w_charge = (in_hbm(x) for x in (wave, w_in, w_out, w_charge))

    edge = pltpu.VMEM((half, width), BF16)
    first, last, near, held, waves = pl.pallas_call(
        pack_kernel,
        out_shape=(edge,) * 3
        + (pltpu.VMEM(positions.shape, F32), pltpu.VMEM(wave.shape, F32)),
        in_specs=[HBM] * 5,
        out_specs=(VMEM,) * 5,
        scratch_shapes=[
            pltpu.VMEM(neighbours.shape[::-1], jnp.int32),
            pltpu.VMEM((1, own), jnp.int32),
            dma((6,)),
        ],
    )(*(in_hbm(x) for x in (features, positions, neighbours.T, counts.reshape(1, own))), wave)
    near = exchanged(near, 0)
    far, coef, hist = pl.pallas_call(
        functools.partial(prepare_kernel, tile=256, factor=factor),
        out_shape=(edge, pltpu.VMEM((8, total), F32), pltpu.VMEM((own, LANES), F32)),
        in_specs=[VMEM] * 3,
        out_specs=(VMEM,) * 3,
        compiler_params=pltpu.CompilerParams(vmem_limit_bytes=4 << 20),
        cost_estimate=pl.CostEstimate(
            flops=own * total * 4, bytes_accessed=own * total, transcendentals=0
        ),
    )(waves, first, last)
    far = exchanged(far, 1)

    tile, chunk = 256, 32
    early = (total - 8 * tile) // 2
    kept = pltpu.VMEM(w_in.shape, BF16)
    table = pltpu.VMEM((early, own), BF16)
    phases = [pltpu.VMEM((tile, own), F32)] * 2
    grant = pltpu.CompilerParams(vmem_limit_bytes=16 << 20)
    cos_head, sin_head, w_first, w_second, w_read = pl.pallas_call(
        functools.partial(early_kernel, tile=tile, chunk=chunk),
        out_shape=(
            table,
            table,
            kept,
            kept,
            pltpu.VMEM((1, channels), F32),
        ),
        in_specs=[VMEM] * 2 + [HBM] * 3,
        out_specs=(VMEM,) * 5,
        scratch_shapes=[pltpu.VMEM((32, own), BF16)] + phases + [dma((3,))],
        compiler_params=grant,
        cost_estimate=pl.CostEstimate(
            flops=own * early * 40, bytes_accessed=4 * own * early, transcendentals=0
        ),
    )(held, waves, w_in, w_out, w_charge)

    table = pltpu.VMEM((total - early, own), BF16)
    hidden, partial, cos_late, sin_late = pl.pallas_call(
        functools.partial(layer_kernel, tile=tile, chunk=chunk),
        out_shape=(
            jax.ShapeDtypeStruct((own, channels), BF16),
            jax.ShapeDtypeStruct((devices, 2, share), F32),
            table,
            table,
        ),
        in_specs=[VMEM] * 12,
        out_specs=(HBM,) + (VMEM,) * 3,
        scratch_shapes=[
            pltpu.VMEM((4 * half + HALO, channels), BF16),
            pltpu.VMEM((own + 3 * HALO, channels), BF16),
            pltpu.VMEM((own // HALO + 2, 2 * HALO, 2 * LANES), BF16),
            pltpu.VMEM((32, own), BF16),
            pltpu.VMEM((8, own), BF16),
        ]
        + phases
        + [pltpu.VMEM((2, tile, own), BF16)] * 2
        + [pltpu.VMEM((own, channels), BF16)]
        + [pltpu.VMEM((half, width), BF16)] * 2
        + [dma],
        compiler_params=grant,
    )(near, first, last, far, w_first, w_second, w_read, hist, held, waves, cos_head, sin_head)

    swapped = lax.all_to_all(partial.astype(BF16), AXES, 0, 0, tiled=True)
    spread = pl.pallas_call(
        sum_kernel,
        out_shape=jax.ShapeDtypeStruct((devices, 2, share), BF16),
        in_specs=[VMEM],
        out_specs=VMEM,
        compiler_params=pltpu.CompilerParams(vmem_limit_bytes=4 << 20),
    )(swapped)
    sums = lax.all_to_all(spread, AXES, 0, 0, tiled=True)

    tables = [
        pltpu.with_memory_space_constraint(x, pltpu.VMEM)
        for x in (cos_head, sin_head, cos_late, sin_late)
    ]
    potential, field = pl.pallas_call(
        functools.partial(response_kernel, tile=1024),
        out_shape=(
            jax.ShapeDtypeStruct((1, own), F32),
            jax.ShapeDtypeStruct((3, own), F32),
        ),
        in_specs=[VMEM] * 6,
        out_specs=(VMEM, VMEM),
        compiler_params=pltpu.CompilerParams(vmem_limit_bytes=4 << 20),
    )(sums, coef, *tables)
    return (hidden, potential.reshape(own), field)


def solution(mesh):
    placed = (
        P(AXES, None),
        P(None, AXES),
        P(AXES, None),
        P(AXES),
        P(),
        P(),
        P(),
        P(),
    )
    return jax.shard_map(
        per_device,
        mesh=mesh,
        in_specs=placed,
        out_specs=(P(AXES, None), P(AXES), P(None, AXES)),
        check_vma=False,
    )
```

```python
import functools
import math

import jax
import jax.numpy as jnp
from jax import lax
from jax.experimental import pallas as pl
from jax.experimental.pallas import tpu as pltpu
from jax.sharding import PartitionSpec as P

LAYERS = 2
HALO = 64
AXES = ("brick", "kvec")
LANES = 128
F32 = jnp.float32
BF16 = jnp.bfloat16

VMEM = pl.BlockSpec(memory_space=pltpu.VMEM)
HBM = pl.BlockSpec(memory_space=pltpu.HBM)


def pieces(x):
    first = x.astype(BF16).astype(F32)
    rest = x - first
    second = rest.astype(BF16).astype(F32)
    return first, second, rest - second


def even_device():
    index = lax.axis_index("brick") * lax.axis_size("kvec") + lax.axis_index("kvec")
    return index % 2 == 0


def chosen(even, one, other):
    return jnp.where(even, one.astype(F32), other.astype(F32)).astype(BF16)


def pack_kernel(
    feat_ref, pos_ref, neigh_ref, counts_ref, wave_ref, first_ref, last_ref, near_ref, far_ref,
    held_ref, waves_ref, slots_ref, used_ref, sems,
):
    slots, own = neigh_ref.shape
    channels = feat_ref.shape[1]
    half = own // 2
    copies = [
        pltpu.make_async_copy(source, target, sems.at[n])
        for n, (source, target) in enumerate(
            (
                (neigh_ref, slots_ref),
                (pos_ref, held_ref),
                (counts_ref, used_ref),
                (feat_ref.at[:half, :], first_ref.at[:, :channels]),
                (feat_ref.at[half:, :], last_ref.at[:, :channels]),
                (wave_ref, waves_ref),
            )
        )
    ]
    for copy in copies:
        copy.start()
    rows = lax.broadcasted_iota(jnp.int32, (slots, own), 1)
    slot = lax.broadcasted_iota(jnp.int32, (slots, own), 0)
    for copy in copies[:-1]:
        copy.wait()
    delta = (slots_ref[...] - HALO - rows).astype(F32)
    delta = jnp.where(slot < used_ref[...], delta, 0.0)
    zero5 = jnp.zeros((5, own), F32)
    coords = [jnp.concatenate([p, zero5], axis=0) for p in pieces(held_ref[...])]
    rest = jnp.zeros((LANES - slots - 24, own), F32)
    extra = jnp.concatenate([delta] + coords + [rest], axis=0).astype(BF16)
    first_ref[:, channels:] = extra[:, :half]
    last_ref[:, channels:] = extra[:, half:]
    even = even_device()
    near_ref[...] = chosen(even, last_ref[...], first_ref[...])
    far_ref[...] = chosen(even, first_ref[...], last_ref[...])
    copies[-1].wait()


HALF_SINE = (4.438831262995637, -7.228964613368321, 3.149392241482131)


def horner(s, coefs):
    value = coefs[-1] * s + coefs[-2]
    for c in coefs[-3::-1]:
        value = value * s + c
    return value


def atom_pieces(pos_ref):
    a, b, c = pieces(pos_ref[...])
    own = pos_ref.shape[1]
    left = jnp.concatenate([a, a, b, b, a, c, jnp.zeros((14, own), F32)], axis=0)
    return left.astype(BF16)


def place(step, tile):
    return pl.ds(pl.multiple_of(step * tile, tile), tile)


def phase(wave, left_ref, out_ref):
    tile = wave.shape[1]
    u, v, w = pieces(wave * (0.5 / math.pi))
    right = jnp.concatenate([u, v, u, v, w, u, jnp.zeros((14, tile), F32)], axis=0)
    out_ref[...] = jnp.dot(right.T.astype(BF16), left_ref[...], preferred_element_type=F32)


def evaluate(in_ref, stores, chunk):
    for start in range(0, in_ref.shape[0], chunk):
        t = in_ref[start : start + chunk, :]
        r = t - jnp.round(t)
        x = r * horner(r * r, HALF_SINE)
        square = x * x
        rest = 2.000002 - square
        cosine = (1.0 - square).astype(BF16)
        sine = (x * rest * lax.rsqrt(rest)).astype(BF16)
        for store in stores:
            store(start, cosine, sine)


def into_table(cos_ref, sin_ref, step, tile, chunk):
    def store(start, cosine, sine):
        rows = pl.ds(pl.multiple_of(step * tile + start, chunk), chunk)
        cos_ref[rows, :] = cosine
        sin_ref[rows, :] = sine

    return store


def into_tile(tile_ref, chunk):
    def store(start, cosine, sine):
        tile_ref[0, start : start + chunk, :] = cosine
        tile_ref[1, start : start + chunk, :] = sine

    return store


def histogram(delta):
    place = jnp.where(delta > 0, delta + 63.0, delta + 64.0)
    place = jnp.where(delta == 0, -1.0, place)
    deep = lax.broadcasted_iota(jnp.int32, (LANES, LANES), 0).astype(F32).astype(BF16)
    one = jnp.ones((LANES, LANES), BF16)
    zero = jnp.zeros((LANES, LANES), BF16)
    hist = zero
    for slot in range(64):
        row = jnp.broadcast_to(place[slot : slot + 1, :], (16, LANES)).astype(BF16)
        hist = hist + jnp.where(deep == jnp.concatenate([row] * 8, axis=0), one, zero)
    return hist.astype(F32).T


def early_kernel(
    pos_ref, wave_ref, first_ref, last_ref, w_in_ref, w_out_ref, w_charge_ref, cos_ref, sin_ref,
    coef_ref, hist_ref, w_in_out, w_out_out, w_charge_out, left_ref, even_ref, odd_ref, sems,
    *, tile, chunk, factor,
):
    copies = [
        pltpu.make_async_copy(source, target, sems.at[n])
        for n, (source, target) in enumerate(
            (
                (w_in_ref, w_in_out),
                (w_out_ref, w_out_out),
                (w_charge_ref, w_charge_out),
            )
        )
    ]
    for copy in copies:
        copy.start()
    left_ref[...] = atom_pieces(pos_ref)
    channels = w_in_ref.shape[1]
    for n, ref in enumerate((first_ref, last_ref)):
        hist_ref[n * LANES : (n + 1) * LANES, :] = histogram(ref[:64, channels:].astype(F32))
    head = cos_ref.shape[0] // tile
    group = 8

    def scale(step):
        waves = [wave_ref[:, place(step + n, tile)] for n in range(group)]
        ksq = jnp.zeros((group, tile), F32)
        for c in range(3):
            part = jnp.concatenate([w[c : c + 1] for w in waves], axis=0)
            ksq = ksq + part * part
        coef = factor * jnp.exp(-0.1 * ksq) / ksq
        one = jnp.ones((1, tile), F32)
        for n, w in enumerate(waves):
            coef_ref[:, place(step + n, tile)] = coef[n : n + 1] * jnp.concatenate(
                [one, w, one, w], axis=0
            )

    def turn(step, out_ref):
        phase(wave_ref[:, place(step, tile)], left_ref, out_ref)

    scale(0)
    turn(0, even_ref)

    @pl.loop(0, head // 4)
    def _(block):
        base = 4 * block
        scale(2 * base + group)
        for step in range(0, 4, 2):
            turn(base + step + 1, odd_ref)
            evaluate(even_ref, [into_table(cos_ref, sin_ref, base + step, tile, chunk)], chunk)
            turn(jnp.minimum(base + step + 2, head - 1), even_ref)
            evaluate(odd_ref, [into_table(cos_ref, sin_ref, base + step + 1, tile, chunk)], chunk)

    for copy in copies:
        copy.wait()


def silu(x):
    return x / (1.0 + jnp.exp(-x))


def layer_kernel(
    near_ref, first_ref, last_ref, far_ref, w_in_ref, w_out_ref, w_charge_ref, hist_ref,
    pos_ref, wave_ref, cos_head_ref, sin_head_ref, hidden_ref, sums_ref, cos_ref, sin_ref,
    feat_ref, mid_ref, matrix_ref, left_ref, charge_ref, even_ref, odd_ref, even_tile_ref,
    odd_tile_ref, final_ref, before_ref, after_ref, sem, *, tile, chunk,
):
    even = even_device()
    index = lax.axis_index("brick") * lax.axis_size("kvec") + lax.axis_index("kvec")
    last = lax.axis_size("brick") * lax.axis_size("kvec") - 1
    absent = jnp.zeros(far_ref.shape, BF16)
    far = chosen((index == 0) | (index == last), absent, far_ref[...])
    before_ref[...] = chosen(even, far, near_ref[...])
    after_ref[...] = chosen(even, near_ref[...], far)
    parts = (before_ref, first_ref, last_ref, after_ref)
    half = before_ref.shape[0]
    channels = w_in_ref.shape[1]
    own = 2 * half
    for n, ref in enumerate(parts):
        feat_ref[n * half : (n + 1) * half, :] = ref[:, :channels]
    feat_ref[4 * half :, :] = jnp.zeros((HALO, channels), BF16)
    extras = [ref[:, channels:].astype(F32) for ref in parts]
    rows = [e[64:72] + e[72:80] + e[80:88] for e in extras]
    ext_rows = jnp.concatenate(rows + [jnp.zeros((8, LANES), F32)], axis=1)
    ext_cols = jnp.concatenate([r.T for r in rows], axis=0)
    lane = lax.broadcasted_iota(jnp.int32, (HALO, LANES), 1)
    ends = histogram(jnp.where(lane < HALO, extras[3][:64], extras[0][:64]))
    inner = [hist_ref[n * HALO : (n + 1) * HALO, :] for n in range(own // HALO)]
    hist_all = [ends[HALO:]] + inner + [ends[:HALO]]
    blocks = (own + 2 * HALO) // HALO
    zeros = jnp.zeros((HALO, LANES), F32)
    for block in range(blocks):
        base = HALO * (block + 1)
        hist = hist_all[block]
        low = jnp.concatenate([jnp.where(lane < 64, hist, 0.0), zeros], axis=1)
        high = jnp.concatenate([jnp.where(lane < 64, 0.0, hist), zeros], axis=1)
        counted = pltpu.roll(low, 0, 1, stride=1, stride_axis=0) + pltpu.roll(
            high, 1, 1, stride=1, stride_axis=0
        )
        dist = jnp.zeros((HALO, 2 * LANES), F32)
        for c in range(3):
            there = ext_rows[c : c + 1, HALO * block : HALO * block + 2 * LANES]
            diff = there - ext_cols[base : base + HALO, c : c + 1]
            dist = dist + diff * diff
        weight = counted / (1.0 + dist)
        upper = weight.astype(BF16)
        lower = (weight - upper.astype(F32)).astype(BF16)
        matrix_ref[block, :HALO, :] = upper
        matrix_ref[block, HALO:, :] = lower

    left_ref[...] = atom_pieces(pos_ref)
    head = cos_head_ref.shape[0] // tile
    late = cos_ref.shape[0] // tile
    filled = 8
    slots = (even_ref, odd_ref)

    def turn(step, out_ref):
        phase(wave_ref[:, place(head + step, tile)], left_ref, out_ref)

    def filler(step):
        turn(step + 1, slots[(step + 1) % 2])
        evaluate(
            slots[step % 2], [into_table(cos_ref, sin_ref, step, tile, chunk)], chunk
        )

    turn(0, even_ref)

    def advance(source_ref, layer, block_ids, row0, residual):
        messages = []
        for block in block_ids:
            start = HALO * (block - row0)
            out = jnp.dot(
                matrix_ref[block],
                source_ref[start : start + 2 * LANES, :],
                preferred_element_type=F32,
            )
            messages.append(out[:HALO] + out[HALO:])
        filler(4 * layer)
        message = jnp.concatenate(messages, axis=0)
        scale = lax.rsqrt(jnp.mean(message * message, axis=-1, keepdims=True) + 1e-05)
        filler(4 * layer + 1)
        normed = (message * scale).astype(BF16)
        inner = jnp.dot(normed, w_in_ref[layer], preferred_element_type=F32)
        filler(4 * layer + 2)
        inner = silu(inner).astype(BF16)
        update = jnp.dot(inner, w_out_ref[layer], preferred_element_type=F32)
        filler(4 * layer + 3)
        return (residual.astype(F32) + update).astype(BF16)

    grown = own + 2 * HALO
    mid_ref[:grown, :] = advance(
        feat_ref, 0, range(blocks), 0, feat_ref[HALO : HALO + grown, :]
    )
    mid_ref[grown:, :] = jnp.zeros((HALO, channels), BF16)
    final = advance(mid_ref, 1, range(1, blocks - 1), 1, mid_ref[HALO : HALO + own, :])
    final_ref[...] = final
    leave = pltpu.make_async_copy(final_ref, hidden_ref, sem)
    leave.start()
    reader = jnp.concatenate(
        list(pieces(w_charge_ref[...])) + [jnp.zeros((5, channels), F32)], axis=0
    ).astype(BF16)
    read = lax.dot_general(
        reader, final, (((1,), (1,)), ((), ())), preferred_element_type=F32
    )
    charge = read[0:1] + read[1:2] + read[2:3]
    hi, mid, lo = pieces(charge)
    charges = jnp.concatenate([hi, mid, lo, jnp.zeros((5, own), F32)], axis=0).astype(BF16)

    charge_ref[...] = charges
    share = sums_ref.shape[2]
    per = 2 * tile // share
    dims = (((1,), (1,)), ((), ()))

    def added(step, cos_tile, sin_tile, odd):
        rows = []
        for table in (cos_tile, sin_tile):
            part = lax.dot_general(charge_ref[...], table, dims, preferred_element_type=F32)
            rows.append(part[0:1] + part[1:2] + part[2:3])
        index = (step - odd) // 2 * per + odd * (per - 1)
        lanes = odd * (2 - per) * tile
        sums_ref[index, :, lanes : lanes + tile] = jnp.concatenate(rows, axis=0)

    for step in range(filled - 1):
        rows = place(step, tile)
        added(head + step, cos_ref[rows, :], sin_ref[rows, :], step % 2)

    @pl.loop(0, (late - filled) // 4)
    def _(block):
        for pair in range(2):
            early = 4 * block + 2 * pair
            step = early + filled
            for n in range(2):
                rows = place(early + n, tile)
                added(early + n, cos_head_ref[rows, :], sin_head_ref[rows, :], n)
            turn(step + 1, odd_ref)
            added(head + step - 1, odd_tile_ref[0], odd_tile_ref[1], 1)
            evaluate(
                even_ref,
                [into_table(cos_ref, sin_ref, step, tile, chunk), into_tile(even_tile_ref, chunk)],
                chunk,
            )
            turn(jnp.minimum(step + 2, late - 1), even_ref)
            added(head + step, even_tile_ref[0], even_tile_ref[1], 0)
            evaluate(
                odd_ref,
                [
                    into_table(cos_ref, sin_ref, step + 1, tile, chunk),
                    into_tile(odd_tile_ref, chunk),
                ],
                chunk,
            )

    rows = place(filled - 1, tile)
    added(head + filled - 1, cos_ref[rows, :], sin_ref[rows, :], 1)
    added(head + late - 1, odd_tile_ref[0], odd_tile_ref[1], 1)
    leave.wait()


def sum_kernel(parts_ref, out_ref):
    total = jnp.sum(parts_ref[...].astype(F32), axis=0, keepdims=True)
    out_ref[...] = jnp.broadcast_to(total, parts_ref.shape).astype(BF16)


def response_kernel(
    sums_ref, coef_ref, cos_head_ref, sin_head_ref, cos_ref, sin_ref, pot_ref, field_ref, *, tile
):
    share = sums_ref.shape[2]
    per = tile // share
    row = lax.broadcasted_iota(jnp.int32, (8, share), 0)
    lead = row % 4 == 0
    upper = row < 4
    totals = []
    segments = [(cos_head_ref, sin_head_ref, k) for k in range(0, cos_head_ref.shape[0], tile)]
    segments += [(cos_ref, sin_ref, k) for k in range(0, cos_ref.shape[0], tile)]
    for index, (cos_part, sin_part, start) in enumerate(segments):
        factors = ([], [])
        for q in range(index * per, (index + 1) * per):
            scaled = coef_ref[:, q * share : (q + 1) * share]
            sums = sums_ref[q].astype(F32)
            cosine = sums[0:1]
            sine = sums[1:2]
            for n, (top, other) in enumerate(((cosine, -sine), (sine, cosine))):
                full = scaled * jnp.where(lead, top, other)
                hi = full.astype(BF16).astype(F32)
                factors[n].append(jnp.where(upper, hi, full - hi))
        for n, ref in enumerate((cos_part, sin_part)):
            wide = jnp.concatenate(factors[n], axis=1).astype(BF16)
            totals.append(
                jnp.dot(wide, ref[start : start + tile, :], preferred_element_type=F32)
            )
    total = sum(totals[1:], totals[0])
    result = total[:4] + total[4:]
    pot_ref[...] = result[0:1]
    field_ref[...] = result[1:4]


def exchanged(x, start):
    devices = lax.axis_size(AXES)
    pairs = [(i, (i + 1) % devices) for i in range(start, devices, 2)]
    return lax.ppermute(x, AXES, pairs + [(j, i) for i, j in pairs])


def per_device(features, positions, neighbours, counts, w_in, w_out, w_charge, wave):
    own, channels = features.shape
    total = wave.shape[1]
    devices = lax.axis_size(AXES)
    half = own // 2
    width = channels + LANES
    share = total // devices
    factor = 4.0 / math.sqrt(own * devices * total)
    dma = pltpu.SemaphoreType.DMA
    w_charge = w_charge.reshape(1, channels)
    in_hbm = functools.partial(pltpu.with_memory_space_constraint, memory_space=pltpu.HBM)
    wave, w_in, w_out, w_charge = (in_hbm(x) for x in (wave, w_in, w_out, w_charge))

    edge = pltpu.VMEM((half, width), BF16)
    first, last, near, far, held, waves = pl.pallas_call(
        pack_kernel,
        out_shape=(edge,) * 4
        + (pltpu.VMEM(positions.shape, F32), pltpu.VMEM(wave.shape, F32)),
        in_specs=[HBM] * 5,
        out_specs=(VMEM,) * 6,
        scratch_shapes=[
            pltpu.VMEM(neighbours.shape[::-1], jnp.int32),
            pltpu.VMEM((1, own), jnp.int32),
            dma((6,)),
        ],
    )(*(in_hbm(x) for x in (features, positions, neighbours.T, counts.reshape(1, own))), wave)
    near = exchanged(near, 0)
    far = exchanged(far, 1)

    tile, chunk = 256, 32
    early = (total - 8 * tile) // 2
    kept = pltpu.VMEM(w_in.shape, BF16)
    table = pltpu.VMEM((early, own), BF16)
    phases = [pltpu.VMEM((tile, own), F32)] * 2
    grant = pltpu.CompilerParams(vmem_limit_bytes=16 << 20)
    cos_head, sin_head, coef, hist, w_first, w_second, w_read = pl.pallas_call(
        functools.partial(early_kernel, tile=tile, chunk=chunk, factor=factor),
        out_shape=(
            table,
            table,
            pltpu.VMEM((8, total), F32),
            pltpu.VMEM((own, LANES), F32),
            kept,
            kept,
            pltpu.VMEM((1, channels), F32),
        ),
        in_specs=[VMEM] * 4 + [HBM] * 3,
        out_specs=(VMEM,) * 7,
        scratch_shapes=[pltpu.VMEM((32, own), BF16)] + phases + [dma((3,))],
        compiler_params=grant,
        cost_estimate=pl.CostEstimate(
            flops=own * early * 40, bytes_accessed=4 * own * early, transcendentals=0
        ),
    )(held, waves, first, last, w_in, w_out, w_charge)

    table = pltpu.VMEM((total - early, own), BF16)
    hidden, partial, cos_late, sin_late = pl.pallas_call(
        functools.partial(layer_kernel, tile=tile, chunk=chunk),
        out_shape=(
            jax.ShapeDtypeStruct((own, channels), BF16),
            jax.ShapeDtypeStruct((devices, 2, share), F32),
            table,
            table,
        ),
        in_specs=[VMEM] * 12,
        out_specs=(HBM,) + (VMEM,) * 3,
        scratch_shapes=[
            pltpu.VMEM((4 * half + HALO, channels), BF16),
            pltpu.VMEM((own + 3 * HALO, channels), BF16),
            pltpu.VMEM((own // HALO + 2, 2 * HALO, 2 * LANES), BF16),
            pltpu.VMEM((32, own), BF16),
            pltpu.VMEM((8, own), BF16),
        ]
        + phases
        + [pltpu.VMEM((2, tile, own), BF16)] * 2
        + [pltpu.VMEM((own, channels), BF16)]
        + [pltpu.VMEM((half, width), BF16)] * 2
        + [dma],
        compiler_params=grant,
    )(near, first, last, far, w_first, w_second, w_read, hist, held, waves, cos_head, sin_head)

    swapped = lax.all_to_all(partial.astype(BF16), AXES, 0, 0, tiled=True)
    spread = pl.pallas_call(
        sum_kernel,
        out_shape=jax.ShapeDtypeStruct((devices, 2, share), BF16),
        in_specs=[VMEM],
        out_specs=VMEM,
        compiler_params=pltpu.CompilerParams(vmem_limit_bytes=4 << 20),
    )(swapped)
    sums = lax.all_to_all(spread, AXES, 0, 0, tiled=True)

    tables = [
        pltpu.with_memory_space_constraint(x, pltpu.VMEM)
        for x in (cos_head, sin_head, cos_late, sin_late)
    ]
    potential, field = pl.pallas_call(
        functools.partial(response_kernel, tile=1024),
        out_shape=(
            jax.ShapeDtypeStruct((1, own), F32),
            jax.ShapeDtypeStruct((3, own), F32),
        ),
        in_specs=[VMEM] * 6,
        out_specs=(VMEM, VMEM),
        compiler_params=pltpu.CompilerParams(vmem_limit_bytes=4 << 20),
    )(sums, coef, *tables)
    return (hidden, potential.reshape(own), field)


def solution(mesh):
    placed = (
        P(AXES, None),
        P(None, AXES),
        P(AXES, None),
        P(AXES),
        P(),
        P(),
        P(),
        P(),
    )
    return jax.shard_map(
        per_device,
        mesh=mesh,
        in_specs=placed,
        out_specs=(P(AXES, None), P(AXES), P(None, AXES)),
        check_vma=False,
    )
```

```python
import functools
import math

import jax
import jax.numpy as jnp
from jax import lax
from jax.experimental import pallas as pl
from jax.experimental.pallas import tpu as pltpu
from jax.sharding import PartitionSpec as P

LAYERS = 2
HALO = 64
AXES = ("brick", "kvec")
LANES = 128
F32 = jnp.float32
BF16 = jnp.bfloat16

VMEM = pl.BlockSpec(memory_space=pltpu.VMEM)
HBM = pl.BlockSpec(memory_space=pltpu.HBM)


def pieces(x):
    first = x.astype(BF16).astype(F32)
    rest = x - first
    second = rest.astype(BF16).astype(F32)
    return first, second, rest - second


def even_device():
    index = lax.axis_index("brick") * lax.axis_size("kvec") + lax.axis_index("kvec")
    return index % 2 == 0


def chosen(even, one, other):
    return jnp.where(even, one.astype(F32), other.astype(F32)).astype(BF16)


def pack_kernel(
    feat_ref, pos_ref, neigh_ref, counts_ref, wave_ref, first_ref, last_ref, near_ref, far_ref,
    held_ref, waves_ref, slots_ref, used_ref, sems,
):
    slots, own = neigh_ref.shape
    channels = feat_ref.shape[1]
    half = own // 2
    copies = [
        pltpu.make_async_copy(source, target, sems.at[n])
        for n, (source, target) in enumerate(
            (
                (neigh_ref, slots_ref),
                (pos_ref, held_ref),
                (counts_ref, used_ref),
                (feat_ref.at[:half, :], first_ref.at[:, :channels]),
                (feat_ref.at[half:, :], last_ref.at[:, :channels]),
                (wave_ref, waves_ref),
            )
        )
    ]
    for copy in copies:
        copy.start()
    rows = lax.broadcasted_iota(jnp.int32, (slots, own), 1)
    slot = lax.broadcasted_iota(jnp.int32, (slots, own), 0)
    for copy in copies[:-1]:
        copy.wait()
    delta = (slots_ref[...] - HALO - rows).astype(F32)
    delta = jnp.where(slot < used_ref[...], delta, 0.0)
    zero5 = jnp.zeros((5, own), F32)
    coords = [jnp.concatenate([p, zero5], axis=0) for p in pieces(held_ref[...])]
    rest = jnp.zeros((LANES - slots - 24, own), F32)
    extra = jnp.concatenate([delta] + coords + [rest], axis=0).astype(BF16)
    first_ref[:, channels:] = extra[:, :half]
    last_ref[:, channels:] = extra[:, half:]
    even = even_device()
    near_ref[...] = chosen(even, last_ref[...], first_ref[...])
    far_ref[...] = chosen(even, first_ref[...], last_ref[...])
    copies[-1].wait()


HALF_SINE = (4.438831262995637, -7.228964613368321, 3.149392241482131)


def horner(s, coefs):
    value = coefs[-1] * s + coefs[-2]
    for c in coefs[-3::-1]:
        value = value * s + c
    return value


def atom_pieces(pos_ref):
    a, b, c = pieces(pos_ref[...])
    own = pos_ref.shape[1]
    left = jnp.concatenate([a, a, b, b, a, c, jnp.zeros((14, own), F32)], axis=0)
    return left.astype(BF16)


def place(step, tile):
    return pl.ds(pl.multiple_of(step * tile, tile), tile)


def phase(wave, left_ref, out_ref):
    tile = wave.shape[1]
    u, v, w = pieces(wave * (0.5 / math.pi))
    right = jnp.concatenate([u, v, u, v, w, u, jnp.zeros((14, tile), F32)], axis=0)
    out_ref[...] = jnp.dot(right.T.astype(BF16), left_ref[...], preferred_element_type=F32)


def evaluate(in_ref, stores, chunk):
    for start in range(0, in_ref.shape[0], chunk):
        t = in_ref[start : start + chunk, :]
        r = t - jnp.round(t)
        x = r * horner(r * r, HALF_SINE)
        square = x * x
        rest = 2.000002 - square
        cosine = (1.0 - square).astype(BF16)
        sine = (x * rest * lax.rsqrt(rest)).astype(BF16)
        for store in stores:
            store(start, cosine, sine)


def into_table(cos_ref, sin_ref, step, tile, chunk):
    def store(start, cosine, sine):
        rows = pl.ds(pl.multiple_of(step * tile + start, chunk), chunk)
        cos_ref[rows, :] = cosine
        sin_ref[rows, :] = sine

    return store


def into_tile(tile_ref, chunk):
    def store(start, cosine, sine):
        tile_ref[0, start : start + chunk, :] = cosine
        tile_ref[1, start : start + chunk, :] = sine

    return store


def histogram(delta):
    place = jnp.where(delta > 0, delta + 63.0, delta + 64.0)
    place = jnp.where(delta == 0, -1.0, place)
    deep = lax.broadcasted_iota(jnp.int32, (LANES, LANES), 0).astype(F32).astype(BF16)
    one = jnp.ones((LANES, LANES), BF16)
    zero = jnp.zeros((LANES, LANES), BF16)
    hist = zero
    for slot in range(64):
        row = jnp.broadcast_to(place[slot : slot + 1, :], (16, LANES)).astype(BF16)
        hist = hist + jnp.where(deep == jnp.concatenate([row] * 8, axis=0), one, zero)
    return hist.astype(F32).T


def early_kernel(
    pos_ref, wave_ref, first_ref, last_ref, w_in_ref, w_out_ref, w_charge_ref, cos_ref, sin_ref,
    coef_ref, hist_ref, w_in_out, w_out_out, w_charge_out, left_ref, even_ref, odd_ref, sems,
    *, tile, chunk, factor,
):
    copies = [
        pltpu.make_async_copy(source, target, sems.at[n])
        for n, (source, target) in enumerate(
            (
                (w_in_ref, w_in_out),
                (w_out_ref, w_out_out),
                (w_charge_ref, w_charge_out),
            )
        )
    ]
    for copy in copies:
        copy.start()
    left_ref[...] = atom_pieces(pos_ref)
    channels = w_in_ref.shape[1]
    for n, ref in enumerate((first_ref, last_ref)):
        hist_ref[n * LANES : (n + 1) * LANES, :] = histogram(ref[:64, channels:].astype(F32))
    head = cos_ref.shape[0] // tile
    group = 8

    def scale(step):
        waves = [wave_ref[:, place(step + n, tile)] for n in range(group)]
        ksq = jnp.zeros((group, tile), F32)
        for c in range(3):
            part = jnp.concatenate([w[c : c + 1] for w in waves], axis=0)
            ksq = ksq + part * part
        coef = factor * jnp.exp(-0.1 * ksq) / ksq
        one = jnp.ones((1, tile), F32)
        for n, w in enumerate(waves):
            coef_ref[:, place(step + n, tile)] = coef[n : n + 1] * jnp.concatenate(
                [one, w, one, w], axis=0
            )

    def turn(step, out_ref):
        phase(wave_ref[:, place(step, tile)], left_ref, out_ref)

    scale(0)
    turn(0, even_ref)

    @pl.loop(0, head // 4)
    def _(block):
        base = 4 * block
        scale(2 * base + group)
        for step in range(0, 4, 2):
            turn(base + step + 1, odd_ref)
            evaluate(even_ref, [into_table(cos_ref, sin_ref, base + step, tile, chunk)], chunk)
            turn(jnp.minimum(base + step + 2, head - 1), even_ref)
            evaluate(odd_ref, [into_table(cos_ref, sin_ref, base + step + 1, tile, chunk)], chunk)

    for copy in copies:
        copy.wait()


def silu(x):
    return x / (1.0 + jnp.exp(-x))


def layer_kernel(
    near_ref, first_ref, last_ref, far_ref, w_in_ref, w_out_ref, w_charge_ref, hist_ref,
    pos_ref, wave_ref, cos_head_ref, sin_head_ref, hidden_ref, sums_ref, cos_ref, sin_ref,
    feat_ref, mid_ref, matrix_ref, left_ref, charge_ref, even_ref, odd_ref, even_tile_ref,
    odd_tile_ref, final_ref, before_ref, after_ref, sem, *, tile, chunk,
):
    even = even_device()
    index = lax.axis_index("brick") * lax.axis_size("kvec") + lax.axis_index("kvec")
    last = lax.axis_size("brick") * lax.axis_size("kvec") - 1
    absent = jnp.zeros(far_ref.shape, BF16)
    far = chosen((index == 0) | (index == last), absent, far_ref[...])
    before_ref[...] = chosen(even, far, near_ref[...])
    after_ref[...] = chosen(even, near_ref[...], far)
    parts = (before_ref, first_ref, last_ref, after_ref)
    half = before_ref.shape[0]
    channels = w_in_ref.shape[1]
    own = 2 * half
    for n, ref in enumerate(parts):
        feat_ref[n * half : (n + 1) * half, :] = ref[:, :channels]
    feat_ref[4 * half :, :] = jnp.zeros((HALO, channels), BF16)
    extras = [ref[:, channels:].astype(F32) for ref in parts]
    rows = [e[64:72] + e[72:80] + e[80:88] for e in extras]
    ext_rows = jnp.concatenate(rows + [jnp.zeros((8, LANES), F32)], axis=1)
    ext_cols = jnp.concatenate([r.T for r in rows], axis=0)
    lane = lax.broadcasted_iota(jnp.int32, (HALO, LANES), 1)
    ends = histogram(jnp.where(lane < HALO, extras[3][:64], extras[0][:64]))
    inner = [hist_ref[n * HALO : (n + 1) * HALO, :] for n in range(own // HALO)]
    hist_all = [ends[HALO:]] + inner + [ends[:HALO]]
    blocks = (own + 2 * HALO) // HALO
    zeros = jnp.zeros((HALO, LANES), F32)
    for block in range(blocks):
        base = HALO * (block + 1)
        hist = hist_all[block]
        low = jnp.concatenate([jnp.where(lane < 64, hist, 0.0), zeros], axis=1)
        high = jnp.concatenate([jnp.where(lane < 64, 0.0, hist), zeros], axis=1)
        counted = pltpu.roll(low, 0, 1, stride=1, stride_axis=0) + pltpu.roll(
            high, 1, 1, stride=1, stride_axis=0
        )
        dist = jnp.zeros((HALO, 2 * LANES), F32)
        for c in range(3):
            there = ext_rows[c : c + 1, HALO * block : HALO * block + 2 * LANES]
            diff = there - ext_cols[base : base + HALO, c : c + 1]
            dist = dist + diff * diff
        weight = counted / (1.0 + dist)
        upper = weight.astype(BF16)
        lower = (weight - upper.astype(F32)).astype(BF16)
        matrix_ref[block, :HALO, :] = upper
        matrix_ref[block, HALO:, :] = lower

    left_ref[...] = atom_pieces(pos_ref)
    head = cos_head_ref.shape[0] // tile
    late = cos_ref.shape[0] // tile
    filled = 8
    slots = (even_ref, odd_ref)

    def turn(step, out_ref):
        phase(wave_ref[:, place(head + step, tile)], left_ref, out_ref)

    def filler(step):
        turn(step + 1, slots[(step + 1) % 2])
        evaluate(
            slots[step % 2], [into_table(cos_ref, sin_ref, step, tile, chunk)], chunk
        )

    turn(0, even_ref)

    def advance(source_ref, layer, block_ids, row0, residual):
        messages = []
        for block in block_ids:
            start = HALO * (block - row0)
            out = jnp.dot(
                matrix_ref[block],
                source_ref[start : start + 2 * LANES, :],
                preferred_element_type=F32,
            )
            messages.append(out[:HALO] + out[HALO:])
        filler(4 * layer)
        message = jnp.concatenate(messages, axis=0)
        scale = lax.rsqrt(jnp.mean(message * message, axis=-1, keepdims=True) + 1e-05)
        filler(4 * layer + 1)
        normed = (message * scale).astype(BF16)
        inner = jnp.dot(normed, w_in_ref[layer], preferred_element_type=F32)
        filler(4 * layer + 2)
        inner = silu(inner).astype(BF16)
        update = jnp.dot(inner, w_out_ref[layer], preferred_element_type=F32)
        filler(4 * layer + 3)
        return (residual.astype(F32) + update).astype(BF16)

    grown = own + 2 * HALO
    mid_ref[:grown, :] = advance(
        feat_ref, 0, range(blocks), 0, feat_ref[HALO : HALO + grown, :]
    )
    mid_ref[grown:, :] = jnp.zeros((HALO, channels), BF16)
    final = advance(mid_ref, 1, range(1, blocks - 1), 1, mid_ref[HALO : HALO + own, :])
    final_ref[...] = final
    leave = pltpu.make_async_copy(final_ref, hidden_ref, sem)
    leave.start()
    reader = jnp.concatenate(
        list(pieces(w_charge_ref[...])) + [jnp.zeros((5, channels), F32)], axis=0
    ).astype(BF16)
    read = lax.dot_general(
        reader, final, (((1,), (1,)), ((), ())), preferred_element_type=F32
    )
    charge = read[0:1] + read[1:2] + read[2:3]
    hi, mid, lo = pieces(charge)
    charges = jnp.concatenate([hi, mid, lo, jnp.zeros((5, own), F32)], axis=0).astype(BF16)

    charge_ref[...] = charges
    share = sums_ref.shape[2]
    per = 2 * tile // share
    dims = (((1,), (1,)), ((), ()))

    def added(step, cos_tile, sin_tile, odd):
        rows = []
        for table in (cos_tile, sin_tile):
            part = lax.dot_general(charge_ref[...], table, dims, preferred_element_type=F32)
            rows.append(part[0:1] + part[1:2] + part[2:3])
        index = (step - odd) // 2 * per + odd * (per - 1)
        lanes = odd * (2 - per) * tile
        sums_ref[index, :, lanes : lanes + tile] = jnp.concatenate(rows, axis=0)

    for step in range(filled - 1):
        rows = place(step, tile)
        added(head + step, cos_ref[rows, :], sin_ref[rows, :], step % 2)

    @pl.loop(0, (late - filled) // 4)
    def _(block):
        for pair in range(2):
            early = 4 * block + 2 * pair
            step = early + filled
            for n in range(2):
                rows = place(early + n, tile)
                added(early + n, cos_head_ref[rows, :], sin_head_ref[rows, :], n)
            turn(step + 1, odd_ref)
            added(head + step - 1, odd_tile_ref[0], odd_tile_ref[1], 1)
            evaluate(
                even_ref,
                [into_table(cos_ref, sin_ref, step, tile, chunk), into_tile(even_tile_ref, chunk)],
                chunk,
            )
            turn(jnp.minimum(step + 2, late - 1), even_ref)
            added(head + step, even_tile_ref[0], even_tile_ref[1], 0)
            evaluate(
                odd_ref,
                [
                    into_table(cos_ref, sin_ref, step + 1, tile, chunk),
                    into_tile(odd_tile_ref, chunk),
                ],
                chunk,
            )

    rows = place(filled - 1, tile)
    added(head + filled - 1, cos_ref[rows, :], sin_ref[rows, :], 1)
    added(head + late - 1, odd_tile_ref[0], odd_tile_ref[1], 1)
    leave.wait()


def sum_kernel(parts_ref, out_ref):
    total = jnp.sum(parts_ref[...].astype(F32), axis=0, keepdims=True)
    out_ref[...] = jnp.broadcast_to(total, parts_ref.shape).astype(BF16)


def response_kernel(
    sums_ref, coef_ref, cos_head_ref, sin_head_ref, cos_ref, sin_ref, pot_ref, field_ref, *, tile
):
    share = sums_ref.shape[2]
    per = tile // share
    row = lax.broadcasted_iota(jnp.int32, (8, share), 0)
    lead = row % 4 == 0
    upper = row < 4
    totals = []
    segments = [(cos_head_ref, sin_head_ref, k) for k in range(0, cos_head_ref.shape[0], tile)]
    segments += [(cos_ref, sin_ref, k) for k in range(0, cos_ref.shape[0], tile)]
    for index, (cos_part, sin_part, start) in enumerate(segments):
        factors = ([], [])
        for q in range(index * per, (index + 1) * per):
            scaled = coef_ref[:, q * share : (q + 1) * share]
            sums = sums_ref[q].astype(F32)
            cosine = sums[0:1]
            sine = sums[1:2]
            for n, (top, other) in enumerate(((cosine, -sine), (sine, cosine))):
                full = scaled * jnp.where(lead, top, other)
                hi = full.astype(BF16).astype(F32)
                factors[n].append(jnp.where(upper, hi, full - hi))
        for n, ref in enumerate((cos_part, sin_part)):
            wide = jnp.concatenate(factors[n], axis=1).astype(BF16)
            totals.append(
                jnp.dot(wide, ref[start : start + tile, :], preferred_element_type=F32)
            )
    total = sum(totals[1:], totals[0])
    result = total[:4] + total[4:]
    pot_ref[...] = result[0:1]
    field_ref[...] = result[1:4]


def exchanged(x, start):
    devices = lax.axis_size(AXES)
    pairs = [(i, (i + 1) % devices) for i in range(start, devices, 2)]
    return lax.ppermute(x, AXES, pairs + [(j, i) for i, j in pairs])


def per_device(features, positions, neighbours, counts, w_in, w_out, w_charge, wave):
    own, channels = features.shape
    total = wave.shape[1]
    devices = lax.axis_size(AXES)
    half = own // 2
    width = channels + LANES
    share = total // devices
    factor = 4.0 / math.sqrt(own * devices * total)
    dma = pltpu.SemaphoreType.DMA
    w_charge = w_charge.reshape(1, channels)
    in_hbm = functools.partial(pltpu.with_memory_space_constraint, memory_space=pltpu.HBM)
    wave, w_in, w_out, w_charge = (in_hbm(x) for x in (wave, w_in, w_out, w_charge))

    edge = pltpu.VMEM((half, width), BF16)
    first, last, near, far, held, waves = pl.pallas_call(
        pack_kernel,
        out_shape=(edge,) * 4
        + (pltpu.VMEM(positions.shape, F32), pltpu.VMEM(wave.shape, F32)),
        in_specs=[HBM] * 5,
        out_specs=(VMEM,) * 6,
        scratch_shapes=[
            pltpu.VMEM(neighbours.shape[::-1], jnp.int32),
            pltpu.VMEM((1, own), jnp.int32),
            dma((6,)),
        ],
    )(*(in_hbm(x) for x in (features, positions, neighbours.T, counts.reshape(1, own))), wave)
    far = exchanged(far, 1)
    near = exchanged(near, 0)

    tile, chunk = 256, 32
    early = (total - 8 * tile) // 2
    kept = pltpu.VMEM(w_in.shape, BF16)
    table = pltpu.VMEM((early, own), BF16)
    phases = [pltpu.VMEM((tile, own), F32)] * 2
    grant = pltpu.CompilerParams(vmem_limit_bytes=16 << 20)
    cos_head, sin_head, coef, hist, w_first, w_second, w_read = pl.pallas_call(
        functools.partial(early_kernel, tile=tile, chunk=chunk, factor=factor),
        out_shape=(
            table,
            table,
            pltpu.VMEM((8, total), F32),
            pltpu.VMEM((own, LANES), F32),
            kept,
            kept,
            pltpu.VMEM((1, channels), F32),
        ),
        in_specs=[VMEM] * 4 + [HBM] * 3,
        out_specs=(VMEM,) * 7,
        scratch_shapes=[pltpu.VMEM((32, own), BF16)] + phases + [dma((3,))],
        compiler_params=grant,
        cost_estimate=pl.CostEstimate(
            flops=own * early * 40, bytes_accessed=4 * own * early, transcendentals=0
        ),
    )(held, waves, first, last, w_in, w_out, w_charge)

    table = pltpu.VMEM((total - early, own), BF16)
    hidden, partial, cos_late, sin_late = pl.pallas_call(
        functools.partial(layer_kernel, tile=tile, chunk=chunk),
        out_shape=(
            jax.ShapeDtypeStruct((own, channels), BF16),
            jax.ShapeDtypeStruct((devices, 2, share), F32),
            table,
            table,
        ),
        in_specs=[VMEM] * 12,
        out_specs=(HBM,) + (VMEM,) * 3,
        scratch_shapes=[
            pltpu.VMEM((4 * half + HALO, channels), BF16),
            pltpu.VMEM((own + 3 * HALO, channels), BF16),
            pltpu.VMEM((own // HALO + 2, 2 * HALO, 2 * LANES), BF16),
            pltpu.VMEM((32, own), BF16),
            pltpu.VMEM((8, own), BF16),
        ]
        + phases
        + [pltpu.VMEM((2, tile, own), BF16)] * 2
        + [pltpu.VMEM((own, channels), BF16)]
        + [pltpu.VMEM((half, width), BF16)] * 2
        + [dma],
        compiler_params=grant,
    )(near, first, last, far, w_first, w_second, w_read, hist, held, waves, cos_head, sin_head)

    swapped = lax.all_to_all(partial.astype(BF16), AXES, 0, 0, tiled=True)
    spread = pl.pallas_call(
        sum_kernel,
        out_shape=jax.ShapeDtypeStruct((devices, 2, share), BF16),
        in_specs=[VMEM],
        out_specs=VMEM,
        compiler_params=pltpu.CompilerParams(vmem_limit_bytes=4 << 20),
    )(swapped)
    sums = lax.all_to_all(spread, AXES, 0, 0, tiled=True)

    tables = [
        pltpu.with_memory_space_constraint(x, pltpu.VMEM)
        for x in (cos_head, sin_head, cos_late, sin_late)
    ]
    potential, field = pl.pallas_call(
        functools.partial(response_kernel, tile=1024),
        out_shape=(
            jax.ShapeDtypeStruct((1, own), F32),
            jax.ShapeDtypeStruct((3, own), F32),
        ),
        in_specs=[VMEM] * 6,
        out_specs=(VMEM, VMEM),
        compiler_params=pltpu.CompilerParams(vmem_limit_bytes=4 << 20),
    )(sums, coef, *tables)
    return (hidden, potential.reshape(own), field)


def solution(mesh):
    placed = (
        P(AXES, None),
        P(None, AXES),
        P(AXES, None),
        P(AXES),
        P(),
        P(),
        P(),
        P(),
    )
    return jax.shard_map(
        per_device,
        mesh=mesh,
        in_specs=placed,
        out_specs=(P(AXES, None), P(AXES), P(None, AXES)),
        check_vma=False,
    )
```
